32 devices in a mesh: seq: 16 (over z, y, core), head: 2 (over x).
Axes of the slice: x: 2, y: 2, z: 4, core: 2. Of those that a mesh axis runs over, the one named last changes fastest.
Arguments:
- query_rows: bfloat16 [4096, 3072], P(('seq', 'head')), may hold values from -16 to 16
- key_rows: bfloat16 [4096, 1024], P(('seq', 'head')), may hold values from -16 to 16
- value_rows: bfloat16 [4096, 1024], P(('seq', 'head')), may hold values from -6 to 6
- residual: bfloat16 [4096, 3072], P(('seq', 'head')), may hold values from -6 to 6
- out_weight: bfloat16 [3072, 3072], P('head'), may hold values from -0.109375 to 0.109375
- gate_table: float32 [64, 3072], replicated, may hold values from -4 to 4
- noise_steps: int32 [8], replicated, may hold values from 0 to 63
- segment_mask: int32 [8, 8], replicated, may hold values from 0 to 1, as said below
- segment_map: int32 [16], replicated, may hold values from 0 to 7, as said below
Outputs:
- layer_output: bfloat16 [4096, 3072], P(('seq', 'head'))
The draws below stay inside these ranges and needn't reach their ends.
Inputs may be any that keep to these rules, and one draw needn't show every extreme that they name: `segment_mask`: ones on the diagonal, zeros above it. `segment_map`: each segment number stands in exactly 2 entries.
All inputs are finite; a program needn't handle non-finite values.
Results may differ from the reference program's by a relative error of at most 0.0095.
Values may be sent and summed in bfloat16 or wider, within the bound.
No kernel may reach another device: no remote copies, remote signals or barrier semaphores. Data moves between devices by JAX's collectives and lax.ppermute only.
A program may use at most 64 MiB of HBM per device.

```python
import math
import jax
import jax.numpy as jnp
from jax import lax

Q_HEADS = 24
KV_HEADS = 8
HEAD_DIM = 128
D = 3072
TOK_DEV = 256
SEGMENTS = 8
STEPS = 64
SEG_DEVS = 2
TOKENS = 4096


def draw_query_rows(key, part):
    key = jax.random.fold_in(key, 11)
    drawn = 1.5 * jnp.clip(jax.random.normal(key, (TOKENS, D), jnp.float32), -6.0, 6.0)
    return drawn.astype(jnp.bfloat16)


def draw_key_rows(key, part):
    key = jax.random.fold_in(key, 13)
    drawn = 2.5 * jnp.clip(jax.random.normal(key, (TOKENS, KV_HEADS * HEAD_DIM), jnp.float32), -6.0, 6.0)
    return drawn.astype(jnp.bfloat16)


def draw_segment_mask(key, part):
    key = jax.random.fold_in(key, 17)
    coins = jax.random.randint(key, (SEGMENTS, SEGMENTS), 0, 4)
    later = jnp.arange(SEGMENTS, dtype=jnp.int32)[:, None]
    earlier = jnp.arange(SEGMENTS, dtype=jnp.int32)[None, :]
    return jnp.where(later == earlier, 1, jnp.where(earlier < later, (coins > 0).astype(jnp.int32), 0)).astype(jnp.int32)


def draw_segment_map(key, part):
    key = jax.random.fold_in(key, 19)
    return (jax.random.permutation(key, SEGMENTS * SEG_DEVS) // SEG_DEVS).astype(jnp.int32)


def with_ends(values, key, low, largest):
    place = [jax.random.randint(jax.random.fold_in(key, axis), (), 0, length) for axis, length in enumerate(values.shape)]
    widest = values.shape.index(max(values.shape))
    next_to = place[:widest] + [(place[widest] + 1) % values.shape[widest]] + place[widest + 1:]
    return values.at[tuple(place)].set(low).at[tuple(next_to)].set(largest)


def block_scale(rng, dims, split, least, top_value):
    def one(dim, parts):
        heights = jax.random.uniform(jax.random.fold_in(jax.random.fold_in(rng, 6), dim), (parts,), jnp.float32, least / len(split), top_value / len(split))
        return jnp.repeat(jnp.exp(heights), dims[dim] // parts).reshape((-1,) + (1,) * (len(dims) - dim - 1))

    level = one(*split[0])
    for cut in split[1:]:
        level = level * one(*cut)
    return level


def scatter_about(rng, dims, width, reach, shards=(), held_as=jnp.bfloat16):
    values = width * jax.random.normal(rng, dims, jnp.float32)
    if shards:
        values = values * block_scale(rng, dims, shards, -0.22, 0.18)
    return jnp.clip(values, -reach, reach).astype(held_as)


def setup_inputs(seed: int = 0) -> dict:
    keys = jax.random.split(jax.random.key(seed), 10)
    query_rows = draw_query_rows(jax.random.fold_in(keys[9], 71), 0)
    key_rows = draw_key_rows(jax.random.fold_in(keys[9], 71), 0)
    value_rows = scatter_about(keys[2], (TOKENS, KV_HEADS * HEAD_DIM), 1.0, 6.0, ((0, 32),))
    residual = scatter_about(keys[3], (TOKENS, D), 1.0, 6.0, ((0, 32),))
    out_weight = scatter_about(keys[4], (D, D), D ** -0.5, 0.109375, ((0, 2),))
    gate_table = scatter_about(keys[5], (STEPS, D), 1.0, 4.0, (), jnp.float32)
    noise_steps = with_ends(jax.random.randint(keys[6], (SEGMENTS,), 0, STEPS), jax.random.fold_in(keys[6], 1), 0, STEPS - 1).astype(jnp.int32)
    segment_mask = draw_segment_mask(jax.random.fold_in(keys[9], 71), 0)
    segment_map = draw_segment_map(jax.random.fold_in(keys[9], 71), 0)
    return dict(query_rows=query_rows, key_rows=key_rows, value_rows=value_rows, residual=residual, out_weight=out_weight, gate_table=gate_table, noise_steps=noise_steps, segment_mask=segment_mask, segment_map=segment_map)


NEG = -1.0e30


def reference(query_rows, key_rows, value_rows, residual, out_weight, gate_table, noise_steps, segment_mask, segment_map):
    tokens = query_rows.shape[0]
    group_size = Q_HEADS // KV_HEADS
    token_segment = segment_map[jnp.arange(tokens, dtype=jnp.int32) // TOK_DEV].astype(jnp.int32)
    key_all = key_rows.astype(jnp.float32).reshape(tokens, KV_HEADS, HEAD_DIM)
    value_all = value_rows.astype(jnp.float32).reshape(tokens, KV_HEADS, HEAD_DIM)
    query_all = query_rows.astype(jnp.float32).reshape(tokens, KV_HEADS, group_size, HEAD_DIM)
    block_size = math.gcd(tokens, 128)

    def attend(position):
        start_row = (position * block_size).astype(jnp.int32)
        query_blk = lax.dynamic_slice_in_dim(query_all, start_row, block_size, 0)
        segment_blk = lax.dynamic_slice_in_dim(token_segment, start_row, block_size, 0)
        visible = segment_mask[segment_blk][:, token_segment] > 0
        scores = jnp.einsum("qcgd,kcd->cgqk", query_blk, key_all, precision=lax.Precision.HIGHEST) * (HEAD_DIM ** -0.5)
        scores = jnp.where(visible[None, None], scores, NEG)
        row_max = jnp.max(scores, axis=-1, keepdims=True)
        weights = jnp.where(visible[None, None], jnp.exp(scores - row_max), 0.0)
        weight_sum = jnp.sum(weights, axis=-1)
        rounded = lax.optimization_barrier(weights.astype(jnp.bfloat16)).astype(jnp.float32)
        mixed = jnp.einsum("cgqk,kcd->cgqd", rounded, value_all, precision=lax.Precision.HIGHEST) / weight_sum[..., None]
        return jnp.transpose(mixed, (2, 0, 1, 3)).reshape(block_size, Q_HEADS * HEAD_DIM).astype(jnp.bfloat16)

    attended = lax.map(attend, jnp.arange(tokens // block_size, dtype=jnp.int32)).reshape(tokens, Q_HEADS * HEAD_DIM)
    projected = jnp.dot(attended, out_weight, preferred_element_type=jnp.float32)
    gate_rows = gate_table[noise_steps[token_segment]]
    return (residual.astype(jnp.float32) + gate_rows * projected).astype(jnp.bfloat16)
```

```python
import functools
import math

import jax
import jax.numpy as jnp
from jax import lax
from jax.experimental import pallas as pl
from jax.experimental.pallas import tpu as pltpu
from jax.sharding import PartitionSpec as P

Q_HEADS = 24
KV_HEADS = 8
HEAD_DIM = 128
GROUP = Q_HEADS // KV_HEADS
CORES = 2
NEG = -1e30
SCALE = 1.4426950408889634 * HEAD_DIM ** -0.5
STAT = 8
ONES = 16
LARGE = 1e27
VMEM_LIMIT = 24 * 1024 * 1024
LITTLE = pl.CostEstimate(flops=1, bytes_accessed=1, transcendentals=0)


def grid_of(n_seq):
    chips = n_seq // CORES
    inner = 2 ** (int(math.log2(chips)) // 2)
    return chips // inner, inner


def attend_kernel(place, n_items, parts, mine, rows, tok, first, last, refs):
    own_ref, map_ref, mask_ref, qt = refs[:4]
    state_in = None if first else refs[4]
    items = refs[4 if first else 5 : -10]
    out_ref = refs[-10]
    st_s, kv_s, vt_s, list_s, land_s, full_s, count_s, top_s, sems = refs[-9:]
    st = st_s if last else out_ref
    heads = qt.shape[1]
    kv_heads = heads // GROUP
    kvw = kv_heads * HEAD_DIM
    own = own_ref[0]
    sums = slice(0, HEAD_DIM + STAT)
    weights = slice(HEAD_DIM, HEAD_DIM + STAT)
    point = slice(HEAD_DIM + STAT, HEAD_DIM + 2 * STAT)

    def copies(i, kp, ik):
        pieces = place.refs(items, i, kp)
        size = tok // len(pieces)
        return [
            pltpu.make_async_copy(piece, kv_s.at[ik, pl.ds(j * size, size)], sems.at[ik, j])
            for j, piece in enumerate(pieces)
        ]

    seg_q = [map_ref[place.query(own, j)] for j in range(parts)]
    counts = [jnp.int32(0)] * parts
    landed = jnp.int32(0)
    for i in range(n_items):
        for kp in range(parts):
            ik = i * parts + kp
            valid, src = place.source(own, i, kp)
            seg_k = map_ref[src]
            any_seen = jnp.int32(0)
            for qp in mine:
                seen = (mask_ref[seg_q[qp], seg_k] > 0).astype(jnp.int32)
                if valid is not None:
                    seen = seen * valid.astype(jnp.int32)
                list_s[qp, counts[qp]] = ik
                counts[qp] = counts[qp] + seen
                any_seen = jnp.maximum(any_seen, seen)
            land_s[landed] = ik
            landed = landed + any_seen

            @pl.when(any_seen > 0)
            def _():
                for one in copies(i, kp, ik):
                    one.start()

    ones = jnp.ones((ONES, tok), jnp.bfloat16)

    def land(t, carry):
        ik = land_s[t]
        for one in copies(0, 0, ik):
            one.wait()
        for kh in range(kv_heads):
            v = kv_s[ik, :, kvw + kh * HEAD_DIM : kvw + (kh + 1) * HEAD_DIM]
            vt_s[ik, kh, :HEAD_DIM] = v.astype(jnp.float32).T.astype(jnp.bfloat16)
            vt_s[ik, kh, HEAD_DIM:] = ones
        return carry

    lax.fori_loop(0, landed, land, 0)

    def blocks(qp, t):
        single = 2 * t + 1 >= full_s[qp]
        i0 = list_s[qp, 2 * t]
        i1 = list_s[qp, jnp.where(single, 2 * t, 2 * t + 1)]
        return i0, i1, jnp.where(single, jnp.float32(NEG), jnp.float32(0.0))

    def scores(qp, h, i0, i1):
        lanes = slice((h // GROUP) * HEAD_DIM, (h // GROUP + 1) * HEAD_DIM)
        k = jnp.concatenate([kv_s[i0, :, lanes], kv_s[i1, :, lanes]], axis=0)
        s = jnp.dot(k, qt[qp, h], preferred_element_type=jnp.float32)
        return s.reshape(2, tok // STAT, STAT, rows) * SCALE

    def product(h, i0, i1, s, ref0, ref1):
        p0 = jnp.exp2(s[0] - ref0[None]).reshape(tok, rows).astype(jnp.bfloat16)
        p1 = jnp.exp2(s[1] - ref1[None]).reshape(tok, rows).astype(jnp.bfloat16)
        vt = jnp.concatenate([vt_s[i0, h // GROUP], vt_s[i1, h // GROUP]], axis=1)
        pv = jnp.dot(vt, jnp.concatenate([p0, p1], axis=0), preferred_element_type=jnp.float32)
        return pv[sums]

    def slow(qp, t):
        i0, i1, bias = blocks(qp, t)
        for h in range(heads):
            s = scores(qp, h, i0, i1)
            before = st[qp, h, point]
            top = jnp.maximum(jnp.max(s[0], axis=0), jnp.max(s[1], axis=0) + bias)
            now = jnp.maximum(before, jnp.max(top, axis=0, keepdims=True))
            pv = product(h, i0, i1, s, now, now - bias)
            kept = st[qp, h, sums].reshape(-1, STAT, rows) * jnp.exp2(before - now)[None]
            st[qp, h, sums] = kept.reshape(-1, rows) + pv
            st[qp, h, point] = now

    def fast(qp, t):
        i0, i1, bias = blocks(qp, t)
        old = [st[qp, h] for h in range(heads)]
        new = []
        for h in range(heads):
            ref = old[h][point]
            new.append(old[h][sums] + product(h, i0, i1, scores(qp, h, i0, i1), ref, ref - bias))
        for h in range(heads):
            st[qp, h, sums] = new[h]

    for qp in mine:
        full_s[qp] = counts[qp]
        count_s[qp] = (counts[qp] + 1) // 2

    def attempt(again, carry):
        @pl.when(jnp.logical_or(again == 0, top_s[0] > 0))
        def _():
            for qp in mine:
                for h in range(heads):
                    if first:
                        st[qp, h, sums] = jnp.zeros((HEAD_DIM + STAT, rows), jnp.float32)
                        st[qp, h, point] = jnp.full((STAT, rows), NEG, jnp.float32)
                    else:
                        st[qp, h] = state_in[qp, h]

            def one_part(qp, carry):
                pairs = count_s[qp]
                switch = jnp.where(again > 0, pairs, 1 if first else 0)

                def one_slow(t, carry):
                    slow(qp, t)
                    return carry

                def one_fast(t, carry):
                    fast(qp, t)
                    return carry

                lax.fori_loop(0, switch, one_slow, 0)
                lax.fori_loop(switch, pairs, one_fast, 0)
                return carry

            lax.fori_loop(mine[0], mine[-1] + 1, one_part, 0)
            top = jnp.zeros((STAT, rows), jnp.float32)
            for qp in mine:
                for h in range(heads):
                    top = jnp.maximum(top, jnp.where(st[qp, h, weights] < LARGE, 0.0, 1.0))
            top_s[0] = (jnp.max(top) > 0.0).astype(jnp.int32)

        return carry

    top_s[0] = 0
    lax.fori_loop(0, 2, attempt, 0)
    if last:
        for j, qp in enumerate(mine):
            for h in range(heads):
                inv = 1.0 / st[qp, h, weights]
                att = st[qp, h, :HEAD_DIM].reshape(-1, STAT, rows) * inv[None]
                out_ref[j * rows : (j + 1) * rows, h * HEAD_DIM : (h + 1) * HEAD_DIM] = (
                    att.reshape(HEAD_DIM, rows).T.astype(jnp.bfloat16)
                )


class GridPlace:
    def __init__(self, metas, n_a, n_b):
        self.metas, self.n_a, self.n_b = metas, n_a, n_b

    def query(self, own, part):
        return (own // CORES) * CORES + (own % CORES + part) % CORES

    def source(self, own, i, part):
        flip, db, only, _ = self.metas[i]
        a, b, c = own // (CORES * self.n_b), (own // CORES) % self.n_b, own % CORES
        valid = None
        if len(only) < self.n_a:
            valid = functools.reduce(jnp.logical_or, [a == one for one in only])
        return valid, ((a ^ flip) * self.n_b + (b + db) % self.n_b) * CORES + (c + part) % CORES

    def refs(self, items, i, part):
        first = sum(len(meta[3]) for meta in self.metas[:i])
        out = []
        for ref, halves in zip(items[first:], self.metas[i][3]):
            rows = ref.shape[0] // (CORES * halves)
            out += [ref.at[pl.ds((half * CORES + part) * rows, rows)] for half in range(halves)]
        return out


class FlatPlace:
    def __init__(self, tok):
        self.tok = tok

    def query(self, own, part):
        return own

    def source(self, own, i, part):
        return None, i

    def refs(self, items, i, part):
        return [items[0].at[pl.ds(i * self.tok, self.tok)]]


def other_columns(own, pieces):
    rows, width = pieces[0].shape
    half = width // CORES
    vmem = pl.BlockSpec(memory_space=pltpu.VMEM)

    def kernel(own_ref, *refs):
        lanes = pl.ds(pl.multiple_of((own_ref[0] + 1) % CORES * half, half), half)
        for i, ref in enumerate(refs[:-1]):
            refs[-1][i * rows : (i + 1) * rows] = ref[:, lanes]

    return pl.pallas_call(
        kernel,
        out_shape=jax.ShapeDtypeStruct((len(pieces) * rows, half), pieces[0].dtype),
        in_specs=[pl.BlockSpec(memory_space=pltpu.SMEM)] + [vmem] * len(pieces),
        out_specs=vmem,
        compiler_params=pltpu.CompilerParams(vmem_limit_bytes=VMEM_LIMIT),
        cost_estimate=LITTLE,
        name="other_columns",
    )(own, *pieces)


def turn(own, parts):
    pieces = [x for part in parts for x in part]
    heads = min(x.shape[1] for x in pieces) // HEAD_DIM
    rows = sum(x.shape[0] for x in parts[0])
    vmem = pl.BlockSpec(memory_space=pltpu.VMEM)

    def kernel(own_ref, *refs):
        begin = own_ref[0] % CORES * heads * HEAD_DIM
        at = 0
        for qp, part in enumerate(parts):
            some = refs[at : at + len(part)]
            at += len(part)
            for h in range(heads):
                turned = []
                for ref in some:
                    first = h * HEAD_DIM
                    if ref.shape[1] > heads * HEAD_DIM:
                        first = pl.multiple_of(begin + first, HEAD_DIM)
                    turned.append(ref[:, pl.ds(first, HEAD_DIM)].astype(jnp.float32).T)
                refs[-1][qp, h] = jnp.concatenate(turned, axis=1).astype(jnp.bfloat16)

    return pl.pallas_call(
        kernel,
        out_shape=pltpu.VMEM((len(parts), heads, HEAD_DIM, rows), jnp.bfloat16),
        in_specs=[pl.BlockSpec(memory_space=pltpu.SMEM)] + [vmem] * len(pieces),
        out_specs=vmem,
        compiler_params=pltpu.CompilerParams(vmem_limit_bytes=VMEM_LIMIT),
        cost_estimate=LITTLE,
        name="turn",
    )(own, *pieces)


def attend(scalars, q, state, arrays, place, n_items, parts, tok, last, mine=None):
    mine = tuple(range(parts)) if mine is None else mine
    first = state is None
    heads, rows = q.shape[1], q.shape[3]
    width = arrays[0].shape[1]
    smem = pl.BlockSpec(memory_space=pltpu.SMEM)
    vmem = pl.BlockSpec(memory_space=pltpu.VMEM)
    args = list(scalars) + [pinned(q)] + ([] if first else [pinned(state)]) + list(arrays)
    specs = [smem] * 3 + [vmem] + ([] if first else [vmem])
    specs += [pl.BlockSpec(memory_space=pl.ANY)] * len(arrays)
    shape = (parts, heads, HEAD_DIM + 2 * STAT, rows)
    blocks = n_items * parts
    scratch = [
        pltpu.VMEM(shape if last else (STAT, HEAD_DIM), jnp.float32),
        pltpu.VMEM((blocks, tok, width), jnp.bfloat16),
        pltpu.VMEM((blocks, heads // GROUP, HEAD_DIM + ONES, tok), jnp.bfloat16),
        pltpu.SMEM((parts, blocks + 1), jnp.int32),
        pltpu.SMEM((blocks + 1,), jnp.int32),
        pltpu.SMEM((parts,), jnp.int32),
        pltpu.SMEM((parts,), jnp.int32),
        pltpu.SMEM((1,), jnp.int32),
        pltpu.SemaphoreType.DMA((blocks, 2)),
    ]
    if last:
        out_shape = [jax.ShapeDtypeStruct((len(mine) * rows, heads * HEAD_DIM), jnp.bfloat16)]
    else:
        out_shape = [pltpu.VMEM(shape, jnp.float32)]

    def kernel(*refs):
        attend_kernel(place, n_items, parts, mine, rows, tok, first, last, refs)

    return pl.pallas_call(
        kernel,
        out_shape=out_shape,
        in_specs=specs,
        out_specs=[vmem] * len(out_shape),
        scratch_shapes=scratch,
        compiler_params=pltpu.CompilerParams(vmem_limit_bytes=VMEM_LIMIT),
        cost_estimate=LITTLE,
        name="attend",
    )(*args)


def pinned(x):
    return pltpu.with_memory_space_constraint(x, pltpu.VMEM)


def fetch(weight):
    chunks = 12
    rows = weight.shape[0] // chunks

    def kernel(weight_ref, out_ref, sems):
        copies = [
            pltpu.make_async_copy(
                weight_ref.at[pl.ds(i * rows, rows)], out_ref.at[pl.ds(i * rows, rows)], sems.at[i]
            )
            for i in range(chunks)
        ]
        for one in copies:
            one.start()
        for one in copies:
            one.wait()

    return pl.pallas_call(
        kernel,
        out_shape=pltpu.VMEM(weight.shape, weight.dtype),
        in_specs=[pl.BlockSpec(memory_space=pltpu.HBM)],
        out_specs=pl.BlockSpec(memory_space=pltpu.VMEM),
        scratch_shapes=[pltpu.SemaphoreType.DMA((chunks,))],
        compiler_params=pltpu.CompilerParams(vmem_limit_bytes=VMEM_LIMIT),
        cost_estimate=LITTLE,
        name="fetch",
    )(pltpu.with_memory_space_constraint(weight, pltpu.HBM))


def project(own, parts, weight, rows, partial=None, ending=None):
    width = weight.shape[1]
    depth = parts[0][0].shape[1]
    tile = math.gcd(width, 512)
    smem = pl.BlockSpec(memory_space=pltpu.SMEM)
    vmem = pl.BlockSpec(memory_space=pltpu.VMEM)
    n = len(parts)
    args = [own] + [x for x, _, _ in parts] + [pinned(weight)]
    specs = [smem] + [vmem] * (n + 1)
    scratch = []
    out_shape = [jax.ShapeDtypeStruct((rows, width), jnp.bfloat16)]
    if partial is not None:
        args.append(pinned(partial))
        specs.append(vmem)
    elif ending is not None:
        args += list(ending)
        args[-2] = pltpu.with_memory_space_constraint(args[-2], pltpu.HBM)
        specs += [smem] * 2 + [pl.BlockSpec(memory_space=pltpu.HBM), vmem]
        out_shape = [pltpu.VMEM((rows, width), jnp.float32), pltpu.VMEM((STAT, width), jnp.float32)]
        scratch = [pltpu.VMEM((STAT, width), jnp.float32), pltpu.SemaphoreType.DMA]
    else:
        out_shape = [pltpu.VMEM((rows, width), jnp.float32)]

    def kernel(*refs):
        own_ref, part_refs, weight_ref, refs = refs[0], refs[1 : n + 1], refs[n + 1], refs[n + 2 :]
        if ending is not None:
            steps_ref, map_ref, gate_ref, residual_ref, out_ref, row_ref, near, sem = refs
            step = steps_ref[map_ref[own_ref[0]]]
            copy = pltpu.make_async_copy(
                gate_ref.at[pl.ds(pl.multiple_of((step // STAT) * STAT, STAT), STAT)], near, sem
            )
            copy.start()
            copy.wait()
            chosen = lax.broadcasted_iota(jnp.int32, (STAT, width), 0) == step % STAT
            row = jnp.sum(jnp.where(chosen, near[...], 0.0), axis=0, keepdims=True)
            row_ref[...] = jnp.broadcast_to(row, (STAT, width))
        else:
            out_ref = refs[-1]

        def one(t, carry):
            lanes = pl.ds(pl.multiple_of(t * tile, tile), tile)
            total = None
            for j in range(n):
                first_row = parts[j][2]
                group = (own_ref[0] + parts[j][1]) % CORES
                weight_rows = pl.ds(pl.multiple_of(group * depth, depth), depth)
                term = jnp.dot(
                    part_refs[j][first_row : first_row + rows],
                    weight_ref[weight_rows, lanes],
                    preferred_element_type=jnp.float32,
                )
                total = term if total is None else total + term
            if partial is not None:
                total = total + refs[0][:, lanes]
            if ending is not None:
                gate = jnp.concatenate([row_ref[:, lanes]] * (rows // STAT), axis=0)
                total = residual_ref[:, lanes].astype(jnp.float32) + gate * total
            out_ref[:, lanes] = total.astype(out_ref.dtype)
            return carry

        lax.fori_loop(0, width // tile, one, 0)

    return pl.pallas_call(
        kernel,
        out_shape=out_shape,
        in_specs=specs,
        out_specs=[vmem] * len(out_shape),
        scratch_shapes=scratch,
        compiler_params=pltpu.CompilerParams(vmem_limit_bytes=VMEM_LIMIT),
        cost_estimate=pl.CostEstimate(
            flops=2 * rows * depth * n * width, bytes_accessed=2 * depth * n * width, transcendentals=0
        ),
        name="project",
    )(*args)


def columns(x, part, width):
    return lax.dynamic_slice_in_dim(x, part * width, width, 1)


def paired(query_rows, key_rows, value_rows, out_weight, scalars, ending, n_a, n_b):
    n_seq = n_a * n_b * CORES
    groups = 2 * CORES
    own = scalars[0]
    kvw = key_rows.shape[1] // groups
    rows = query_rows.shape[0]
    tok = 2 * rows
    x = lax.axis_index("head")
    c = lax.axis_index("seq") % CORES

    def index(a, b, k):
        return (a * n_b + b) * CORES + k

    def swapped(piece, dx, dc):
        pairs = [
            ((s ^ dc) * 2 + (h ^ dx), s * 2 + h) for s in range(n_seq) for h in range(2)
        ]
        return lax.ppermute(piece, ("seq", "head"), pairs)

    def along_a(piece, moves):
        pairs = [
            (index(a, b, k), index(to, b, k)) for a, to in moves for b in range(n_b) for k in range(CORES)
        ]
        return lax.ppermute(piece, "seq", pairs)

    def beside_of(piece, only):
        pairs = [
            (index(a, 1 - b, k), index(a, b, k)) for a in only for b in range(n_b) for k in range(CORES)
        ]
        return lax.ppermute(piece, "seq", pairs)

    def stage(state, q, waiting, last=False, mine=None):
        return attend(
            scalars, q, state, [x for w, _ in waiting for x in w], GridPlace([m for _, m in waiting], n_a, n_b),
            len(waiting), CORES, tok, last, mine,
        )

    def kv_for(dx, dc):
        j = (x ^ dx) * CORES + (c ^ dc)
        return jnp.concatenate([columns(key_rows, j, kvw), columns(value_rows, j, kvw)], axis=1)

    ends, middle, chips = [0, 3], [1, 2], list(range(n_a))
    order = [(0, 0), (1, 0), (0, 1), (1, 1)]
    pieces = {d: kv_for(*d) if sum(d) == 0 else swapped(kv_for(*d), *d) for d in order}
    early = jnp.concatenate([pieces[0, 0], pieces[0, 1]], axis=0)
    later = jnp.concatenate([pieces[1, 0], pieces[1, 1]], axis=0)
    next_early = along_a(early, [(a, a ^ 1) for a in chips])
    block = jnp.concatenate([early, later], axis=0)
    qw = query_rows.shape[1] // 2
    q_own, q_other = columns(query_rows, x, qw), columns(query_rows, 1 - x, qw)
    block, later, out_weight, q_own, q_other = lax.optimization_barrier(
        (block, later, out_weight, q_own, q_other)
    )
    beside = beside_of(block, chips)
    far = along_a(block, [(a, a ^ 2) for a in chips])
    next_later = along_a(later, [(a, a ^ 1) for a in chips])
    q_came = swapped(q_other, 1, 0)
    weight = fetch(out_weight)
    q_came, weight = lax.optimization_barrier((q_came, weight))
    q_core = swapped(other_columns(own, [q_own, q_came]), 0, 1)
    q = turn(own, [[q_own, q_came], [q_core]])
    beside_early = beside_of(next_early, chips)
    (state,) = stage(None, q, [([block], (0, 0, chips, [2])), ([beside], (0, 1, chips, [2]))])
    next_later, beside_early, state = lax.optimization_barrier((next_later, beside_early, state))
    beside_later = beside_of(next_later, chips)
    far, again, state = lax.optimization_barrier((far, block, state))
    to_ends = along_a(far, [(1, 0), (2, 3)])
    beside_far = beside_of(far, chips)
    to_middle = along_a(again, [(1, 2), (2, 1)])
    (state,) = stage(state, q, [([next_early, next_later], (1, 0, chips, [1, 1])), ([far], (2, 0, chips, [2]))])
    (state,) = stage(state, q, [([beside_early, beside_later], (1, 1, chips, [1, 1]))])
    to_ends, to_middle, state = lax.optimization_barrier((to_ends, to_middle, state))
    beside_last = [
        ([beside_of(to_ends, ends)], (3, 1, ends, [2])),
        ([beside_of(to_middle, middle)], (3, 1, middle, [2])),
    ]
    last = [([to_ends], (3, 0, ends, [2])), ([to_middle], (3, 0, middle, [2]))]
    (state,) = stage(state, q, [([beside_far], (2, 1, chips, [2]))] + last)
    (sent,) = stage(state, q, beside_last, True, (1,))
    came = swapped(sent, 0, 1)
    state, sent = lax.optimization_barrier((state, sent))
    (kept,) = stage(state, q, beside_last, True, (0,))
    (begun,) = project(own, [(kept, 0, rows)], weight, rows)
    (theirs,) = project(own, [(came, 1, rows)], weight, rows, partial=begun)
    came_back = lax.ppermute(theirs, "head", [(0, 1), (1, 0)])
    base, gate = project(own, [(kept, 0, 0), (came, 1, 0)], weight, rows, ending=ending)
    return (base + gate[:1] * came_back.astype(jnp.float32)).astype(jnp.bfloat16)


def gathered_attention(query_rows, key_rows, value_rows, scalars):
    spread = functools.partial(lax.all_to_all, axis_name="head", split_axis=1, concat_axis=0, tiled=True)
    local = jnp.concatenate([spread(key_rows), spread(value_rows)], axis=1)
    every = lax.all_gather(local, "seq", axis=0, tiled=True)
    tok = local.shape[0]
    return attend(
        scalars, turn(scalars[0], [[spread(query_rows)]]), None, [every], FlatPlace(tok), every.shape[0] // tok, 1, tok, True
    )[0]


def per_device(
    query_rows,
    key_rows,
    value_rows,
    residual,
    out_weight,
    gate_table,
    noise_steps,
    segment_mask,
    segment_map,
):
    n_seq = lax.axis_size("seq")
    n_head = lax.axis_size("head")
    own_seq = lax.axis_index("seq").astype(jnp.int32)
    own = own_seq.reshape(1)
    scalars = (own, segment_map, segment_mask)
    n_a, n_b = grid_of(n_seq)
    if n_head == 2 and n_a == 4 and n_b == 2:
        ending = (noise_steps, segment_map, gate_table, residual)
        return paired(query_rows, key_rows, value_rows, out_weight, scalars, ending, n_a, n_b)
    attended = gathered_attention(query_rows, key_rows, value_rows, scalars)
    projected = lax.psum_scatter(
        jnp.dot(attended, out_weight, preferred_element_type=jnp.float32).astype(jnp.bfloat16),
        "head",
        scatter_dimension=0,
        tiled=True,
    ).astype(jnp.float32)
    gate_row = lax.dynamic_slice_in_dim(gate_table, noise_steps[segment_map[own_seq]], 1, 0)
    return (residual.astype(jnp.float32) + gate_row * projected).astype(jnp.bfloat16)


def solution(mesh):
    placed = (
        P(("seq", "head"), None),
        P(("seq", "head"), None),
        P(("seq", "head"), None),
        P(("seq", "head"), None),
        P("head", None),
        P(),
        P(),
        P(),
        P(),
    )
    return jax.shard_map(
        per_device, mesh=mesh, in_specs=placed, out_specs=P(("seq", "head"), None), check_vma=False
    )
```

```python
import functools
import math

import jax
import jax.numpy as jnp
from jax import lax
from jax.experimental import pallas as pl
from jax.experimental.pallas import tpu as pltpu
from jax.sharding import PartitionSpec as P

Q_HEADS = 24
KV_HEADS = 8
HEAD_DIM = 128
GROUP = Q_HEADS // KV_HEADS
CORES = 2
UNITS = 2
NEG = -1e30
SCALE = 1.4426950408889634 * HEAD_DIM ** -0.5
STAT = 8
ONES = 16
LARGE = 1e27
VMEM_LIMIT = 24 * 1024 * 1024
LITTLE = pl.CostEstimate(flops=1, bytes_accessed=1, transcendentals=0)


def grid_of(n_seq):
    chips = n_seq // CORES
    inner = 2 ** (int(math.log2(chips)) // 2)
    return chips // inner, inner


def attend_kernel(place, n_items, parts, half, rows, tok, first, last, refs):
    own_ref, map_ref, mask_ref, q_ref = refs[:4]
    mixed = half is not None
    tiles = 1 if mixed else parts
    state_in = None if first else refs[4]
    st_s, qt_s, kv_s, vt_s, list_s, land_s, seen_s, full_s, count_s, top_s, sems = refs[-11:]
    outs = 2 if mixed else 1
    items, outs = refs[4 if first else 5 : -11 - outs], refs[-11 - outs : -11]
    st, qt = st_s if last else outs[0], qt_s if mixed else q_ref
    heads = qt.shape[1]
    kv_heads = heads // GROUP
    kvw = kv_heads * HEAD_DIM
    own = own_ref[0]
    sums = slice(0, HEAD_DIM + STAT)
    weights = slice(HEAD_DIM, HEAD_DIM + STAT)
    point = slice(HEAD_DIM + STAT, HEAD_DIM + 2 * STAT)

    def copies(i, kp, ik):
        pieces = place.refs(items, i, kp)
        size = tok // len(pieces)
        return [
            pltpu.make_async_copy(piece, kv_s.at[ik, pl.ds(j * size, size)], sems.at[ik, j])
            for j, piece in enumerate(pieces)
        ]

    seg_q = [map_ref[place.query(own, j)] for j in range(parts)]
    counts = [jnp.int32(0)] * tiles
    landed = jnp.int32(0)
    for i in range(n_items):
        for kp in range(parts):
            ik = i * parts + kp
            valid, src = place.source(own, i, kp)
            seg_k = map_ref[src]
            any_seen = jnp.int32(0)
            for qp in range(parts):
                seen = (mask_ref[seg_q[qp], seg_k] > 0).astype(jnp.int32)
                if valid is not None:
                    seen = seen * valid.astype(jnp.int32)
                seen_s[qp, ik] = seen
                any_seen = jnp.maximum(any_seen, seen)
                if not mixed:
                    list_s[qp, counts[qp]] = ik
                    counts[qp] = counts[qp] + seen
            if mixed:
                list_s[0, counts[0]] = ik
                counts[0] = counts[0] + any_seen
            land_s[landed] = ik
            landed = landed + any_seen

            @pl.when(any_seen > 0)
            def _():
                for one in copies(i, kp, ik):
                    one.start()

    ones = jnp.ones((ONES, tok), jnp.bfloat16)

    def land(t, carry):
        ik = land_s[t]
        for one in copies(0, 0, ik):
            one.wait()
        for kh in range(kv_heads):
            v = kv_s[ik, :, kvw + kh * HEAD_DIM : kvw + (kh + 1) * HEAD_DIM]
            vt_s[ik, kh, :HEAD_DIM] = v.astype(jnp.float32).T.astype(jnp.bfloat16)
            vt_s[ik, kh, HEAD_DIM:] = ones
        return carry

    lax.fori_loop(0, landed, land, 0)

    def blocks(qp, t):
        single = 2 * t + 1 >= full_s[qp]
        i0 = list_s[qp, 2 * t]
        i1 = list_s[qp, jnp.where(single, 2 * t, 2 * t + 1)]
        bias = [jnp.float32(0.0), jnp.where(single, jnp.float32(NEG), jnp.float32(0.0))]
        if mixed:
            left = lax.broadcasted_iota(jnp.int32, (STAT, rows), 1) < rows // 2
            for j, i in enumerate((i0, i1)):
                hidden = [jnp.where(seen_s[part, i] > 0, jnp.float32(0.0), jnp.float32(NEG)) for part in range(2)]
                bias[j] = bias[j] + jnp.where(left, hidden[0], hidden[1])
        return i0, i1, bias

    def operands(kh, i0, i1):
        lanes = slice(kh * HEAD_DIM, (kh + 1) * HEAD_DIM)
        return (
            [jnp.concatenate([kv_s[i, :, lanes]] * 2, axis=1) for i in (i0, i1)],
            [vt_s[i, kh] for i in (i0, i1)],
        )

    def slow(units, qp, t):
        i0, i1, bias = blocks(qp, t)
        for h in range(heads):
            kh = h // GROUP
            unit = kh % UNITS
            s0_acc, s1_acc, pv_acc = units[unit]
            keys, values = operands(kh, i0, i1)
            pltpu.matmul_push_rhs(qt[qp, h], 0, unit)
            pltpu.matmul_acc_lhs(s0_acc, keys[0], 0)
            pltpu.matmul_acc_lhs(s1_acc, keys[1])
            s = [pltpu.matmul_pop(acc).reshape(-1, STAT, rows) for acc in (s0_acc, s1_acc)]
            before = st[qp, h, point]
            top = jnp.maximum(jnp.max(s[0], axis=0) + bias[0], jnp.max(s[1], axis=0) + bias[1])
            now = jnp.maximum(before, jnp.max(top, axis=0, keepdims=True))
            for x, ref, value in zip(s, (now - bias[0], now - bias[1]), values):
                p = jnp.exp2(x - ref[None]).reshape(tok, rows).astype(jnp.bfloat16)
                pltpu.matmul_push_rhs(p, 1, unit)
                pltpu.matmul_acc_lhs(pv_acc, value, 1)
            kept = st[qp, h, sums].reshape(-1, STAT, rows) * jnp.exp2(before - now)[None]
            st[qp, h, sums] = kept.reshape(-1, rows) + pltpu.matmul_pop(pv_acc)[sums]
            st[qp, h, point] = now

    def fast(units, qp, t):
        i0, i1, bias = blocks(qp, t)
        keys, values = zip(*[operands(kh, i0, i1) for kh in range(kv_heads)])

        def begin(kh, g):
            unit = units[kh % len(units)]
            pltpu.matmul_push_rhs(qt[qp, kh * GROUP + g], 0, kh % len(units))
            pltpu.matmul_acc_lhs(unit[0], keys[kh][0], 0)
            pltpu.matmul_acc_lhs(unit[1], keys[kh][1])

        def weights_of(kh, g, j):
            s = pltpu.matmul_pop(units[kh % len(units)][j]).reshape(-1, STAT, rows)
            ref = st[qp, kh * GROUP + g, point] - bias[j]
            return jnp.exp2(s - ref[None]).reshape(tok, rows).astype(jnp.bfloat16)

        for first_kh in range(0, kv_heads, len(units)):
            together = range(first_kh, min(first_kh + len(units), kv_heads))
            for kh in together:
                begin(kh, 0)
            for g in range(GROUP):
                p = {(kh, j): weights_of(kh, g, j) for j in range(2) for kh in together}
                if g + 1 < GROUP:
                    for kh in together:
                        begin(kh, g + 1)
                for j in range(2):
                    for kh in together:
                        pltpu.matmul_push_rhs(p[kh, j], 1, kh % len(units))
                        pltpu.matmul_acc_lhs(units[kh % len(units)][2], values[kh][j], 1)
                for kh in together:
                    h = kh * GROUP + g
                    st[qp, h, sums] = st[qp, h, sums] + pltpu.matmul_pop(units[kh % len(units)][2])[sums]

    columns_of = slice(half * rows // 2, (half + 1) * rows // 2) if mixed else slice(0, rows)
    if mixed:
        for h in range(heads):
            qt_s[0, h] = jnp.concatenate([q_ref[part, h, :, columns_of] for part in range(2)], axis=1)
    for qp in range(tiles):
        full_s[qp] = counts[qp]
        count_s[qp] = (counts[qp] + 1) // 2

    def attempt(again, carry):
        @pl.when(jnp.logical_or(again == 0, top_s[0] > 0))
        def _():
            for qp in range(tiles):
                for h in range(heads):
                    if mixed:
                        st[0, h] = jnp.concatenate([state_in[part, h, :, columns_of] for part in range(2)], axis=1)
                    elif first:
                        st[qp, h, sums] = jnp.zeros((HEAD_DIM + STAT, rows), jnp.float32)
                        st[qp, h, point] = jnp.full((STAT, rows), NEG, jnp.float32)
                    else:
                        st[qp, h] = state_in[qp, h]

            def one_part(qp, carry):
                pairs = count_s[qp]
                switch = jnp.where(again > 0, pairs, 1 if first else 0)

                def both(*accs):
                    units = [accs[3 * unit : 3 * unit + 3] for unit in range(UNITS)]

                    def one_slow(t, carry):
                        slow(units, qp, t)
                        return carry

                    def one_fast(t, carry):
                        fast(units, qp, t)
                        return carry

                    lax.fori_loop(0, switch, one_slow, 0)
                    lax.fori_loop(switch, pairs, one_fast, 0)

                accumulators = []
                for unit in range(UNITS):
                    accumulators += [pltpu.ACC(unit)((tok, rows), jnp.float32)] * 2
                    accumulators.append(pltpu.ACC(unit)((HEAD_DIM + ONES, rows), jnp.float32))
                pl.run_scoped(both, *accumulators)
                return carry

            lax.fori_loop(0, tiles, one_part, 0)
            top = jnp.zeros((STAT, rows), jnp.float32)
            for qp in range(tiles):
                for h in range(heads):
                    top = jnp.maximum(top, jnp.where(st[qp, h, weights] < LARGE, 0.0, 1.0))
            top_s[0] = (jnp.max(top) > 0.0).astype(jnp.int32)

        return carry

    top_s[0] = 0
    lax.fori_loop(0, 2, attempt, 0)
    if last:
        for qp in range(tiles):
            for h in range(heads):
                lanes = slice(h * HEAD_DIM, (h + 1) * HEAD_DIM)
                inv = 1.0 / st[qp, h, weights]
                att = st[qp, h, :HEAD_DIM].reshape(-1, STAT, rows) * inv[None]
                att = att.reshape(HEAD_DIM, rows).T.astype(jnp.bfloat16)
                if mixed:
                    outs[0][:, lanes] = att[: rows // 2]
                    outs[1][:, lanes] = att[rows // 2 :]
                else:
                    outs[0][qp * rows : (qp + 1) * rows, lanes] = att


class GridPlace:
    def __init__(self, metas, n_a, n_b, tok):
        self.metas, self.n_a, self.n_b, self.tok = metas, n_a, n_b, tok

    def query(self, own, part):
        return (own // CORES) * CORES + (own % CORES + part) % CORES

    def source(self, own, i, part):
        flip, db, _ = self.metas[i]
        a, b, c = own // (CORES * self.n_b), (own // CORES) % self.n_b, own % CORES
        return None, ((a ^ flip) * self.n_b + (b + db) % self.n_b) * CORES + (c + part) % CORES

    def refs(self, items, i, part):
        first = sum(len(meta[2]) for meta in self.metas[:i])
        out = []
        for ref, (halves, base) in zip(items[first:], self.metas[i][2]):
            rows = self.tok // 2
            out += [ref.at[pl.ds(base + (half * CORES + part) * rows, rows)] for half in range(halves)]
        return out


class FlatPlace:
    def __init__(self, tok):
        self.tok = tok

    def query(self, own, part):
        return own

    def source(self, own, i, part):
        return None, i

    def refs(self, items, i, part):
        return [items[0].at[pl.ds(i * self.tok, self.tok)]]


def other_columns(own, pieces):
    rows, width = pieces[0].shape
    half = width // CORES
    vmem = pl.BlockSpec(memory_space=pltpu.VMEM)

    def kernel(own_ref, *refs):
        lanes = pl.ds(pl.multiple_of((own_ref[0] + 1) % CORES * half, half), half)
        for i, ref in enumerate(refs[:-1]):
            refs[-1][i * rows : (i + 1) * rows] = ref[:, lanes]

    return pl.pallas_call(
        kernel,
        out_shape=jax.ShapeDtypeStruct((len(pieces) * rows, half), pieces[0].dtype),
        in_specs=[pl.BlockSpec(memory_space=pltpu.SMEM)] + [vmem] * len(pieces),
        out_specs=vmem,
        compiler_params=pltpu.CompilerParams(vmem_limit_bytes=VMEM_LIMIT),
        cost_estimate=LITTLE,
        name="other_columns",
    )(own, *pieces)


def moved(kernel, args, shapes, name):
    vmem = pl.BlockSpec(memory_space=pltpu.VMEM)
    return pl.pallas_call(
        kernel,
        out_shape=[jax.ShapeDtypeStruct(shape, jnp.bfloat16) for shape in shapes],
        in_specs=[pl.BlockSpec(memory_space=pltpu.SMEM)] + [vmem] * (len(args) - 1),
        out_specs=[vmem] * len(shapes),
        compiler_params=pltpu.CompilerParams(vmem_limit_bytes=VMEM_LIMIT),
        cost_estimate=LITTLE,
        name=name,
    )(*args)


def joined(own, above, below):
    rows, width = above.shape

    def kernel(own_ref, above_ref, below_ref, out_ref):
        out_ref[:rows] = above_ref[...]
        out_ref[rows:] = below_ref[...]

    return moved(kernel, (own, above, below), [(2 * rows, width)], "joined")[0]


def lower_half(own, x):
    rows, width = x.shape

    def kernel(own_ref, x_ref, out_ref):
        out_ref[...] = x_ref[rows // 2 :]

    return moved(kernel, (own, x), [(rows // 2, width)], "lower_half")[0]


def picked(own, at_ends, at_middle, n_a, n_b):
    rows, width = at_ends.shape

    def kernel(own_ref, ends_ref, middle_ref, whole_ref, half_ref):
        a = own_ref[0] // (CORES * n_b)
        at_end = jnp.logical_or(a == 0, a == n_a - 1)

        def take(ref):
            whole_ref[...] = ref[...]
            half_ref[...] = ref[: rows // 2]

        pl.when(at_end)(lambda: take(ends_ref))
        pl.when(jnp.logical_not(at_end))(lambda: take(middle_ref))

    return moved(kernel, (own, at_ends, at_middle), [(rows, width), (rows // 2, width)], "picked")


def turn(own, parts):
    pieces = [x for part in parts for x in part]
    heads = min(x.shape[1] for x in pieces) // HEAD_DIM
    rows = sum(x.shape[0] for x in parts[0])
    vmem = pl.BlockSpec(memory_space=pltpu.VMEM)

    def kernel(own_ref, *refs):
        begin = own_ref[0] % CORES * heads * HEAD_DIM
        at = 0
        for qp, part in enumerate(parts):
            some = refs[at : at + len(part)]
            at += len(part)
            for h in range(heads):
                turned = []
                for ref in some:
                    first = h * HEAD_DIM
                    if ref.shape[1] > heads * HEAD_DIM:
                        first = pl.multiple_of(begin + first, HEAD_DIM)
                    turned.append(ref[:, pl.ds(first, HEAD_DIM)].astype(jnp.float32).T)
                scaled = jnp.concatenate(turned, axis=1) * SCALE
                high = scaled.astype(jnp.bfloat16)
                refs[-1][qp, h, :HEAD_DIM] = high
                refs[-1][qp, h, HEAD_DIM:] = (scaled - high.astype(jnp.float32)).astype(jnp.bfloat16)

    return pl.pallas_call(
        kernel,
        out_shape=pltpu.VMEM((len(parts), heads, 2 * HEAD_DIM, rows), jnp.bfloat16),
        in_specs=[pl.BlockSpec(memory_space=pltpu.SMEM)] + [vmem] * len(pieces),
        out_specs=vmem,
        compiler_params=pltpu.CompilerParams(vmem_limit_bytes=VMEM_LIMIT),
        cost_estimate=LITTLE,
        name="turn",
    )(own, *pieces)


def attend(scalars, q, state, arrays, place, n_items, parts, tok, last, half=None):
    first = state is None
    heads, rows = q.shape[1], q.shape[3]
    width = arrays[0].shape[1]
    smem = pl.BlockSpec(memory_space=pltpu.SMEM)
    vmem = pl.BlockSpec(memory_space=pltpu.VMEM)
    args = list(scalars) + [pinned(q)] + ([] if first else [pinned(state)]) + list(arrays)
    specs = [smem] * 3 + [vmem] + ([] if first else [vmem])
    specs += [pl.BlockSpec(memory_space=pl.ANY)] * len(arrays)
    shape = (parts, heads, HEAD_DIM + 2 * STAT, rows)
    tile_shape = shape if half is None else (1,) + shape[1:]
    blocks = n_items * parts
    scratch = [
        pltpu.VMEM(tile_shape if last else (STAT, HEAD_DIM), jnp.float32),
        pltpu.VMEM((1,) + q.shape[1:] if half is not None else (ONES, HEAD_DIM), jnp.bfloat16),
        pltpu.VMEM((blocks, tok, width), jnp.bfloat16),
        pltpu.VMEM((blocks, heads // GROUP, HEAD_DIM + ONES, tok), jnp.bfloat16),
        pltpu.SMEM((parts, blocks + 1), jnp.int32),
        pltpu.SMEM((blocks + 1,), jnp.int32),
        pltpu.SMEM((parts, blocks), jnp.int32),
        pltpu.SMEM((parts,), jnp.int32),
        pltpu.SMEM((parts,), jnp.int32),
        pltpu.SMEM((1,), jnp.int32),
        pltpu.SemaphoreType.DMA((blocks, 2)),
    ]
    if last:
        out_shape = [jax.ShapeDtypeStruct((parts * rows, heads * HEAD_DIM), jnp.bfloat16)]
        if half is not None:
            out_shape = [jax.ShapeDtypeStruct((rows // 2, heads * HEAD_DIM), jnp.bfloat16)] * 2
    else:
        out_shape = [pltpu.VMEM(shape, jnp.float32)]

    def kernel(*refs):
        attend_kernel(place, n_items, parts, half, rows, tok, first, last, refs)

    return pl.pallas_call(
        kernel,
        out_shape=out_shape,
        in_specs=specs,
        out_specs=[vmem] * len(out_shape),
        scratch_shapes=scratch,
        compiler_params=pltpu.CompilerParams(vmem_limit_bytes=VMEM_LIMIT),
        cost_estimate=LITTLE,
        name="attend",
    )(*args)


def pinned(x):
    return pltpu.with_memory_space_constraint(x, pltpu.VMEM)


def fetch(weight):
    chunks = 12
    rows = weight.shape[0] // chunks

    def kernel(weight_ref, out_ref, sems):
        copies = [
            pltpu.make_async_copy(
                weight_ref.at[pl.ds(i * rows, rows)], out_ref.at[pl.ds(i * rows, rows)], sems.at[i]
            )
            for i in range(chunks)
        ]
        for one in copies:
            one.start()
        for one in copies:
            one.wait()

    return pl.pallas_call(
        kernel,
        out_shape=pltpu.VMEM(weight.shape, weight.dtype),
        in_specs=[pl.BlockSpec(memory_space=pltpu.HBM)],
        out_specs=pl.BlockSpec(memory_space=pltpu.VMEM),
        scratch_shapes=[pltpu.SemaphoreType.DMA((chunks,))],
        compiler_params=pltpu.CompilerParams(vmem_limit_bytes=VMEM_LIMIT),
        cost_estimate=LITTLE,
        name="fetch",
    )(pltpu.with_memory_space_constraint(weight, pltpu.HBM))


def project(own, parts, weight, rows, partial=None, ending=None):
    width = weight.shape[1]
    depth = parts[0][0].shape[1]
    tile = math.gcd(width, 512)
    smem = pl.BlockSpec(memory_space=pltpu.SMEM)
    vmem = pl.BlockSpec(memory_space=pltpu.VMEM)
    n = len(parts)
    args = [own] + [x for x, _, _ in parts] + [pinned(weight)]
    specs = [smem] + [vmem] * (n + 1)
    scratch = []
    out_shape = [jax.ShapeDtypeStruct((rows, width), jnp.bfloat16)]
    if partial is not None:
        args.append(pinned(partial))
        specs.append(vmem)
    elif ending is not None:
        args += list(ending)
        args[-2] = pltpu.with_memory_space_constraint(args[-2], pltpu.HBM)
        specs += [smem] * 2 + [pl.BlockSpec(memory_space=pltpu.HBM), vmem]
        out_shape = [pltpu.VMEM((rows, width), jnp.float32), pltpu.VMEM((STAT, width), jnp.float32)]
        scratch = [pltpu.VMEM((STAT, width), jnp.float32), pltpu.SemaphoreType.DMA]
    else:
        out_shape = [pltpu.VMEM((rows, width), jnp.float32)]

    def kernel(*refs):
        own_ref, part_refs, weight_ref, refs = refs[0], refs[1 : n + 1], refs[n + 1], refs[n + 2 :]
        if ending is not None:
            steps_ref, map_ref, gate_ref, residual_ref, out_ref, row_ref, near, sem = refs
            step = steps_ref[map_ref[own_ref[0]]]
            copy = pltpu.make_async_copy(
                gate_ref.at[pl.ds(pl.multiple_of((step // STAT) * STAT, STAT), STAT)], near, sem
            )
            copy.start()
            copy.wait()
            chosen = lax.broadcasted_iota(jnp.int32, (STAT, width), 0) == step % STAT
            row = jnp.sum(jnp.where(chosen, near[...], 0.0), axis=0, keepdims=True)
            row_ref[...] = jnp.broadcast_to(row, (STAT, width))
        else:
            out_ref = refs[-1]

        def one(t, carry):
            lanes = pl.ds(pl.multiple_of(t * tile, tile), tile)
            total = None
            for j in range(n):
                first_row = parts[j][2]
                group = (own_ref[0] + parts[j][1]) % CORES
                weight_rows = pl.ds(pl.multiple_of(group * depth, depth), depth)
                term = jnp.dot(
                    part_refs[j][first_row : first_row + rows],
                    weight_ref[weight_rows, lanes],
                    preferred_element_type=jnp.float32,
                )
                total = term if total is None else total + term
            if partial is not None:
                total = total + refs[0][:, lanes]
            if ending is not None:
                gate = jnp.concatenate([row_ref[:, lanes]] * (rows // STAT), axis=0)
                total = residual_ref[:, lanes].astype(jnp.float32) + gate * total
            out_ref[:, lanes] = total.astype(out_ref.dtype)
            return carry

        lax.fori_loop(0, width // tile, one, 0)

    return pl.pallas_call(
        kernel,
        out_shape=out_shape,
        in_specs=specs,
        out_specs=[vmem] * len(out_shape),
        scratch_shapes=scratch,
        compiler_params=pltpu.CompilerParams(vmem_limit_bytes=VMEM_LIMIT),
        cost_estimate=pl.CostEstimate(
            flops=2 * rows * depth * n * width, bytes_accessed=2 * depth * n * width, transcendentals=0
        ),
        name="project",
    )(*args)


def columns(x, part, width):
    return lax.dynamic_slice_in_dim(x, part * width, width, 1)


def paired(query_rows, key_rows, value_rows, out_weight, scalars, ending, n_a, n_b):
    n_seq = n_a * n_b * CORES
    groups = 2 * CORES
    own = scalars[0]
    kvw = key_rows.shape[1] // groups
    rows = query_rows.shape[0]
    tok = 2 * rows
    x = lax.axis_index("head")
    c = lax.axis_index("seq") % CORES

    def index(a, b, k):
        return (a * n_b + b) * CORES + k

    def swapped(piece, dx, dc):
        pairs = [
            ((s ^ dc) * 2 + (h ^ dx), s * 2 + h) for s in range(n_seq) for h in range(2)
        ]
        return lax.ppermute(piece, ("seq", "head"), pairs)

    def along_a(piece, moves):
        pairs = [
            (index(a, b, k), index(to, b, k)) for a, to in moves for b in range(n_b) for k in range(CORES)
        ]
        return lax.ppermute(piece, "seq", pairs)

    def beside_of(piece, only):
        pairs = [
            (index(a, 1 - b, k), index(a, b, k)) for a in only for b in range(n_b) for k in range(CORES)
        ]
        return lax.ppermute(piece, "seq", pairs)

    def stage(state, q, waiting, last=False, half=None):
        return attend(
            scalars, q, state, [x for w, _ in waiting for x in w], GridPlace([m for _, m in waiting], n_a, n_b, tok),
            len(waiting), CORES, tok, last, half,
        )

    def kv_for(dx, dc):
        j = (x ^ dx) * CORES + (c ^ dc)
        return jnp.concatenate([columns(key_rows, j, kvw), columns(value_rows, j, kvw)], axis=1)

    chips = list(range(n_a))
    order = [(0, 0), (1, 0), (0, 1), (1, 1)]
    pieces = {d: kv_for(*d) if sum(d) == 0 else swapped(kv_for(*d), *d) for d in order}
    early = jnp.concatenate([pieces[0, 0], pieces[0, 1]], axis=0)
    later = jnp.concatenate([pieces[1, 0], pieces[1, 1]], axis=0)
    block = jnp.concatenate([early, later], axis=0)
    qw = query_rows.shape[1] // 2
    q_own, q_other = columns(query_rows, x, qw), columns(query_rows, 1 - x, qw)
    block, early, later, out_weight, q_own, q_other = lax.optimization_barrier(
        (block, early, later, out_weight, q_own, q_other)
    )
    by_one, by_two = [(a, a ^ 1) for a in chips], [(a, a ^ 2) for a in chips]
    beside = beside_of(block, chips)
    next_early, far_early = along_a(early, by_one), along_a(early, by_two)
    q_came = swapped(q_other, 1, 0)
    weight = fetch(out_weight)
    beside, next_early, far_early, later, q_came, weight = lax.optimization_barrier(
        (beside, next_early, far_early, later, q_came, weight)
    )
    beside_early = beside_of(joined(own, next_early, far_early), chips)
    next_later, far_later = along_a(later, by_one), along_a(later, by_two)
    q_core = swapped(other_columns(own, [q_own, q_came]), 0, 1)
    q = turn(own, [[q_own, q_came], [q_core]])
    whole, halves = [(2, 0)], [(1, 0), (1, 0)]
    (state,) = stage(None, q, [([block], (0, 0, whole)), ([beside], (0, 1, whole))])
    next_later, far_later, beside_early, again, state = lax.optimization_barrier(
        (next_later, far_later, beside_early, block, state)
    )
    beside_later = beside_of(joined(own, next_later, far_later), chips)
    to_ends = along_a(joined(own, far_early, far_later), [(1, 0), (2, 3)])
    to_middle = along_a(again, [(1, 2), (2, 1)])
    (state,) = stage(
        state, q, [([next_early, next_later], (1, 0, halves)), ([far_early, far_later], (2, 0, halves))]
    )
    to_ends, to_middle, beside_later, state = lax.optimization_barrier((to_ends, to_middle, beside_later, state))
    last, last_upper = picked(own, to_ends, to_middle, n_a, n_b)
    beside_last = [
        ([beside_of(last_upper, chips), along_a(lower_half(own, beside_later), by_one)], (3, 1, halves)),
    ]
    relayed = [beside_early, beside_later]
    (state,) = stage(
        state, q,
        [
            (relayed, (1, 1, halves)),
            (relayed, (2, 1, [(1, tok), (1, tok)])),
            ([last], (3, 0, whole)),
        ],
    )
    kept, sent = stage(state, q, beside_last, True, 1)
    came = swapped(sent, 0, 1)
    (begun,) = project(own, [(kept, 0, 0)], weight, rows)
    (theirs,) = project(own, [(came, 1, 0)], weight, rows, partial=begun)
    came_back = lax.ppermute(theirs, "head", [(0, 1), (1, 0)])
    state, theirs = lax.optimization_barrier((state, theirs))
    kept, sent = stage(state, q, beside_last, True, 0)
    came = swapped(sent, 0, 1)
    base, gate = project(own, [(kept, 0, 0), (came, 1, 0)], weight, rows, ending=ending)
    return (base + gate[:1] * came_back.astype(jnp.float32)).astype(jnp.bfloat16)


def gathered_attention(query_rows, key_rows, value_rows, scalars):
    spread = functools.partial(lax.all_to_all, axis_name="head", split_axis=1, concat_axis=0, tiled=True)
    local = jnp.concatenate([spread(key_rows), spread(value_rows)], axis=1)
    every = lax.all_gather(local, "seq", axis=0, tiled=True)
    tok = local.shape[0]
    return attend(
        scalars, turn(scalars[0], [[spread(query_rows)]]), None, [every], FlatPlace(tok), every.shape[0] // tok, 1, tok, True
    )[0]


def per_device(
    query_rows,
    key_rows,
    value_rows,
    residual,
    out_weight,
    gate_table,
    noise_steps,
    segment_mask,
    segment_map,
):
    n_seq = lax.axis_size("seq")
    n_head = lax.axis_size("head")
    own_seq = lax.axis_index("seq").astype(jnp.int32)
    own = own_seq.reshape(1)
    scalars = (own, segment_map, segment_mask)
    n_a, n_b = grid_of(n_seq)
    if n_head == 2 and n_a == 4 and n_b == 2:
        ending = (noise_steps, segment_map, gate_table, residual)
        return paired(query_rows, key_rows, value_rows, out_weight, scalars, ending, n_a, n_b)
    attended = gathered_attention(query_rows, key_rows, value_rows, scalars)
    projected = lax.psum_scatter(
        jnp.dot(attended, out_weight, preferred_element_type=jnp.float32).astype(jnp.bfloat16),
        "head",
        scatter_dimension=0,
        tiled=True,
    ).astype(jnp.float32)
    gate_row = lax.dynamic_slice_in_dim(gate_table, noise_steps[segment_map[own_seq]], 1, 0)
    return (residual.astype(jnp.float32) + gate_row * projected).astype(jnp.bfloat16)


def solution(mesh):
    placed = (
        P(("seq", "head"), None),
        P(("seq", "head"), None),
        P(("seq", "head"), None),
        P(("seq", "head"), None),
        P("head", None),
        P(),
        P(),
        P(),
        P(),
    )
    return jax.shard_map(
        per_device, mesh=mesh, in_specs=placed, out_specs=P(("seq", "head"), None), check_vma=False
    )
```

```python
import functools
import math

import jax
import jax.numpy as jnp
from jax import lax
from jax.experimental import pallas as pl
from jax.experimental.pallas import tpu as pltpu
from jax.sharding import PartitionSpec as P

Q_HEADS = 24
KV_HEADS = 8
HEAD_DIM = 128
GROUP = Q_HEADS // KV_HEADS
CORES = 2
UNITS = 2
NEG = -1e30
SCALE = 1.4426950408889634 * HEAD_DIM ** -0.5
STAT = 8
ONES = 16
LARGE = 1e27
VMEM_LIMIT = 24 * 1024 * 1024
LITTLE = pl.CostEstimate(flops=1, bytes_accessed=1, transcendentals=0)


def grid_of(n_seq):
    chips = n_seq // CORES
    inner = 2 ** (int(math.log2(chips)) // 2)
    return chips // inner, inner


def attend_kernel(place, n_items, parts, half, rows, tok, first, last, refs):
    own_ref, map_ref, mask_ref, q_ref = refs[:4]
    mixed = half is not None
    tiles = 1 if mixed else parts
    state_in = None if first else refs[4]
    st_s, qt_s, kv_s, vt_s, list_s, land_s, seen_s, full_s, count_s, top_s, sems = refs[-11:]
    outs = 2 if mixed else 1
    items, outs = refs[4 if first else 5 : -11 - outs], refs[-11 - outs : -11]
    st, qt = st_s if last else outs[0], qt_s if mixed else q_ref
    heads = qt.shape[1]
    kv_heads = heads // GROUP
    kvw = kv_heads * HEAD_DIM
    own = own_ref[0]
    sums = slice(0, HEAD_DIM + STAT)
    weights = slice(HEAD_DIM, HEAD_DIM + STAT)
    point = slice(HEAD_DIM + STAT, HEAD_DIM + 2 * STAT)

    def copies(i, kp, ik):
        pieces = place.refs(items, i, kp)
        size = tok // len(pieces)
        return [
            pltpu.make_async_copy(piece, kv_s.at[ik, pl.ds(j * size, size)], sems.at[ik, j])
            for j, piece in enumerate(pieces)
        ]

    seg_q = [map_ref[place.query(own, j)] for j in range(parts)]
    counts = [jnp.int32(0)] * tiles
    landed = jnp.int32(0)
    for i in range(n_items):
        for kp in range(parts):
            ik = i * parts + kp
            seg_k = [map_ref[src] for src in place.sources(own, i, kp)]
            any_seen = jnp.int32(0)
            for qp in range(parts):
                seen = jnp.int32(0)
                for n in range(2):
                    seen_half = (mask_ref[seg_q[qp], seg_k[n]] > 0).astype(jnp.int32)
                    seen_s[qp, 2 * ik + n] = seen_half
                    seen = jnp.maximum(seen, seen_half)
                any_seen = jnp.maximum(any_seen, seen)
                if not mixed:
                    list_s[qp, counts[qp]] = ik
                    counts[qp] = counts[qp] + seen
            if mixed:
                list_s[0, counts[0]] = ik
                counts[0] = counts[0] + any_seen
            land_s[landed] = ik
            landed = landed + any_seen

            @pl.when(any_seen > 0)
            def _():
                for one in copies(i, kp, ik):
                    one.start()

    ones = jnp.ones((ONES, tok), jnp.bfloat16)

    def land(t, carry):
        ik = land_s[t]
        for one in copies(0, 0, ik):
            one.wait()
        for kh in range(kv_heads):
            v = kv_s[ik, :, kvw + kh * HEAD_DIM : kvw + (kh + 1) * HEAD_DIM]
            vt_s[ik, kh, :HEAD_DIM] = v.astype(jnp.float32).T.astype(jnp.bfloat16)
            vt_s[ik, kh, HEAD_DIM:] = ones
        return carry

    lax.fori_loop(0, landed, land, 0)

    def blocks(qp, t):
        single = 2 * t + 1 >= full_s[qp]
        i0 = list_s[qp, 2 * t]
        i1 = list_s[qp, jnp.where(single, 2 * t, 2 * t + 1)]
        if mixed:
            left = lax.broadcasted_iota(jnp.int32, (STAT, rows), 1) < rows // 2
        bias = []
        for i in (i0, i1):
            for n in range(2):
                hidden = [
                    jnp.where(seen_s[part, 2 * i + n] > 0, jnp.float32(0.0), jnp.float32(NEG))
                    for part in ((0, 1) if mixed else (qp,))
                ]
                bias.append(jnp.where(left, hidden[0], hidden[1]) if mixed else hidden[0])
        again = jnp.where(single, jnp.float32(NEG), jnp.float32(0.0))
        bias[2:] = [one + again for one in bias[2:]]
        return i0, i1, bias

    def operands(kh, i0, i1):
        lanes = slice(kh * HEAD_DIM, (kh + 1) * HEAD_DIM)
        return (
            [jnp.concatenate([kv_s[i, :, lanes]] * 2, axis=1) for i in (i0, i1)],
            [vt_s[i, kh] for i in (i0, i1)],
        )

    def slow(units, qp, t):
        i0, i1, bias = blocks(qp, t)
        for h in range(heads):
            kh = h // GROUP
            unit = kh % UNITS
            s0_acc, s1_acc, pv_acc = units[unit]
            keys, values = operands(kh, i0, i1)
            pltpu.matmul_push_rhs(qt[qp, h], 0, unit)
            pltpu.matmul_acc_lhs(s0_acc, keys[0], 0)
            pltpu.matmul_acc_lhs(s1_acc, keys[1])
            s = [pltpu.matmul_pop(acc).reshape(-1, STAT, rows) for acc in (s0_acc, s1_acc)]
            before = st[qp, h, point]
            quarters = [x[n * (tok // 16) : (n + 1) * (tok // 16)] for x in s for n in range(2)]
            top = functools.reduce(jnp.maximum, [jnp.max(x, axis=0) + one for x, one in zip(quarters, bias)])
            now = jnp.maximum(before, jnp.max(top, axis=0, keepdims=True))
            for j, value in enumerate(values):
                p = [jnp.exp2(quarters[2 * j + n] - (now - bias[2 * j + n])[None]) for n in range(2)]
                p = jnp.concatenate(p, axis=0).reshape(tok, rows).astype(jnp.bfloat16)
                pltpu.matmul_push_rhs(p, 1, unit)
                pltpu.matmul_acc_lhs(pv_acc, value, 1)
            kept = st[qp, h, sums].reshape(-1, STAT, rows) * jnp.exp2(before - now)[None]
            st[qp, h, sums] = kept.reshape(-1, rows) + pltpu.matmul_pop(pv_acc)[sums]
            st[qp, h, point] = now

    def fast(units, qp, t):
        i0, i1, bias = blocks(qp, t)
        keys, values = zip(*[operands(kh, i0, i1) for kh in range(kv_heads)])

        def begin(kh, g):
            unit = units[kh % len(units)]
            pltpu.matmul_push_rhs(qt[qp, kh * GROUP + g], 0, kh % len(units))
            pltpu.matmul_acc_lhs(unit[0], keys[kh][0], 0)
            pltpu.matmul_acc_lhs(unit[1], keys[kh][1])

        def weights_of(kh, g, j):
            s = pltpu.matmul_pop(units[kh % len(units)][j]).reshape(-1, STAT, rows)
            ref = st[qp, kh * GROUP + g, point]
            p = [
                jnp.exp2(s[n * (tok // 16) : (n + 1) * (tok // 16)] - (ref - bias[2 * j + n])[None])
                for n in range(2)
            ]
            return jnp.concatenate(p, axis=0).reshape(tok, rows).astype(jnp.bfloat16)

        for first_kh in range(0, kv_heads, len(units)):
            together = range(first_kh, min(first_kh + len(units), kv_heads))
            for kh in together:
                begin(kh, 0)
            for g in range(GROUP):
                p = {(kh, j): weights_of(kh, g, j) for j in range(2) for kh in together}
                if g + 1 < GROUP:
                    for kh in together:
                        begin(kh, g + 1)
                for j in range(2):
                    for kh in together:
                        pltpu.matmul_push_rhs(p[kh, j], 1, kh % len(units))
                        pltpu.matmul_acc_lhs(units[kh % len(units)][2], values[kh][j], 1)
                for kh in together:
                    h = kh * GROUP + g
                    st[qp, h, sums] = st[qp, h, sums] + pltpu.matmul_pop(units[kh % len(units)][2])[sums]

    columns_of = slice(half * rows // 2, (half + 1) * rows // 2) if mixed else slice(0, rows)
    if mixed:
        for h in range(heads):
            qt_s[0, h] = jnp.concatenate([q_ref[part, h, :, columns_of] for part in range(2)], axis=1)
    for qp in range(tiles):
        full_s[qp] = counts[qp]
        count_s[qp] = (counts[qp] + 1) // 2

    def attempt(again, carry):
        @pl.when(jnp.logical_or(again == 0, top_s[0] > 0))
        def _():
            for qp in range(tiles):
                for h in range(heads):
                    if mixed:
                        st[0, h] = jnp.concatenate([state_in[part, h, :, columns_of] for part in range(2)], axis=1)
                    elif first:
                        st[qp, h, sums] = jnp.zeros((HEAD_DIM + STAT, rows), jnp.float32)
                        st[qp, h, point] = jnp.full((STAT, rows), NEG, jnp.float32)
                    else:
                        st[qp, h] = state_in[qp, h]

            def one_part(qp, carry):
                pairs = count_s[qp]
                switch = jnp.where(again > 0, pairs, 1 if first else 0)

                def both(*accs):
                    units = [accs[3 * unit : 3 * unit + 3] for unit in range(UNITS)]

                    def one_slow(t, carry):
                        slow(units, qp, t)
                        return carry

                    def one_fast(t, carry):
                        fast(units, qp, t)
                        return carry

                    lax.fori_loop(0, switch, one_slow, 0)
                    lax.fori_loop(switch, pairs, one_fast, 0)

                accumulators = []
                for unit in range(UNITS):
                    accumulators += [pltpu.ACC(unit)((tok, rows), jnp.float32)] * 2
                    accumulators.append(pltpu.ACC(unit)((HEAD_DIM + ONES, rows), jnp.float32))
                pl.run_scoped(both, *accumulators)
                return carry

            lax.fori_loop(0, tiles, one_part, 0)
            top = jnp.zeros((STAT, rows), jnp.float32)
            for qp in range(tiles):
                for h in range(heads):
                    top = jnp.maximum(top, jnp.where(st[qp, h, weights] < LARGE, 0.0, 1.0))
            top_s[0] = (jnp.max(top) > 0.0).astype(jnp.int32)

        return carry

    top_s[0] = 0
    lax.fori_loop(0, 2, attempt, 0)
    if last:
        for qp in range(tiles):
            for h in range(heads):
                lanes = slice(h * HEAD_DIM, (h + 1) * HEAD_DIM)
                inv = 1.0 / st[qp, h, weights]
                att = st[qp, h, :HEAD_DIM].reshape(-1, STAT, rows) * inv[None]
                att = att.reshape(HEAD_DIM, rows).T.astype(jnp.bfloat16)
                if mixed:
                    outs[0][:, lanes] = att[: rows // 2]
                    outs[1][:, lanes] = att[rows // 2 :]
                else:
                    outs[0][qp * rows : (qp + 1) * rows, lanes] = att


class GridPlace:
    def __init__(self, metas, n_a, n_b, tok):
        self.metas, self.n_a, self.n_b, self.tok = metas, n_a, n_b, tok

    def query(self, own, part):
        return (own // CORES) * CORES + (own % CORES + part) % CORES

    def sources(self, own, i, part):
        a, b, c = own // (CORES * self.n_b), (own // CORES) % self.n_b, own % CORES
        return [
            ((a ^ flip) * self.n_b + (b + db) % self.n_b) * CORES + (c + part) % CORES
            for _, _, flip, db in self.metas[i]
        ]

    def refs(self, items, i, part):
        rows = self.tok // 2
        return [items[n].at[pl.ds(base + part * rows, rows)] for n, base, _, _ in self.metas[i]]


class FlatPlace:
    def __init__(self, tok):
        self.tok = tok

    def query(self, own, part):
        return own

    def sources(self, own, i, part):
        return [i, i]

    def refs(self, items, i, part):
        return [items[0].at[pl.ds(i * self.tok, self.tok)]]


def other_columns(own, pieces):
    rows, width = pieces[0].shape
    half = width // CORES
    vmem = pl.BlockSpec(memory_space=pltpu.VMEM)

    def kernel(own_ref, *refs):
        lanes = pl.ds(pl.multiple_of((own_ref[0] + 1) % CORES * half, half), half)
        for i, ref in enumerate(refs[:-1]):
            refs[-1][i * rows : (i + 1) * rows] = ref[:, lanes]

    return pl.pallas_call(
        kernel,
        out_shape=jax.ShapeDtypeStruct((len(pieces) * rows, half), pieces[0].dtype),
        in_specs=[pl.BlockSpec(memory_space=pltpu.SMEM)] + [vmem] * len(pieces),
        out_specs=vmem,
        compiler_params=pltpu.CompilerParams(vmem_limit_bytes=VMEM_LIMIT),
        cost_estimate=LITTLE,
        name="other_columns",
    )(own, *pieces)


def moved(kernel, args, shapes, name):
    vmem = pl.BlockSpec(memory_space=pltpu.VMEM)
    return pl.pallas_call(
        kernel,
        out_shape=[jax.ShapeDtypeStruct(shape, jnp.bfloat16) for shape in shapes],
        in_specs=[pl.BlockSpec(memory_space=pltpu.SMEM)] + [vmem] * (len(args) - 1),
        out_specs=[vmem] * len(shapes),
        compiler_params=pltpu.CompilerParams(vmem_limit_bytes=VMEM_LIMIT),
        cost_estimate=LITTLE,
        name=name,
    )(*args)


def joined(own, above, below):
    rows, width = above.shape

    def kernel(own_ref, above_ref, below_ref, out_ref):
        out_ref[:rows] = above_ref[...]
        out_ref[rows:] = below_ref[...]

    return moved(kernel, (own, above, below), [(2 * rows, width)], "joined")[0]


def lower_half(own, x):
    rows, width = x.shape

    def kernel(own_ref, x_ref, out_ref):
        out_ref[...] = x_ref[rows // 2 :]

    return moved(kernel, (own, x), [(rows // 2, width)], "lower_half")[0]


def picked(own, at_ends, at_middle, n_a, n_b):
    rows, width = at_ends.shape

    def kernel(own_ref, ends_ref, middle_ref, whole_ref, half_ref):
        a = own_ref[0] // (CORES * n_b)
        at_end = jnp.logical_or(a == 0, a == n_a - 1)

        def take(ref):
            whole_ref[...] = ref[...]
            half_ref[...] = ref[: rows // 2]

        pl.when(at_end)(lambda: take(ends_ref))
        pl.when(jnp.logical_not(at_end))(lambda: take(middle_ref))

    return moved(kernel, (own, at_ends, at_middle), [(rows, width), (rows // 2, width)], "picked")


def turn(own, parts):
    pieces = [x for part in parts for x in part]
    heads = min(x.shape[1] for x in pieces) // HEAD_DIM
    rows = sum(x.shape[0] for x in parts[0])
    vmem = pl.BlockSpec(memory_space=pltpu.VMEM)

    def kernel(own_ref, *refs):
        begin = own_ref[0] % CORES * heads * HEAD_DIM
        at = 0
        for qp, part in enumerate(parts):
            some = refs[at : at + len(part)]
            at += len(part)
            for h in range(heads):
                turned = []
                for ref in some:
                    first = h * HEAD_DIM
                    if ref.shape[1] > heads * HEAD_DIM:
                        first = pl.multiple_of(begin + first, HEAD_DIM)
                    turned.append(ref[:, pl.ds(first, HEAD_DIM)].astype(jnp.float32).T)
                scaled = jnp.concatenate(turned, axis=1) * SCALE
                high = scaled.astype(jnp.bfloat16)
                refs[-1][qp, h, :HEAD_DIM] = high
                refs[-1][qp, h, HEAD_DIM:] = (scaled - high.astype(jnp.float32)).astype(jnp.bfloat16)

    return pl.pallas_call(
        kernel,
        out_shape=pltpu.VMEM((len(parts), heads, 2 * HEAD_DIM, rows), jnp.bfloat16),
        in_specs=[pl.BlockSpec(memory_space=pltpu.SMEM)] + [vmem] * len(pieces),
        out_specs=vmem,
        compiler_params=pltpu.CompilerParams(vmem_limit_bytes=VMEM_LIMIT),
        cost_estimate=LITTLE,
        name="turn",
    )(own, *pieces)


def attend(scalars, q, state, arrays, place, n_items, parts, tok, last, half=None):
    first = state is None
    heads, rows = q.shape[1], q.shape[3]
    width = arrays[0].shape[1]
    smem = pl.BlockSpec(memory_space=pltpu.SMEM)
    vmem = pl.BlockSpec(memory_space=pltpu.VMEM)
    args = list(scalars) + [pinned(q)] + ([] if first else [pinned(state)]) + list(arrays)
    specs = [smem] * 3 + [vmem] + ([] if first else [vmem])
    specs += [pl.BlockSpec(memory_space=pl.ANY)] * len(arrays)
    shape = (parts, heads, HEAD_DIM + 2 * STAT, rows)
    tile_shape = shape if half is None else (1,) + shape[1:]
    blocks = n_items * parts
    scratch = [
        pltpu.VMEM(tile_shape if last else (STAT, HEAD_DIM), jnp.float32),
        pltpu.VMEM((1,) + q.shape[1:] if half is not None else (ONES, HEAD_DIM), jnp.bfloat16),
        pltpu.VMEM((blocks, tok, width), jnp.bfloat16),
        pltpu.VMEM((blocks, heads // GROUP, HEAD_DIM + ONES, tok), jnp.bfloat16),
        pltpu.SMEM((parts, blocks + 1), jnp.int32),
        pltpu.SMEM((blocks + 1,), jnp.int32),
        pltpu.SMEM((parts, 2 * blocks), jnp.int32),
        pltpu.SMEM((parts,), jnp.int32),
        pltpu.SMEM((parts,), jnp.int32),
        pltpu.SMEM((1,), jnp.int32),
        pltpu.SemaphoreType.DMA((blocks, 2)),
    ]
    if last:
        out_shape = [jax.ShapeDtypeStruct((parts * rows, heads * HEAD_DIM), jnp.bfloat16)]
        if half is not None:
            out_shape = [jax.ShapeDtypeStruct((rows // 2, heads * HEAD_DIM), jnp.bfloat16)] * 2
    else:
        out_shape = [pltpu.VMEM(shape, jnp.float32)]

    def kernel(*refs):
        attend_kernel(place, n_items, parts, half, rows, tok, first, last, refs)

    return pl.pallas_call(
        kernel,
        out_shape=out_shape,
        in_specs=specs,
        out_specs=[vmem] * len(out_shape),
        scratch_shapes=scratch,
        compiler_params=pltpu.CompilerParams(vmem_limit_bytes=VMEM_LIMIT),
        cost_estimate=LITTLE,
        name="attend",
    )(*args)


def pinned(x):
    return pltpu.with_memory_space_constraint(x, pltpu.VMEM)


def fetch(weight):
    chunks = 12
    rows = weight.shape[0] // chunks

    def kernel(weight_ref, out_ref, sems):
        copies = [
            pltpu.make_async_copy(
                weight_ref.at[pl.ds(i * rows, rows)], out_ref.at[pl.ds(i * rows, rows)], sems.at[i]
            )
            for i in range(chunks)
        ]
        for one in copies:
            one.start()
        for one in copies:
            one.wait()

    return pl.pallas_call(
        kernel,
        out_shape=pltpu.VMEM(weight.shape, weight.dtype),
        in_specs=[pl.BlockSpec(memory_space=pltpu.HBM)],
        out_specs=pl.BlockSpec(memory_space=pltpu.VMEM),
        scratch_shapes=[pltpu.SemaphoreType.DMA((chunks,))],
        compiler_params=pltpu.CompilerParams(vmem_limit_bytes=VMEM_LIMIT),
        cost_estimate=LITTLE,
        name="fetch",
    )(pltpu.with_memory_space_constraint(weight, pltpu.HBM))


def project(own, parts, weight, rows, partial=None, ending=None):
    width = weight.shape[1]
    depth = parts[0][0].shape[1]
    tile = math.gcd(width, 512)
    smem = pl.BlockSpec(memory_space=pltpu.SMEM)
    vmem = pl.BlockSpec(memory_space=pltpu.VMEM)
    n = len(parts)
    args = [own] + [x for x, _, _ in parts] + [pinned(weight)]
    specs = [smem] + [vmem] * (n + 1)
    scratch = []
    out_shape = [jax.ShapeDtypeStruct((rows, width), jnp.bfloat16)]
    if partial is not None:
        args.append(pinned(partial))
        specs.append(vmem)
    elif ending is not None:
        args += list(ending)
        args[-2] = pltpu.with_memory_space_constraint(args[-2], pltpu.HBM)
        specs += [smem] * 2 + [pl.BlockSpec(memory_space=pltpu.HBM), vmem]
        out_shape = [pltpu.VMEM((rows, width), jnp.float32), pltpu.VMEM((STAT, width), jnp.float32)]
        scratch = [pltpu.VMEM((STAT, width), jnp.float32), pltpu.SemaphoreType.DMA]
    else:
        out_shape = [pltpu.VMEM((rows, width), jnp.float32)]

    def kernel(*refs):
        own_ref, part_refs, weight_ref, refs = refs[0], refs[1 : n + 1], refs[n + 1], refs[n + 2 :]
        if ending is not None:
            steps_ref, map_ref, gate_ref, residual_ref, out_ref, row_ref, near, sem = refs
            step = steps_ref[map_ref[own_ref[0]]]
            copy = pltpu.make_async_copy(
                gate_ref.at[pl.ds(pl.multiple_of((step // STAT) * STAT, STAT), STAT)], near, sem
            )
            copy.start()
            copy.wait()
            chosen = lax.broadcasted_iota(jnp.int32, (STAT, width), 0) == step % STAT
            row = jnp.sum(jnp.where(chosen, near[...], 0.0), axis=0, keepdims=True)
            row_ref[...] = jnp.broadcast_to(row, (STAT, width))
        else:
            out_ref = refs[-1]

        def one(t, carry):
            lanes = pl.ds(pl.multiple_of(t * tile, tile), tile)
            total = None
            for j in range(n):
                first_row = parts[j][2]
                group = (own_ref[0] + parts[j][1]) % CORES
                weight_rows = pl.ds(pl.multiple_of(group * depth, depth), depth)
                term = jnp.dot(
                    part_refs[j][first_row : first_row + rows],
                    weight_ref[weight_rows, lanes],
                    preferred_element_type=jnp.float32,
                )
                total = term if total is None else total + term
            if partial is not None:
                total = total + refs[0][:, lanes]
            if ending is not None:
                gate = jnp.concatenate([row_ref[:, lanes]] * (rows // STAT), axis=0)
                total = residual_ref[:, lanes].astype(jnp.float32) + gate * total
            out_ref[:, lanes] = total.astype(out_ref.dtype)
            return carry

        lax.fori_loop(0, width // tile, one, 0)

    return pl.pallas_call(
        kernel,
        out_shape=out_shape,
        in_specs=specs,
        out_specs=[vmem] * len(out_shape),
        scratch_shapes=scratch,
        compiler_params=pltpu.CompilerParams(vmem_limit_bytes=VMEM_LIMIT),
        cost_estimate=pl.CostEstimate(
            flops=2 * rows * depth * n * width, bytes_accessed=2 * depth * n * width, transcendentals=0
        ),
        name="project",
    )(*args)


def columns(x, part, width):
    return lax.dynamic_slice_in_dim(x, part * width, width, 1)


def paired(query_rows, key_rows, value_rows, out_weight, scalars, ending, n_a, n_b):
    n_seq = n_a * n_b * CORES
    groups = 2 * CORES
    own = scalars[0]
    kvw = key_rows.shape[1] // groups
    rows = query_rows.shape[0]
    tok = 2 * rows
    x = lax.axis_index("head")
    c = lax.axis_index("seq") % CORES

    def index(a, b, k):
        return (a * n_b + b) * CORES + k

    def swapped(piece, dx, dc):
        pairs = [
            ((s ^ dc) * 2 + (h ^ dx), s * 2 + h) for s in range(n_seq) for h in range(2)
        ]
        return lax.ppermute(piece, ("seq", "head"), pairs)

    def along_a(piece, moves):
        pairs = [
            (index(a, b, k), index(to, b, k)) for a, to in moves for b in range(n_b) for k in range(CORES)
        ]
        return lax.ppermute(piece, "seq", pairs)

    def beside_of(piece, only):
        pairs = [
            (index(a, 1 - b, k), index(a, b, k)) for a in only for b in range(n_b) for k in range(CORES)
        ]
        return lax.ppermute(piece, "seq", pairs)

    def stage(state, q, arrays, metas, last=False, half=None):
        return attend(
            scalars, q, state, arrays, GridPlace(metas, n_a, n_b, tok), len(metas), CORES, tok, last, half
        )

    def halves_of(first, base, flip, db):
        if isinstance(first, int):
            return [(first, base, flip, db), (first, base + tok, flip, db)]
        return [(n, base, flip, db) for n in first]

    def kv_for(dx, dc):
        j = (x ^ dx) * CORES + (c ^ dc)
        return jnp.concatenate([columns(key_rows, j, kvw), columns(value_rows, j, kvw)], axis=1)

    chips = list(range(n_a))
    order = [(0, 0), (1, 0), (0, 1), (1, 1)]
    pieces = {d: kv_for(*d) if sum(d) == 0 else swapped(kv_for(*d), *d) for d in order}
    early = jnp.concatenate([pieces[0, 0], pieces[0, 1]], axis=0)
    later = jnp.concatenate([pieces[1, 0], pieces[1, 1]], axis=0)
    block = jnp.concatenate([early, later], axis=0)
    qw = query_rows.shape[1] // 2
    q_own, q_other = columns(query_rows, x, qw), columns(query_rows, 1 - x, qw)
    block, early, later, out_weight, q_own, q_other = lax.optimization_barrier(
        (block, early, later, out_weight, q_own, q_other)
    )
    by_one, by_two = [(a, a ^ 1) for a in chips], [(a, a ^ 2) for a in chips]
    beside = beside_of(block, chips)
    next_early, far_early = along_a(early, by_one), along_a(early, by_two)
    q_came = swapped(q_other, 1, 0)
    weight = fetch(out_weight)
    beside, next_early, far_early, later, q_came, weight = lax.optimization_barrier(
        (beside, next_early, far_early, later, q_came, weight)
    )
    beside_early = beside_of(joined(own, next_early, far_early), chips)
    next_later, far_later = along_a(later, by_one), along_a(later, by_two)
    q_core = swapped(other_columns(own, [q_own, q_came]), 0, 1)
    q = turn(own, [[q_own, q_came], [q_core]])
    (state,) = stage(None, q, [block, beside], [halves_of(0, 0, 0, 0), halves_of(1, 0, 0, 1)])
    next_later, far_later, beside_early, again, state = lax.optimization_barrier(
        (next_later, far_later, beside_early, block, state)
    )
    beside_later = beside_of(joined(own, next_later, far_later), chips)
    to_ends = along_a(joined(own, far_early, far_later), [(1, 0), (2, 3)])
    to_middle = along_a(again, [(1, 2), (2, 1)])
    (state,) = stage(
        state, q, [next_early, next_later, far_early, far_later, beside_early],
        [halves_of((0, 1), 0, 1, 0), halves_of((2, 3), 0, 2, 0), [(4, 0, 1, 1), (4, tok, 2, 1)]],
    )
    to_ends, to_middle, beside_later, state = lax.optimization_barrier((to_ends, to_middle, beside_later, state))
    last, last_upper = picked(own, to_ends, to_middle, n_a, n_b)
    beside_last = [beside_of(last_upper, chips), along_a(lower_half(own, beside_later), by_one)]
    (state,) = stage(
        state, q, [beside_later, last], [[(0, 0, 1, 1), (0, tok, 2, 1)], halves_of(1, 0, 3, 0)]
    )
    last_block = [halves_of((0, 1), 0, 3, 1)]
    kept, sent = stage(state, q, beside_last, last_block, True, 1)
    came = swapped(sent, 0, 1)
    (begun,) = project(own, [(kept, 0, 0)], weight, rows)
    (theirs,) = project(own, [(came, 1, 0)], weight, rows, partial=begun)
    came_back = lax.ppermute(theirs, "head", [(0, 1), (1, 0)])
    state, theirs = lax.optimization_barrier((state, theirs))
    kept, sent = stage(state, q, beside_last, last_block, True, 0)
    came = swapped(sent, 0, 1)
    base, gate = project(own, [(kept, 0, 0), (came, 1, 0)], weight, rows, ending=ending)
    return (base + gate[:1] * came_back.astype(jnp.float32)).astype(jnp.bfloat16)


def gathered_attention(query_rows, key_rows, value_rows, scalars):
    spread = functools.partial(lax.all_to_all, axis_name="head", split_axis=1, concat_axis=0, tiled=True)
    local = jnp.concatenate([spread(key_rows), spread(value_rows)], axis=1)
    every = lax.all_gather(local, "seq", axis=0, tiled=True)
    tok = local.shape[0]
    return attend(
        scalars, turn(scalars[0], [[spread(query_rows)]]), None, [every], FlatPlace(tok), every.shape[0] // tok, 1, tok, True
    )[0]


def per_device(
    query_rows,
    key_rows,
    value_rows,
    residual,
    out_weight,
    gate_table,
    noise_steps,
    segment_mask,
    segment_map,
):
    n_seq = lax.axis_size("seq")
    n_head = lax.axis_size("head")
    own_seq = lax.axis_index("seq").astype(jnp.int32)
    own = own_seq.reshape(1)
    scalars = (own, segment_map, segment_mask)
    n_a, n_b = grid_of(n_seq)
    if n_head == 2 and n_a == 4 and n_b == 2:
        ending = (noise_steps, segment_map, gate_table, residual)
        return paired(query_rows, key_rows, value_rows, out_weight, scalars, ending, n_a, n_b)
    attended = gathered_attention(query_rows, key_rows, value_rows, scalars)
    projected = lax.psum_scatter(
        jnp.dot(attended, out_weight, preferred_element_type=jnp.float32).astype(jnp.bfloat16),
        "head",
        scatter_dimension=0,
        tiled=True,
    ).astype(jnp.float32)
    gate_row = lax.dynamic_slice_in_dim(gate_table, noise_steps[segment_map[own_seq]], 1, 0)
    return (residual.astype(jnp.float32) + gate_row * projected).astype(jnp.bfloat16)


def solution(mesh):
    placed = (
        P(("seq", "head"), None),
        P(("seq", "head"), None),
        P(("seq", "head"), None),
        P(("seq", "head"), None),
        P("head", None),
        P(),
        P(),
        P(),
        P(),
    )
    return jax.shard_map(
        per_device, mesh=mesh, in_specs=placed, out_specs=P(("seq", "head"), None), check_vma=False
    )
```

```python
import functools
import math

import jax
import jax.numpy as jnp
from jax import lax
from jax.experimental import pallas as pl
from jax.experimental.pallas import tpu as pltpu
from jax.sharding import PartitionSpec as P

Q_HEADS = 24
KV_HEADS = 8
HEAD_DIM = 128
GROUP = Q_HEADS // KV_HEADS
CORES = 2
UNITS = 2
NEG = -1e30
SCALE = 1.4426950408889634 * HEAD_DIM ** -0.5
STAT = 8
ONES = 16
LARGE = 1e27
VMEM_LIMIT = 24 * 1024 * 1024
LITTLE = pl.CostEstimate(flops=1, bytes_accessed=1, transcendentals=0)


def grid_of(n_seq):
    chips = n_seq // CORES
    inner = 2 ** (int(math.log2(chips)) // 2)
    return chips // inner, inner


def attend_kernel(place, n_items, parts, half, rows, tok, first, last, refs):
    own_ref, map_ref, mask_ref, q_ref = refs[:4]
    mixed = half is not None
    tiles = 1 if mixed else parts
    state_in = None if first else refs[4]
    st_s, qt_s, kv_s, vt_s, list_s, land_s, seen_s, full_s, count_s, top_s, sems = refs[-11:]
    outs = 2 if mixed else 1
    items, outs = refs[4 if first else 5 : -11 - outs], refs[-11 - outs : -11]
    st, qt = st_s if last else outs[0], qt_s if mixed else q_ref
    heads = qt.shape[1]
    kv_heads = heads // GROUP
    kvw = kv_heads * HEAD_DIM
    own = own_ref[0]
    sums = slice(0, HEAD_DIM + STAT)
    weights = slice(HEAD_DIM, HEAD_DIM + STAT)
    point = slice(HEAD_DIM + STAT, HEAD_DIM + 2 * STAT)

    def copies(i, kp, ik):
        pieces = place.refs(items, i, kp)
        size = tok // len(pieces)
        return [
            pltpu.make_async_copy(piece, kv_s.at[ik, pl.ds(j * size, size)], sems.at[ik, j])
            for j, piece in enumerate(pieces)
        ]

    seg_q = [map_ref[place.query(own, j)] for j in range(parts)]
    counts = [jnp.int32(0)] * tiles
    landed = jnp.int32(0)
    for i in range(n_items):
        for kp in range(parts):
            ik = i * parts + kp
            seg_k = [map_ref[src] for src in place.sources(own, i, kp)]
            any_seen = jnp.int32(0)
            for qp in range(parts):
                seen = jnp.int32(0)
                for n in range(2):
                    seen_half = (mask_ref[seg_q[qp], seg_k[n]] > 0).astype(jnp.int32)
                    seen_s[qp, 2 * ik + n] = seen_half
                    seen = jnp.maximum(seen, seen_half)
                any_seen = jnp.maximum(any_seen, seen)
                if not mixed:
                    list_s[qp, counts[qp]] = ik
                    counts[qp] = counts[qp] + seen
            if mixed:
                list_s[0, counts[0]] = ik
                counts[0] = counts[0] + any_seen
            land_s[landed] = ik
            landed = landed + any_seen

            @pl.when(any_seen > 0)
            def _():
                if place.near:
                    pieces = place.refs(items, i, kp)
                    size = tok // len(pieces)
                    for j, piece in enumerate(pieces):
                        kv_s[ik, j * size : (j + 1) * size] = piece[...]
                else:
                    for one in copies(i, kp, ik):
                        one.start()

    ones = jnp.ones((ONES, tok), jnp.bfloat16)

    def land(t, carry):
        ik = land_s[t]
        if not place.near:
            for one in copies(0, 0, ik):
                one.wait()
        for kh in range(kv_heads):
            v = kv_s[ik, :, kvw + kh * HEAD_DIM : kvw + (kh + 1) * HEAD_DIM]
            vt_s[ik, kh, :HEAD_DIM] = v.T
            vt_s[ik, kh, HEAD_DIM:] = ones
        return carry

    lax.fori_loop(0, landed, land, 0)

    def blocks(qp, t):
        single = 2 * t + 1 >= full_s[qp]
        i0 = list_s[qp, 2 * t]
        i1 = list_s[qp, jnp.where(single, 2 * t, 2 * t + 1)]
        if mixed:
            left = lax.broadcasted_iota(jnp.int32, (STAT, rows), 1) < rows // 2
        bias = []
        for i in (i0, i1):
            for n in range(2):
                hidden = [
                    jnp.where(seen_s[part, 2 * i + n] > 0, jnp.float32(0.0), jnp.float32(NEG))
                    for part in ((0, 1) if mixed else (qp,))
                ]
                bias.append(jnp.where(left, hidden[0], hidden[1]) if mixed else hidden[0])
        again = jnp.where(single, jnp.float32(NEG), jnp.float32(0.0))
        bias[2:] = [one + again for one in bias[2:]]
        return i0, i1, bias

    def operands(kh, i0, i1):
        lanes = slice(kh * HEAD_DIM, (kh + 1) * HEAD_DIM)
        return (
            [jnp.concatenate([kv_s[i, :, lanes]] * 2, axis=1) for i in (i0, i1)],
            [vt_s[i, kh] for i in (i0, i1)],
        )

    def slow(units, qp, t):
        i0, i1, bias = blocks(qp, t)
        for h in range(heads):
            kh = h // GROUP
            unit = kh % UNITS
            s0_acc, s1_acc, pv_acc = units[unit]
            keys, values = operands(kh, i0, i1)
            pltpu.matmul_push_rhs(qt[qp, h], 0, unit)
            pltpu.matmul_acc_lhs(s0_acc, keys[0], 0)
            pltpu.matmul_acc_lhs(s1_acc, keys[1])
            s = [pltpu.matmul_pop(acc).reshape(-1, STAT, rows) for acc in (s0_acc, s1_acc)]
            before = st[qp, h, point]
            quarters = [x[n * (tok // 16) : (n + 1) * (tok // 16)] for x in s for n in range(2)]
            top = functools.reduce(jnp.maximum, [jnp.max(x, axis=0) + one for x, one in zip(quarters, bias)])
            now = jnp.maximum(before, jnp.max(top, axis=0, keepdims=True))
            for j, value in enumerate(values):
                p = [jnp.exp2(quarters[2 * j + n] - (now - bias[2 * j + n])[None]) for n in range(2)]
                p = jnp.concatenate(p, axis=0).reshape(tok, rows).astype(jnp.bfloat16)
                pltpu.matmul_push_rhs(p, 1, unit)
                pltpu.matmul_acc_lhs(pv_acc, value, 1)
            kept = st[qp, h, sums].reshape(-1, STAT, rows) * jnp.exp2(before - now)[None]
            st[qp, h, sums] = kept.reshape(-1, rows) + pltpu.matmul_pop(pv_acc)[sums]
            st[qp, h, point] = now

    def fast(units, qp, t):
        i0, i1, bias = blocks(qp, t)
        keys, values = zip(*[operands(kh, i0, i1) for kh in range(kv_heads)])

        def begin(kh, g):
            unit = units[kh % len(units)]
            pltpu.matmul_push_rhs(qt[qp, kh * GROUP + g], 0, kh % len(units))
            pltpu.matmul_acc_lhs(unit[0], keys[kh][0], 0)
            pltpu.matmul_acc_lhs(unit[1], keys[kh][1])

        def weights_of(kh, g, j):
            s = pltpu.matmul_pop(units[kh % len(units)][j]).reshape(-1, STAT, rows)
            ref = st[qp, kh * GROUP + g, point]
            p = [
                jnp.exp2(s[n * (tok // 16) : (n + 1) * (tok // 16)] - (ref - bias[2 * j + n])[None])
                for n in range(2)
            ]
            return jnp.concatenate(p, axis=0).reshape(tok, rows).astype(jnp.bfloat16)

        for first_kh in range(0, kv_heads, len(units)):
            together = range(first_kh, min(first_kh + len(units), kv_heads))
            for kh in together:
                begin(kh, 0)
            for g in range(GROUP):
                p = {(kh, j): weights_of(kh, g, j) for j in range(2) for kh in together}
                if g + 1 < GROUP:
                    for kh in together:
                        begin(kh, g + 1)
                for j in range(2):
                    for kh in together:
                        pltpu.matmul_push_rhs(p[kh, j], 1, kh % len(units))
                        pltpu.matmul_acc_lhs(units[kh % len(units)][2], values[kh][j], 1)
                for kh in together:
                    h = kh * GROUP + g
                    st[qp, h, sums] = st[qp, h, sums] + pltpu.matmul_pop(units[kh % len(units)][2])[sums]

    columns_of = slice(half * rows // 2, (half + 1) * rows // 2) if mixed else slice(0, rows)
    if mixed:
        for h in range(heads):
            qt_s[0, h] = jnp.concatenate([q_ref[part, h, :, columns_of] for part in range(2)], axis=1)
    for qp in range(tiles):
        full_s[qp] = counts[qp]
        count_s[qp] = (counts[qp] + 1) // 2

    def attempt(again, carry):
        @pl.when(jnp.logical_or(again == 0, top_s[0] > 0))
        def _():
            for qp in range(tiles):
                for h in range(heads):
                    if mixed:
                        st[0, h] = jnp.concatenate([state_in[part, h, :, columns_of] for part in range(2)], axis=1)
                    elif first:
                        st[qp, h, sums] = jnp.zeros((HEAD_DIM + STAT, rows), jnp.float32)
                        st[qp, h, point] = jnp.full((STAT, rows), NEG, jnp.float32)
                    else:
                        st[qp, h] = state_in[qp, h]

            def one_part(qp, carry):
                pairs = count_s[qp]
                switch = jnp.where(again > 0, pairs, 1 if first else 0)

                def both(*accs):
                    units = [accs[3 * unit : 3 * unit + 3] for unit in range(UNITS)]

                    def one_slow(t, carry):
                        slow(units, qp, t)
                        return carry

                    def one_fast(t, carry):
                        fast(units, qp, t)
                        return carry

                    lax.fori_loop(0, switch, one_slow, 0)
                    lax.fori_loop(switch, pairs, one_fast, 0)

                accumulators = []
                for unit in range(UNITS):
                    accumulators += [pltpu.ACC(unit)((tok, rows), jnp.float32)] * 2
                    accumulators.append(pltpu.ACC(unit)((HEAD_DIM + ONES, rows), jnp.float32))
                pl.run_scoped(both, *accumulators)
                return carry

            lax.fori_loop(0, tiles, one_part, 0)
            top = jnp.zeros((STAT, rows), jnp.float32)
            for qp in range(tiles):
                for h in range(heads):
                    top = jnp.maximum(top, jnp.where(st[qp, h, weights] < LARGE, 0.0, 1.0))
            top_s[0] = (jnp.max(top) > 0.0).astype(jnp.int32)

        return carry

    top_s[0] = 0
    lax.fori_loop(0, 2, attempt, 0)
    if last:
        for qp in range(tiles):
            for h in range(heads):
                lanes = slice(h * HEAD_DIM, (h + 1) * HEAD_DIM)
                inv = 1.0 / st[qp, h, weights]
                att = st[qp, h, :HEAD_DIM].reshape(-1, STAT, rows) * inv[None]
                att = att.reshape(HEAD_DIM, rows).T.astype(jnp.bfloat16)
                if mixed:
                    outs[0][:, lanes] = att[: rows // 2]
                    outs[1][:, lanes] = att[rows // 2 :]
                else:
                    outs[0][qp * rows : (qp + 1) * rows, lanes] = att


class GridPlace:
    near = True

    def __init__(self, metas, n_a, n_b, tok):
        self.metas, self.n_a, self.n_b, self.tok = metas, n_a, n_b, tok

    def query(self, own, part):
        return (own // CORES) * CORES + (own % CORES + part) % CORES

    def sources(self, own, i, part):
        a, b, c = own // (CORES * self.n_b), (own // CORES) % self.n_b, own % CORES
        return [
            ((a ^ flip) * self.n_b + (b + db) % self.n_b) * CORES + (c + part) % CORES
            for _, _, flip, db in self.metas[i]
        ]

    def refs(self, items, i, part):
        rows = self.tok // 2
        return [items[n].at[pl.ds(base + part * rows, rows)] for n, base, _, _ in self.metas[i]]


class FlatPlace:
    near = False

    def __init__(self, tok):
        self.tok = tok

    def query(self, own, part):
        return own

    def sources(self, own, i, part):
        return [i, i]

    def refs(self, items, i, part):
        return [items[0].at[pl.ds(i * self.tok, self.tok)]]


def other_columns(own, pieces):
    rows, width = pieces[0].shape
    half = width // CORES
    vmem = pl.BlockSpec(memory_space=pltpu.VMEM)

    def kernel(own_ref, *refs):
        lanes = pl.ds(pl.multiple_of((own_ref[0] + 1) % CORES * half, half), half)
        for i, ref in enumerate(refs[:-1]):
            refs[-1][i * rows : (i + 1) * rows] = ref[:, lanes]

    return pl.pallas_call(
        kernel,
        out_shape=jax.ShapeDtypeStruct((len(pieces) * rows, half), pieces[0].dtype),
        in_specs=[pl.BlockSpec(memory_space=pltpu.SMEM)] + [vmem] * len(pieces),
        out_specs=vmem,
        compiler_params=pltpu.CompilerParams(vmem_limit_bytes=VMEM_LIMIT),
        cost_estimate=LITTLE,
        name="other_columns",
    )(own, *pieces)


def moved(kernel, args, shapes, name):
    vmem = pl.BlockSpec(memory_space=pltpu.VMEM)
    return pl.pallas_call(
        kernel,
        out_shape=[jax.ShapeDtypeStruct(shape, jnp.bfloat16) for shape in shapes],
        in_specs=[pl.BlockSpec(memory_space=pltpu.SMEM)] + [vmem] * (len(args) - 1),
        out_specs=[vmem] * len(shapes),
        compiler_params=pltpu.CompilerParams(vmem_limit_bytes=VMEM_LIMIT),
        cost_estimate=LITTLE,
        name=name,
    )(*args)


def joined(own, above, below):
    rows, width = above.shape

    def kernel(own_ref, above_ref, below_ref, out_ref):
        out_ref[:rows] = above_ref[...]
        out_ref[rows:] = below_ref[...]

    return moved(kernel, (own, above, below), [(2 * rows, width)], "joined")[0]


def lower_half(own, x):
    rows, width = x.shape

    def kernel(own_ref, x_ref, out_ref):
        out_ref[...] = x_ref[rows // 2 :]

    return moved(kernel, (own, x), [(rows // 2, width)], "lower_half")[0]


def picked(own, at_ends, at_middle, n_a, n_b):
    rows, width = at_ends.shape

    def kernel(own_ref, ends_ref, middle_ref, whole_ref, half_ref):
        a = own_ref[0] // (CORES * n_b)
        at_end = jnp.logical_or(a == 0, a == n_a - 1)

        def take(ref):
            whole_ref[...] = ref[...]
            half_ref[...] = ref[: rows // 2]

        pl.when(at_end)(lambda: take(ends_ref))
        pl.when(jnp.logical_not(at_end))(lambda: take(middle_ref))

    return moved(kernel, (own, at_ends, at_middle), [(rows, width), (rows // 2, width)], "picked")


def turn(own, parts):
    pieces = [x for part in parts for x in part]
    heads = min(x.shape[1] for x in pieces) // HEAD_DIM
    rows = sum(x.shape[0] for x in parts[0])
    vmem = pl.BlockSpec(memory_space=pltpu.VMEM)

    def kernel(own_ref, *refs):
        begin = own_ref[0] % CORES * heads * HEAD_DIM
        at = 0
        for qp, part in enumerate(parts):
            some = refs[at : at + len(part)]
            at += len(part)
            for h in range(heads):
                turned = []
                for ref in some:
                    first = h * HEAD_DIM
                    if ref.shape[1] > heads * HEAD_DIM:
                        first = pl.multiple_of(begin + first, HEAD_DIM)
                    turned.append(ref[:, pl.ds(first, HEAD_DIM)].astype(jnp.float32).T)
                scaled = jnp.concatenate(turned, axis=1) * SCALE
                high = scaled.astype(jnp.bfloat16)
                refs[-1][qp, h, :HEAD_DIM] = high
                refs[-1][qp, h, HEAD_DIM:] = (scaled - high.astype(jnp.float32)).astype(jnp.bfloat16)

    return pl.pallas_call(
        kernel,
        out_shape=pltpu.VMEM((len(parts), heads, 2 * HEAD_DIM, rows), jnp.bfloat16),
        in_specs=[pl.BlockSpec(memory_space=pltpu.SMEM)] + [vmem] * len(pieces),
        out_specs=vmem,
        compiler_params=pltpu.CompilerParams(vmem_limit_bytes=VMEM_LIMIT),
        cost_estimate=LITTLE,
        name="turn",
    )(own, *pieces)


def attend(scalars, q, state, arrays, place, n_items, parts, tok, last, half=None):
    first = state is None
    heads, rows = q.shape[1], q.shape[3]
    width = arrays[0].shape[1]
    smem = pl.BlockSpec(memory_space=pltpu.SMEM)
    vmem = pl.BlockSpec(memory_space=pltpu.VMEM)
    args = list(scalars) + [pinned(q)] + ([] if first else [pinned(state)])
    args += [pinned(x) if place.near else x for x in arrays]
    specs = [smem] * 3 + [vmem] + ([] if first else [vmem])
    specs += [vmem if place.near else pl.BlockSpec(memory_space=pl.ANY)] * len(arrays)
    shape = (parts, heads, HEAD_DIM + 2 * STAT, rows)
    tile_shape = shape if half is None else (1,) + shape[1:]
    blocks = n_items * parts
    scratch = [
        pltpu.VMEM(tile_shape if last else (STAT, HEAD_DIM), jnp.float32),
        pltpu.VMEM((1,) + q.shape[1:] if half is not None else (ONES, HEAD_DIM), jnp.bfloat16),
        pltpu.VMEM((blocks, tok, width), jnp.bfloat16),
        pltpu.VMEM((blocks, heads // GROUP, HEAD_DIM + ONES, tok), jnp.bfloat16),
        pltpu.SMEM((parts, blocks + 1), jnp.int32),
        pltpu.SMEM((blocks + 1,), jnp.int32),
        pltpu.SMEM((parts, 2 * blocks), jnp.int32),
        pltpu.SMEM((parts,), jnp.int32),
        pltpu.SMEM((parts,), jnp.int32),
        pltpu.SMEM((1,), jnp.int32),
        pltpu.SemaphoreType.DMA((blocks, 2)),
    ]
    if last:
        out_shape = [jax.ShapeDtypeStruct((parts * rows, heads * HEAD_DIM), jnp.bfloat16)]
        if half is not None:
            out_shape = [jax.ShapeDtypeStruct((rows // 2, heads * HEAD_DIM), jnp.bfloat16)] * 2
    else:
        out_shape = [pltpu.VMEM(shape, jnp.float32)]

    def kernel(*refs):
        attend_kernel(place, n_items, parts, half, rows, tok, first, last, refs)

    return pl.pallas_call(
        kernel,
        out_shape=out_shape,
        in_specs=specs,
        out_specs=[vmem] * len(out_shape),
        scratch_shapes=scratch,
        compiler_params=pltpu.CompilerParams(vmem_limit_bytes=VMEM_LIMIT),
        cost_estimate=LITTLE,
        name="attend",
    )(*args)


def pinned(x):
    return pltpu.with_memory_space_constraint(x, pltpu.VMEM)


def fetch(weight):
    chunks = 12
    rows = weight.shape[0] // chunks

    def kernel(weight_ref, out_ref, sems):
        copies = [
            pltpu.make_async_copy(
                weight_ref.at[pl.ds(i * rows, rows)], out_ref.at[pl.ds(i * rows, rows)], sems.at[i]
            )
            for i in range(chunks)
        ]
        for one in copies:
            one.start()
        for one in copies:
            one.wait()

    return pl.pallas_call(
        kernel,
        out_shape=pltpu.VMEM(weight.shape, weight.dtype),
        in_specs=[pl.BlockSpec(memory_space=pltpu.HBM)],
        out_specs=pl.BlockSpec(memory_space=pltpu.VMEM),
        scratch_shapes=[pltpu.SemaphoreType.DMA((chunks,))],
        compiler_params=pltpu.CompilerParams(vmem_limit_bytes=VMEM_LIMIT),
        cost_estimate=LITTLE,
        name="fetch",
    )(pltpu.with_memory_space_constraint(weight, pltpu.HBM))


def project(own, parts, weight, rows, partial=None, ending=None):
    width = weight.shape[1]
    depth = parts[0][0].shape[1]
    tile = math.gcd(width, 512)
    smem = pl.BlockSpec(memory_space=pltpu.SMEM)
    vmem = pl.BlockSpec(memory_space=pltpu.VMEM)
    n = len(parts)
    args = [own] + [x for x, _, _ in parts] + [pinned(weight)]
    specs = [smem] + [vmem] * (n + 1)
    scratch = []
    out_shape = [jax.ShapeDtypeStruct((rows, width), jnp.bfloat16)]
    if partial is not None:
        args.append(pinned(partial))
        specs.append(vmem)
    elif ending is not None:
        args += list(ending)
        args[-2] = pltpu.with_memory_space_constraint(args[-2], pltpu.HBM)
        specs += [smem] * 2 + [pl.BlockSpec(memory_space=pltpu.HBM), vmem]
        out_shape = [pltpu.VMEM((rows, width), jnp.float32), pltpu.VMEM((STAT, width), jnp.float32)]
        scratch = [pltpu.VMEM((STAT, width), jnp.float32), pltpu.SemaphoreType.DMA]
    else:
        out_shape = [pltpu.VMEM((rows, width), jnp.float32)]

    def kernel(*refs):
        own_ref, part_refs, weight_ref, refs = refs[0], refs[1 : n + 1], refs[n + 1], refs[n + 2 :]
        if ending is not None:
            steps_ref, map_ref, gate_ref, residual_ref, out_ref, row_ref, near, sem = refs
            step = steps_ref[map_ref[own_ref[0]]]
            copy = pltpu.make_async_copy(
                gate_ref.at[pl.ds(pl.multiple_of((step // STAT) * STAT, STAT), STAT)], near, sem
            )
            copy.start()
            copy.wait()
            chosen = lax.broadcasted_iota(jnp.int32, (STAT, width), 0) == step % STAT
            row = jnp.sum(jnp.where(chosen, near[...], 0.0), axis=0, keepdims=True)
            row_ref[...] = jnp.broadcast_to(row, (STAT, width))
        else:
            out_ref = refs[-1]

        def one(t, carry):
            lanes = pl.ds(pl.multiple_of(t * tile, tile), tile)
            total = None
            for j in range(n):
                first_row = parts[j][2]
                group = (own_ref[0] + parts[j][1]) % CORES
                weight_rows = pl.ds(pl.multiple_of(group * depth, depth), depth)
                term = jnp.dot(
                    part_refs[j][first_row : first_row + rows],
                    weight_ref[weight_rows, lanes],
                    preferred_element_type=jnp.float32,
                )
                total = term if total is None else total + term
            if partial is not None:
                total = total + refs[0][:, lanes]
            if ending is not None:
                gate = jnp.concatenate([row_ref[:, lanes]] * (rows // STAT), axis=0)
                total = residual_ref[:, lanes].astype(jnp.float32) + gate * total
            out_ref[:, lanes] = total.astype(out_ref.dtype)
            return carry

        lax.fori_loop(0, width // tile, one, 0)

    return pl.pallas_call(
        kernel,
        out_shape=out_shape,
        in_specs=specs,
        out_specs=[vmem] * len(out_shape),
        scratch_shapes=scratch,
        compiler_params=pltpu.CompilerParams(vmem_limit_bytes=VMEM_LIMIT),
        cost_estimate=pl.CostEstimate(
            flops=2 * rows * depth * n * width, bytes_accessed=2 * depth * n * width, transcendentals=0
        ),
        name="project",
    )(*args)


def columns(x, part, width):
    return lax.dynamic_slice_in_dim(x, part * width, width, 1)


def paired(query_rows, key_rows, value_rows, out_weight, scalars, ending, n_a, n_b):
    n_seq = n_a * n_b * CORES
    groups = 2 * CORES
    own = scalars[0]
    kvw = key_rows.shape[1] // groups
    rows = query_rows.shape[0]
    tok = 2 * rows
    x = lax.axis_index("head")
    c = lax.axis_index("seq") % CORES

    def index(a, b, k):
        return (a * n_b + b) * CORES + k

    def swapped(piece, dx, dc):
        pairs = [
            ((s ^ dc) * 2 + (h ^ dx), s * 2 + h) for s in range(n_seq) for h in range(2)
        ]
        return lax.ppermute(piece, ("seq", "head"), pairs)

    def along_a(piece, moves):
        pairs = [
            (index(a, b, k), index(to, b, k)) for a, to in moves for b in range(n_b) for k in range(CORES)
        ]
        return lax.ppermute(piece, "seq", pairs)

    def beside_of(piece, only):
        pairs = [
            (index(a, 1 - b, k), index(a, b, k)) for a in only for b in range(n_b) for k in range(CORES)
        ]
        return lax.ppermute(piece, "seq", pairs)

    def stage(state, q, arrays, metas, last=False, half=None):
        return attend(
            scalars, q, state, arrays, GridPlace(metas, n_a, n_b, tok), len(metas), CORES, tok, last, half
        )

    def halves_of(first, base, flip, db):
        if isinstance(first, int):
            return [(first, base, flip, db), (first, base + tok, flip, db)]
        return [(n, base, flip, db) for n in first]

    def kv_for(dx, dc):
        j = (x ^ dx) * CORES + (c ^ dc)
        return jnp.concatenate([columns(key_rows, j, kvw), columns(value_rows, j, kvw)], axis=1)

    chips = list(range(n_a))
    order = [(0, 0), (1, 0), (0, 1), (1, 1)]
    pieces = {d: kv_for(*d) if sum(d) == 0 else swapped(kv_for(*d), *d) for d in order}
    early = jnp.concatenate([pieces[0, 0], pieces[0, 1]], axis=0)
    later = jnp.concatenate([pieces[1, 0], pieces[1, 1]], axis=0)
    block = jnp.concatenate([early, later], axis=0)
    qw = query_rows.shape[1] // 2
    q_own, q_other = columns(query_rows, x, qw), columns(query_rows, 1 - x, qw)
    block, early, later, out_weight, q_own, q_other = lax.optimization_barrier(
        (block, early, later, out_weight, q_own, q_other)
    )
    by_one, by_two = [(a, a ^ 1) for a in chips], [(a, a ^ 2) for a in chips]
    beside = beside_of(block, chips)
    next_early, far_early = along_a(early, by_one), along_a(early, by_two)
    q_came = swapped(q_other, 1, 0)
    weight = fetch(out_weight)
    beside, next_early, far_early, q_came, weight = lax.optimization_barrier(
        (beside, next_early, far_early, q_came, weight)
    )
    beside_early = beside_of(joined(own, next_early, far_early), chips)
    next_later, far_later = along_a(later, by_one), along_a(later, by_two)
    q_core = swapped(other_columns(own, [q_own, q_came]), 0, 1)
    q = turn(own, [[q_own, q_came], [q_core]])
    (state,) = stage(None, q, [block, beside], [halves_of(0, 0, 0, 0), halves_of(1, 0, 0, 1)])
    again, state = lax.optimization_barrier((block, state))
    to_middle = along_a(again, [(1, 2), (2, 1)])
    next_later, far_later, beside_early, state = lax.optimization_barrier(
        (next_later, far_later, beside_early, state)
    )
    beside_later = beside_of(joined(own, next_later, far_later), chips)
    to_ends = along_a(joined(own, far_early, far_later), [(1, 0), (2, 3)])
    (state,) = stage(
        state, q, [next_early, next_later, far_early, far_later],
        [halves_of((0, 1), 0, 1, 0), halves_of((2, 3), 0, 2, 0)],
    )
    to_middle, state = lax.optimization_barrier((to_middle, state))
    (state,) = stage(state, q, [beside_early], [[(0, 0, 1, 1), (0, tok, 2, 1)]])
    to_ends, to_middle, beside_later, state = lax.optimization_barrier((to_ends, to_middle, beside_later, state))
    last, last_upper = picked(own, to_ends, to_middle, n_a, n_b)
    beside_last = [beside_of(last_upper, chips), along_a(lower_half(own, beside_later), by_one)]
    (state,) = stage(
        state, q, [beside_later, last], [[(0, 0, 1, 1), (0, tok, 2, 1)], halves_of(1, 0, 3, 0)]
    )
    last_block = [halves_of((0, 1), 0, 3, 1)]
    kept, sent = stage(state, q, beside_last, last_block, True, 1)
    came = swapped(sent, 0, 1)
    (begun,) = project(own, [(kept, 0, 0)], weight, rows)
    (theirs,) = project(own, [(came, 1, 0)], weight, rows, partial=begun)
    came_back = lax.ppermute(theirs, "head", [(0, 1), (1, 0)])
    state, theirs = lax.optimization_barrier((state, theirs))
    kept, sent = stage(state, q, beside_last, last_block, True, 0)
    came = swapped(sent, 0, 1)
    base, gate = project(own, [(kept, 0, 0), (came, 1, 0)], weight, rows, ending=ending)
    return (base + gate[:1] * came_back.astype(jnp.float32)).astype(jnp.bfloat16)


def gathered_attention(query_rows, key_rows, value_rows, scalars):
    spread = functools.partial(lax.all_to_all, axis_name="head", split_axis=1, concat_axis=0, tiled=True)
    local = jnp.concatenate([spread(key_rows), spread(value_rows)], axis=1)
    every = lax.all_gather(local, "seq", axis=0, tiled=True)
    tok = local.shape[0]
    return attend(
        scalars, turn(scalars[0], [[spread(query_rows)]]), None, [every], FlatPlace(tok), every.shape[0] // tok, 1, tok, True
    )[0]


def per_device(
    query_rows,
    key_rows,
    value_rows,
    residual,
    out_weight,
    gate_table,
    noise_steps,
    segment_mask,
    segment_map,
):
    n_seq = lax.axis_size("seq")
    n_head = lax.axis_size("head")
    own_seq = lax.axis_index("seq").astype(jnp.int32)
    own = own_seq.reshape(1)
    scalars = (own, segment_map, segment_mask)
    n_a, n_b = grid_of(n_seq)
    if n_head == 2 and n_a == 4 and n_b == 2:
        ending = (noise_steps, segment_map, gate_table, residual)
        return paired(query_rows, key_rows, value_rows, out_weight, scalars, ending, n_a, n_b)
    attended = gathered_attention(query_rows, key_rows, value_rows, scalars)
    projected = lax.psum_scatter(
        jnp.dot(attended, out_weight, preferred_element_type=jnp.float32).astype(jnp.bfloat16),
        "head",
        scatter_dimension=0,
        tiled=True,
    ).astype(jnp.float32)
    gate_row = lax.dynamic_slice_in_dim(gate_table, noise_steps[segment_map[own_seq]], 1, 0)
    return (residual.astype(jnp.float32) + gate_row * projected).astype(jnp.bfloat16)


def solution(mesh):
    placed = (
        P(("seq", "head"), None),
        P(("seq", "head"), None),
        P(("seq", "head"), None),
        P(("seq", "head"), None),
        P("head", None),
        P(),
        P(),
        P(),
        P(),
    )
    return jax.shard_map(
        per_device, mesh=mesh, in_specs=placed, out_specs=P(("seq", "head"), None), check_vma=False
    )
```

```python
import functools
import math

import jax
import jax.numpy as jnp
from jax import lax
from jax.experimental import pallas as pl
from jax.experimental.pallas import tpu as pltpu
from jax.sharding import PartitionSpec as P

Q_HEADS = 24
KV_HEADS = 8
HEAD_DIM = 128
GROUP = Q_HEADS // KV_HEADS
CORES = 2
UNITS = 2
NEG = -1e30
SCALE = 1.4426950408889634 * HEAD_DIM ** -0.5
STAT = 8
ONES = 16
LARGE = 1e27
VMEM_LIMIT = 24 * 1024 * 1024
SOME = pl.CostEstimate(flops=3000000000, bytes_accessed=1, transcendentals=0)
LITTLE = pl.CostEstimate(flops=1, bytes_accessed=1, transcendentals=0)


def grid_of(n_seq):
    chips = n_seq // CORES
    inner = 2 ** (int(math.log2(chips)) // 2)
    return chips // inner, inner


def attend_kernel(place, n_items, parts, half, rows, tok, first, last, refs):
    own_ref, map_ref, mask_ref, q_ref = refs[:4]
    mixed = half is not None
    tiles = 1 if mixed else parts
    state_in = None if first else refs[4]
    st_s, qt_s, kv_s, vt_s, list_s, land_s, seen_s, full_s, count_s, top_s, sems = refs[-11:]
    outs = 2 if mixed else 1
    items, outs = refs[4 if first else 5 : -11 - outs], refs[-11 - outs : -11]
    st, qt = st_s if last else outs[0], qt_s if mixed else q_ref
    heads = qt.shape[1]
    kv_heads = heads // GROUP
    kvw = kv_heads * HEAD_DIM
    own = own_ref[0]
    sums = slice(0, HEAD_DIM + STAT)
    weights = slice(HEAD_DIM, HEAD_DIM + STAT)
    point = slice(HEAD_DIM + STAT, HEAD_DIM + 2 * STAT)

    def copies(i, kp, ik):
        pieces = place.refs(items, i, kp)
        size = tok // len(pieces)
        return [
            pltpu.make_async_copy(piece, kv_s.at[ik, pl.ds(j * size, size)], sems.at[ik, j])
            for j, piece in enumerate(pieces)
        ]

    seg_q = [map_ref[place.query(own, j)] for j in range(parts)]
    counts = [jnp.int32(0)] * tiles
    landed = jnp.int32(0)
    for i in range(n_items):
        for kp in range(parts):
            ik = i * parts + kp
            seg_k = [map_ref[src] for src in place.sources(own, i, kp)]
            any_seen = jnp.int32(0)
            for qp in range(parts):
                seen = jnp.int32(0)
                for n in range(2):
                    seen_half = (mask_ref[seg_q[qp], seg_k[n]] > 0).astype(jnp.int32)
                    seen_s[qp, 2 * ik + n] = seen_half
                    seen = jnp.maximum(seen, seen_half)
                any_seen = jnp.maximum(any_seen, seen)
                if not mixed:
                    list_s[qp, counts[qp]] = ik
                    counts[qp] = counts[qp] + seen
            if mixed:
                list_s[0, counts[0]] = ik
                counts[0] = counts[0] + any_seen
            land_s[landed] = ik
            landed = landed + any_seen

            @pl.when(any_seen > 0)
            def _():
                if place.near:
                    pieces = place.refs(items, i, kp)
                    size = tok // len(pieces)
                    for j, piece in enumerate(pieces):
                        kv_s[ik, j * size : (j + 1) * size] = piece[...]
                else:
                    for one in copies(i, kp, ik):
                        one.start()

    ones = jnp.ones((ONES, tok), jnp.bfloat16)

    def land(t, carry):
        ik = land_s[t]
        if not place.near:
            for one in copies(0, 0, ik):
                one.wait()
        for kh in range(kv_heads):
            v = kv_s[ik, :, kvw + kh * HEAD_DIM : kvw + (kh + 1) * HEAD_DIM]
            vt_s[ik, kh, :HEAD_DIM] = v.T
            vt_s[ik, kh, HEAD_DIM:] = ones
        return carry

    lax.fori_loop(0, landed, land, 0)

    def blocks(qp, t):
        single = 2 * t + 1 >= full_s[qp]
        i0 = list_s[qp, 2 * t]
        i1 = list_s[qp, jnp.where(single, 2 * t, 2 * t + 1)]
        if mixed:
            left = lax.broadcasted_iota(jnp.int32, (STAT, rows), 1) < rows // 2
        bias = []
        for i in (i0, i1):
            for n in range(2):
                hidden = [
                    jnp.where(seen_s[part, 2 * i + n] > 0, jnp.float32(0.0), jnp.float32(NEG))
                    for part in ((0, 1) if mixed else (qp,))
                ]
                bias.append(jnp.where(left, hidden[0], hidden[1]) if mixed else hidden[0])
        again = jnp.where(single, jnp.float32(NEG), jnp.float32(0.0))
        bias[2:] = [one + again for one in bias[2:]]
        return i0, i1, bias

    def operands(kh, i0, i1):
        lanes = slice(kh * HEAD_DIM, (kh + 1) * HEAD_DIM)
        return (
            [jnp.concatenate([kv_s[i, :, lanes]] * 2, axis=1) for i in (i0, i1)],
            [vt_s[i, kh] for i in (i0, i1)],
        )

    def slow(units, qp, t):
        i0, i1, bias = blocks(qp, t)
        for h in range(heads):
            kh = h // GROUP
            unit = kh % UNITS
            s0_acc, s1_acc, pv_acc = units[unit]
            keys, values = operands(kh, i0, i1)
            pltpu.matmul_push_rhs(qt[qp, h], 0, unit)
            pltpu.matmul_acc_lhs(s0_acc, keys[0], 0)
            pltpu.matmul_acc_lhs(s1_acc, keys[1])
            s = [pltpu.matmul_pop(acc).reshape(-1, STAT, rows) for acc in (s0_acc, s1_acc)]
            before = st[qp, h, point]
            quarters = [x[n * (tok // 16) : (n + 1) * (tok // 16)] for x in s for n in range(2)]
            top = functools.reduce(jnp.maximum, [jnp.max(x, axis=0) + one for x, one in zip(quarters, bias)])
            now = jnp.maximum(before, jnp.max(top, axis=0, keepdims=True))
            for j, value in enumerate(values):
                p = [jnp.exp2(quarters[2 * j + n] - (now - bias[2 * j + n])[None]) for n in range(2)]
                p = jnp.concatenate(p, axis=0).reshape(tok, rows).astype(jnp.bfloat16)
                pltpu.matmul_push_rhs(p, 1, unit)
                pltpu.matmul_acc_lhs(pv_acc, value, 1)
            kept = st[qp, h, sums].reshape(-1, STAT, rows) * jnp.exp2(before - now)[None]
            st[qp, h, sums] = kept.reshape(-1, rows) + pltpu.matmul_pop(pv_acc)[sums]
            st[qp, h, point] = now

    def fast(units, qp, t):
        i0, i1, bias = blocks(qp, t)
        keys, values = zip(*[operands(kh, i0, i1) for kh in range(kv_heads)])

        def begin(kh, g):
            unit = units[kh % len(units)]
            pltpu.matmul_push_rhs(qt[qp, kh * GROUP + g], 0, kh % len(units))
            pltpu.matmul_acc_lhs(unit[0], keys[kh][0], 0)
            pltpu.matmul_acc_lhs(unit[1], keys[kh][1])

        def weights_of(kh, g, j):
            s = pltpu.matmul_pop(units[kh % len(units)][j]).reshape(-1, STAT, rows)
            ref = st[qp, kh * GROUP + g, point]
            p = [
                jnp.exp2(s[n * (tok // 16) : (n + 1) * (tok // 16)] - (ref - bias[2 * j + n])[None])
                for n in range(2)
            ]
            return jnp.concatenate(p, axis=0).reshape(tok, rows).astype(jnp.bfloat16)

        for first_kh in range(0, kv_heads, len(units)):
            together = range(first_kh, min(first_kh + len(units), kv_heads))
            for kh in together:
                begin(kh, 0)
            for g in range(GROUP):
                p = {(kh, j): weights_of(kh, g, j) for j in range(2) for kh in together}
                if g + 1 < GROUP:
                    for kh in together:
                        begin(kh, g + 1)
                for j in range(2):
                    for kh in together:
                        pltpu.matmul_push_rhs(p[kh, j], 1, kh % len(units))
                        pltpu.matmul_acc_lhs(units[kh % len(units)][2], values[kh][j], 1)
                for kh in together:
                    h = kh * GROUP + g
                    st[qp, h, sums] = st[qp, h, sums] + pltpu.matmul_pop(units[kh % len(units)][2])[sums]

    columns_of = slice(half * rows // 2, (half + 1) * rows // 2) if mixed else slice(0, rows)
    if mixed:
        for h in range(heads):
            qt_s[0, h] = jnp.concatenate([q_ref[part, h, :, columns_of] for part in range(2)], axis=1)
    for qp in range(tiles):
        full_s[qp] = counts[qp]
        count_s[qp] = (counts[qp] + 1) // 2

    def attempt(again, carry):
        @pl.when(jnp.logical_or(again == 0, top_s[0] > 0))
        def _():
            for qp in range(tiles):
                for h in range(heads):
                    if mixed:
                        st[0, h] = jnp.concatenate([state_in[part, h, :, columns_of] for part in range(2)], axis=1)
                    elif first:
                        st[qp, h, sums] = jnp.zeros((HEAD_DIM + STAT, rows), jnp.float32)
                        st[qp, h, point] = jnp.full((STAT, rows), NEG, jnp.float32)
                    else:
                        st[qp, h] = state_in[qp, h]

            def one_part(qp, carry):
                pairs = count_s[qp]
                switch = jnp.where(again > 0, pairs, 1 if first else 0)

                def both(*accs):
                    units = [accs[3 * unit : 3 * unit + 3] for unit in range(UNITS)]

                    def one_slow(t, carry):
                        slow(units, qp, t)
                        return carry

                    def one_fast(t, carry):
                        fast(units, qp, t)
                        return carry

                    lax.fori_loop(0, switch, one_slow, 0)
                    lax.fori_loop(switch, pairs, one_fast, 0)

                accumulators = []
                for unit in range(UNITS):
                    accumulators += [pltpu.ACC(unit)((tok, rows), jnp.float32)] * 2
                    accumulators.append(pltpu.ACC(unit)((HEAD_DIM + ONES, rows), jnp.float32))
                pl.run_scoped(both, *accumulators)
                return carry

            lax.fori_loop(0, tiles, one_part, 0)
            top = jnp.zeros((STAT, rows), jnp.float32)
            for qp in range(tiles):
                for h in range(heads):
                    top = jnp.maximum(top, jnp.where(st[qp, h, weights] < LARGE, 0.0, 1.0))
            top_s[0] = (jnp.max(top) > 0.0).astype(jnp.int32)

        return carry

    top_s[0] = 0
    lax.fori_loop(0, 2, attempt, 0)
    if last:
        for qp in range(tiles):
            for h in range(heads):
                lanes = slice(h * HEAD_DIM, (h + 1) * HEAD_DIM)
                inv = 1.0 / st[qp, h, weights]
                att = st[qp, h, :HEAD_DIM].reshape(-1, STAT, rows) * inv[None]
                att = att.reshape(HEAD_DIM, rows).T.astype(jnp.bfloat16)
                if mixed:
                    outs[0][:, lanes] = att[: rows // 2]
                    outs[1][:, lanes] = att[rows // 2 :]
                else:
                    outs[0][qp * rows : (qp + 1) * rows, lanes] = att


class GridPlace:
    near = True

    def __init__(self, metas, n_a, n_b, tok):
        self.metas, self.n_a, self.n_b, self.tok = metas, n_a, n_b, tok

    def query(self, own, part):
        return (own // CORES) * CORES + (own % CORES + part) % CORES

    def sources(self, own, i, part):
        a, b, c = own // (CORES * self.n_b), (own // CORES) % self.n_b, own % CORES
        return [
            ((a ^ flip) * self.n_b + (b + db) % self.n_b) * CORES + (c + part) % CORES
            for _, _, flip, db in self.metas[i]
        ]

    def refs(self, items, i, part):
        rows = self.tok // 2
        return [items[n].at[pl.ds(base + part * rows, rows)] for n, base, _, _ in self.metas[i]]


class FlatPlace:
    near = False

    def __init__(self, tok):
        self.tok = tok

    def query(self, own, part):
        return own

    def sources(self, own, i, part):
        return [i, i]

    def refs(self, items, i, part):
        return [items[0].at[pl.ds(i * self.tok, self.tok)]]


def other_columns(own, pieces):
    rows, width = pieces[0].shape
    half = width // CORES
    vmem = pl.BlockSpec(memory_space=pltpu.VMEM)

    def kernel(own_ref, *refs):
        lanes = pl.ds(pl.multiple_of((own_ref[0] + 1) % CORES * half, half), half)
        for i, ref in enumerate(refs[:-1]):
            refs[-1][i * rows : (i + 1) * rows] = ref[:, lanes]

    return pl.pallas_call(
        kernel,
        out_shape=jax.ShapeDtypeStruct((len(pieces) * rows, half), pieces[0].dtype),
        in_specs=[pl.BlockSpec(memory_space=pltpu.SMEM)] + [vmem] * len(pieces),
        out_specs=vmem,
        compiler_params=pltpu.CompilerParams(vmem_limit_bytes=VMEM_LIMIT),
        cost_estimate=LITTLE,
        name="other_columns",
    )(own, *pieces)


def moved(kernel, args, shapes, name):
    vmem = pl.BlockSpec(memory_space=pltpu.VMEM)
    return pl.pallas_call(
        kernel,
        out_shape=[jax.ShapeDtypeStruct(shape, jnp.bfloat16) for shape in shapes],
        in_specs=[pl.BlockSpec(memory_space=pltpu.SMEM)] + [vmem] * (len(args) - 1),
        out_specs=[vmem] * len(shapes),
        compiler_params=pltpu.CompilerParams(vmem_limit_bytes=VMEM_LIMIT),
        cost_estimate=SOME if name == "joined" else LITTLE,
        name=name,
    )(*args)


def joined(own, above, below):
    rows, width = above.shape

    def kernel(own_ref, above_ref, below_ref, out_ref):
        out_ref[:rows] = above_ref[...]
        out_ref[rows:] = below_ref[...]

    return moved(kernel, (own, above, below), [(2 * rows, width)], "joined")[0]


def lower_half(own, x):
    rows, width = x.shape

    def kernel(own_ref, x_ref, out_ref):
        out_ref[...] = x_ref[rows // 2 :]

    return moved(kernel, (own, x), [(rows // 2, width)], "lower_half")[0]


def picked(own, at_ends, at_middle, n_a, n_b):
    rows, width = at_ends.shape

    def kernel(own_ref, ends_ref, middle_ref, whole_ref, half_ref):
        a = own_ref[0] // (CORES * n_b)
        at_end = jnp.logical_or(a == 0, a == n_a - 1)

        def take(ref):
            whole_ref[...] = ref[...]
            half_ref[...] = ref[: rows // 2]

        pl.when(at_end)(lambda: take(ends_ref))
        pl.when(jnp.logical_not(at_end))(lambda: take(middle_ref))

    return moved(kernel, (own, at_ends, at_middle), [(rows, width), (rows // 2, width)], "picked")


def turn(own, parts):
    pieces = [x for part in parts for x in part]
    heads = min(x.shape[1] for x in pieces) // HEAD_DIM
    rows = sum(x.shape[0] for x in parts[0])
    vmem = pl.BlockSpec(memory_space=pltpu.VMEM)

    def kernel(own_ref, *refs):
        begin = own_ref[0] % CORES * heads * HEAD_DIM
        at = 0
        for qp, part in enumerate(parts):
            some = refs[at : at + len(part)]
            at += len(part)
            for h in range(heads):
                turned = []
                for ref in some:
                    first = h * HEAD_DIM
                    if ref.shape[1] > heads * HEAD_DIM:
                        first = pl.multiple_of(begin + first, HEAD_DIM)
                    turned.append(ref[:, pl.ds(first, HEAD_DIM)].astype(jnp.float32).T)
                scaled = jnp.concatenate(turned, axis=1) * SCALE
                high = scaled.astype(jnp.bfloat16)
                refs[-1][qp, h, :HEAD_DIM] = high
                refs[-1][qp, h, HEAD_DIM:] = (scaled - high.astype(jnp.float32)).astype(jnp.bfloat16)

    return pl.pallas_call(
        kernel,
        out_shape=pltpu.VMEM((len(parts), heads, 2 * HEAD_DIM, rows), jnp.bfloat16),
        in_specs=[pl.BlockSpec(memory_space=pltpu.SMEM)] + [vmem] * len(pieces),
        out_specs=vmem,
        compiler_params=pltpu.CompilerParams(vmem_limit_bytes=VMEM_LIMIT),
        cost_estimate=LITTLE,
        name="turn",
    )(own, *pieces)


def attend(scalars, q, state, arrays, place, n_items, parts, tok, last, half=None):
    first = state is None
    heads, rows = q.shape[1], q.shape[3]
    width = arrays[0].shape[1]
    smem = pl.BlockSpec(memory_space=pltpu.SMEM)
    vmem = pl.BlockSpec(memory_space=pltpu.VMEM)
    args = list(scalars) + [pinned(q)] + ([] if first else [pinned(state)])
    args += [pinned(x) if place.near else x for x in arrays]
    specs = [smem] * 3 + [vmem] + ([] if first else [vmem])
    specs += [vmem if place.near else pl.BlockSpec(memory_space=pl.ANY)] * len(arrays)
    shape = (parts, heads, HEAD_DIM + 2 * STAT, rows)
    tile_shape = shape if half is None else (1,) + shape[1:]
    blocks = n_items * parts
    scratch = [
        pltpu.VMEM(tile_shape if last else (STAT, HEAD_DIM), jnp.float32),
        pltpu.VMEM((1,) + q.shape[1:] if half is not None else (ONES, HEAD_DIM), jnp.bfloat16),
        pltpu.VMEM((blocks, tok, width), jnp.bfloat16),
        pltpu.VMEM((blocks, heads // GROUP, HEAD_DIM + ONES, tok), jnp.bfloat16),
        pltpu.SMEM((parts, blocks + 1), jnp.int32),
        pltpu.SMEM((blocks + 1,), jnp.int32),
        pltpu.SMEM((parts, 2 * blocks), jnp.int32),
        pltpu.SMEM((parts,), jnp.int32),
        pltpu.SMEM((parts,), jnp.int32),
        pltpu.SMEM((1,), jnp.int32),
        pltpu.SemaphoreType.DMA((blocks, 2)),
    ]
    if last:
        out_shape = [jax.ShapeDtypeStruct((parts * rows, heads * HEAD_DIM), jnp.bfloat16)]
        if half is not None:
            out_shape = [jax.ShapeDtypeStruct((rows // 2, heads * HEAD_DIM), jnp.bfloat16)] * 2
    else:
        out_shape = [pltpu.VMEM(shape, jnp.float32)]

    def kernel(*refs):
        attend_kernel(place, n_items, parts, half, rows, tok, first, last, refs)

    return pl.pallas_call(
        kernel,
        out_shape=out_shape,
        in_specs=specs,
        out_specs=[vmem] * len(out_shape),
        scratch_shapes=scratch,
        compiler_params=pltpu.CompilerParams(vmem_limit_bytes=VMEM_LIMIT),
        cost_estimate=LITTLE,
        name="attend",
    )(*args)


def pinned(x):
    return pltpu.with_memory_space_constraint(x, pltpu.VMEM)


def fetch(weight):
    chunks = 12
    rows = weight.shape[0] // chunks

    def kernel(weight_ref, out_ref, sems):
        copies = [
            pltpu.make_async_copy(
                weight_ref.at[pl.ds(i * rows, rows)], out_ref.at[pl.ds(i * rows, rows)], sems.at[i]
            )
            for i in range(chunks)
        ]
        for one in copies:
            one.start()
        for one in copies:
            one.wait()

    return pl.pallas_call(
        kernel,
        out_shape=pltpu.VMEM(weight.shape, weight.dtype),
        in_specs=[pl.BlockSpec(memory_space=pltpu.HBM)],
        out_specs=pl.BlockSpec(memory_space=pltpu.VMEM),
        scratch_shapes=[pltpu.SemaphoreType.DMA((chunks,))],
        compiler_params=pltpu.CompilerParams(vmem_limit_bytes=VMEM_LIMIT),
        cost_estimate=LITTLE,
        name="fetch",
    )(pltpu.with_memory_space_constraint(weight, pltpu.HBM))


def project(own, parts, weight, rows, partial=None, ending=None):
    width = weight.shape[1]
    depth = parts[0][0].shape[1]
    tile = math.gcd(width, 512)
    smem = pl.BlockSpec(memory_space=pltpu.SMEM)
    vmem = pl.BlockSpec(memory_space=pltpu.VMEM)
    n = len(parts)
    args = [own] + [x for x, _, _ in parts] + [pinned(weight)]
    specs = [smem] + [vmem] * (n + 1)
    scratch = []
    out_shape = [jax.ShapeDtypeStruct((rows, width), jnp.bfloat16)]
    if partial is not None:
        args.append(pinned(partial))
        specs.append(vmem)
    elif ending is not None:
        args += list(ending)
        args[-2] = pltpu.with_memory_space_constraint(args[-2], pltpu.HBM)
        specs += [smem] * 2 + [pl.BlockSpec(memory_space=pltpu.HBM), vmem]
        out_shape = [pltpu.VMEM((rows, width), jnp.float32), pltpu.VMEM((STAT, width), jnp.float32)]
        scratch = [pltpu.VMEM((STAT, width), jnp.float32), pltpu.SemaphoreType.DMA]
    else:
        out_shape = [pltpu.VMEM((rows, width), jnp.float32)]

    def kernel(*refs):
        own_ref, part_refs, weight_ref, refs = refs[0], refs[1 : n + 1], refs[n + 1], refs[n + 2 :]
        if ending is not None:
            steps_ref, map_ref, gate_ref, residual_ref, out_ref, row_ref, near, sem = refs
            step = steps_ref[map_ref[own_ref[0]]]
            copy = pltpu.make_async_copy(
                gate_ref.at[pl.ds(pl.multiple_of((step // STAT) * STAT, STAT), STAT)], near, sem
            )
            copy.start()
            copy.wait()
            chosen = lax.broadcasted_iota(jnp.int32, (STAT, width), 0) == step % STAT
            row = jnp.sum(jnp.where(chosen, near[...], 0.0), axis=0, keepdims=True)
            row_ref[...] = jnp.broadcast_to(row, (STAT, width))
        else:
            out_ref = refs[-1]

        def one(t, carry):
            lanes = pl.ds(pl.multiple_of(t * tile, tile), tile)
            total = None
            for j in range(n):
                first_row = parts[j][2]
                group = (own_ref[0] + parts[j][1]) % CORES
                weight_rows = pl.ds(pl.multiple_of(group * depth, depth), depth)
                term = jnp.dot(
                    part_refs[j][first_row : first_row + rows],
                    weight_ref[weight_rows, lanes],
                    preferred_element_type=jnp.float32,
                )
                total = term if total is None else total + term
            if partial is not None:
                total = total + refs[0][:, lanes]
            if ending is not None:
                gate = jnp.concatenate([row_ref[:, lanes]] * (rows // STAT), axis=0)
                total = residual_ref[:, lanes].astype(jnp.float32) + gate * total
            out_ref[:, lanes] = total.astype(out_ref.dtype)
            return carry

        lax.fori_loop(0, width // tile, one, 0)

    return pl.pallas_call(
        kernel,
        out_shape=out_shape,
        in_specs=specs,
        out_specs=[vmem] * len(out_shape),
        scratch_shapes=scratch,
        compiler_params=pltpu.CompilerParams(vmem_limit_bytes=VMEM_LIMIT),
        cost_estimate=pl.CostEstimate(
            flops=2 * rows * depth * n * width, bytes_accessed=2 * depth * n * width, transcendentals=0
        ),
        name="project",
    )(*args)


def columns(x, part, width):
    return lax.dynamic_slice_in_dim(x, part * width, width, 1)


def paired(query_rows, key_rows, value_rows, out_weight, scalars, ending, n_a, n_b):
    n_seq = n_a * n_b * CORES
    groups = 2 * CORES
    own = scalars[0]
    kvw = key_rows.shape[1] // groups
    rows = query_rows.shape[0]
    tok = 2 * rows
    x = lax.axis_index("head")
    c = lax.axis_index("seq") % CORES

    def index(a, b, k):
        return (a * n_b + b) * CORES + k

    def swapped(piece, dx, dc):
        pairs = [
            ((s ^ dc) * 2 + (h ^ dx), s * 2 + h) for s in range(n_seq) for h in range(2)
        ]
        return lax.ppermute(piece, ("seq", "head"), pairs)

    def along_a(piece, moves):
        pairs = [
            (index(a, b, k), index(to, b, k)) for a, to in moves for b in range(n_b) for k in range(CORES)
        ]
        return lax.ppermute(piece, "seq", pairs)

    def beside_of(piece, only):
        pairs = [
            (index(a, 1 - b, k), index(a, b, k)) for a in only for b in range(n_b) for k in range(CORES)
        ]
        return lax.ppermute(piece, "seq", pairs)

    def stage(state, q, arrays, metas, last=False, half=None):
        return attend(
            scalars, q, state, arrays, GridPlace(metas, n_a, n_b, tok), len(metas), CORES, tok, last, half
        )

    def halves_of(first, base, flip, db):
        if isinstance(first, int):
            return [(first, base, flip, db), (first, base + tok, flip, db)]
        return [(n, base, flip, db) for n in first]

    def kv_for(dx, dc):
        j = (x ^ dx) * CORES + (c ^ dc)
        return jnp.concatenate([columns(key_rows, j, kvw), columns(value_rows, j, kvw)], axis=1)

    chips = list(range(n_a))
    order = [(0, 0), (1, 0), (0, 1), (1, 1)]
    pieces = {d: kv_for(*d) if sum(d) == 0 else swapped(kv_for(*d), *d) for d in order}
    early = jnp.concatenate([pieces[0, 0], pieces[0, 1]], axis=0)
    later = jnp.concatenate([pieces[1, 0], pieces[1, 1]], axis=0)
    block = jnp.concatenate([early, later], axis=0)
    qw = query_rows.shape[1] // 2
    q_own, q_other = columns(query_rows, x, qw), columns(query_rows, 1 - x, qw)
    block, later, out_weight, q_own, q_other = lax.optimization_barrier(
        (block, later, out_weight, q_own, q_other)
    )
    by_one, by_two = [(a, a ^ 1) for a in chips], [(a, a ^ 2) for a in chips]
    beside = beside_of(block, chips)
    next_early, far_early = along_a(early, by_one), along_a(early, by_two)
    q_came = swapped(q_other, 1, 0)
    weight = fetch(out_weight)
    both_early = joined(own, next_early, far_early)
    later, both_early = lax.optimization_barrier((later, both_early))
    beside, both_early, q_came, weight = lax.optimization_barrier((beside, both_early, q_came, weight))
    beside_early = beside_of(both_early, chips)
    next_later, far_later = along_a(later, by_one), along_a(later, by_two)
    q_core = swapped(other_columns(own, [q_own, q_came]), 0, 1)
    both_later, far = joined(own, next_later, far_later), joined(own, far_early, far_later)
    both_later, far, q_core = lax.optimization_barrier((both_later, far, q_core))
    q = turn(own, [[q_own, q_came], [q_core]])
    (state,) = stage(None, q, [block, beside], [halves_of(0, 0, 0, 0), halves_of(1, 0, 0, 1)])
    again, state = lax.optimization_barrier((block, state))
    to_middle = along_a(again, [(1, 2), (2, 1)])
    both_later, far, beside_early, state = lax.optimization_barrier((both_later, far, beside_early, state))
    beside_later = beside_of(both_later, chips)
    to_ends = along_a(far, [(1, 0), (2, 3)])
    (state,) = stage(
        state, q, [next_early, next_later, far_early, far_later],
        [halves_of((0, 1), 0, 1, 0), halves_of((2, 3), 0, 2, 0)],
    )
    to_middle, state = lax.optimization_barrier((to_middle, state))
    (state,) = stage(state, q, [beside_early], [[(0, 0, 1, 1), (0, tok, 2, 1)]])
    to_ends, to_middle, beside_later, state = lax.optimization_barrier((to_ends, to_middle, beside_later, state))
    last, last_upper = picked(own, to_ends, to_middle, n_a, n_b)
    beside_last = [beside_of(last_upper, chips), along_a(lower_half(own, beside_later), by_one)]
    (state,) = stage(
        state, q, [beside_later, last], [[(0, 0, 1, 1), (0, tok, 2, 1)], halves_of(1, 0, 3, 0)]
    )
    last_block = [halves_of((0, 1), 0, 3, 1)]
    kept, sent = stage(state, q, beside_last, last_block, True, 1)
    came = swapped(sent, 0, 1)
    (begun,) = project(own, [(kept, 0, 0)], weight, rows)
    (theirs,) = project(own, [(came, 1, 0)], weight, rows, partial=begun)
    came_back = lax.ppermute(theirs, "head", [(0, 1), (1, 0)])
    state, theirs = lax.optimization_barrier((state, theirs))
    kept, sent = stage(state, q, beside_last, last_block, True, 0)
    came = swapped(sent, 0, 1)
    base, gate = project(own, [(kept, 0, 0), (came, 1, 0)], weight, rows, ending=ending)
    return (base + gate[:1] * came_back.astype(jnp.float32)).astype(jnp.bfloat16)


def gathered_attention(query_rows, key_rows, value_rows, scalars):
    spread = functools.partial(lax.all_to_all, axis_name="head", split_axis=1, concat_axis=0, tiled=True)
    local = jnp.concatenate([spread(key_rows), spread(value_rows)], axis=1)
    every = lax.all_gather(local, "seq", axis=0, tiled=True)
    tok = local.shape[0]
    return attend(
        scalars, turn(scalars[0], [[spread(query_rows)]]), None, [every], FlatPlace(tok), every.shape[0] // tok, 1, tok, True
    )[0]


def per_device(
    query_rows,
    key_rows,
    value_rows,
    residual,
    out_weight,
    gate_table,
    noise_steps,
    segment_mask,
    segment_map,
):
    n_seq = lax.axis_size("seq")
    n_head = lax.axis_size("head")
    own_seq = lax.axis_index("seq").astype(jnp.int32)
    own = own_seq.reshape(1)
    scalars = (own, segment_map, segment_mask)
    n_a, n_b = grid_of(n_seq)
    if n_head == 2 and n_a == 4 and n_b == 2:
        ending = (noise_steps, segment_map, gate_table, residual)
        return paired(query_rows, key_rows, value_rows, out_weight, scalars, ending, n_a, n_b)
    attended = gathered_attention(query_rows, key_rows, value_rows, scalars)
    projected = lax.psum_scatter(
        jnp.dot(attended, out_weight, preferred_element_type=jnp.float32).astype(jnp.bfloat16),
        "head",
        scatter_dimension=0,
        tiled=True,
    ).astype(jnp.float32)
    gate_row = lax.dynamic_slice_in_dim(gate_table, noise_steps[segment_map[own_seq]], 1, 0)
    return (residual.astype(jnp.float32) + gate_row * projected).astype(jnp.bfloat16)


def solution(mesh):
    placed = (
        P(("seq", "head"), None),
        P(("seq", "head"), None),
        P(("seq", "head"), None),
        P(("seq", "head"), None),
        P("head", None),
        P(),
        P(),
        P(),
        P(),
    )
    return jax.shard_map(
        per_device, mesh=mesh, in_specs=placed, out_specs=P(("seq", "head"), None), check_vma=False
    )
```

```python
import functools
import math

import jax
import jax.numpy as jnp
from jax import lax
from jax.experimental import pallas as pl
from jax.experimental.pallas import tpu as pltpu
from jax.sharding import PartitionSpec as P

Q_HEADS = 24
KV_HEADS = 8
HEAD_DIM = 128
GROUP = Q_HEADS // KV_HEADS
CORES = 2
UNITS = 2
NEG = -1e30
SCALE = 1.4426950408889634 * HEAD_DIM ** -0.5
STAT = 8
ONES = 16
LARGE = 1e27
VMEM_LIMIT = 24 * 1024 * 1024
SOME = pl.CostEstimate(flops=3000000000, bytes_accessed=1, transcendentals=0)
LITTLE = pl.CostEstimate(flops=1, bytes_accessed=1, transcendentals=0)


def grid_of(n_seq):
    chips = n_seq // CORES
    inner = 2 ** (int(math.log2(chips)) // 2)
    return chips // inner, inner


def attend_kernel(place, n_items, parts, half, rows, tok, first, last, refs):
    own_ref, map_ref, mask_ref, q_ref = refs[:4]
    mixed = half is not None
    tiles = 1 if mixed else parts
    state_in = None if first else refs[4]
    st_s, qt_s, kv_s, vt_s, list_s, land_s, seen_s, full_s, count_s, top_s, sems = refs[-11:]
    outs = 2 if mixed else 1
    items, outs = refs[4 if first else 5 : -11 - outs], refs[-11 - outs : -11]
    st, qt = st_s if last else outs[0], qt_s if mixed else q_ref
    heads = qt.shape[1]
    kv_heads = heads // GROUP
    kvw = kv_heads * HEAD_DIM
    own = own_ref[0]
    sums = slice(0, HEAD_DIM + STAT)
    weights = slice(HEAD_DIM, HEAD_DIM + STAT)
    point = slice(HEAD_DIM + STAT, HEAD_DIM + 2 * STAT)

    def copies(i, kp, ik):
        pieces = place.refs(items, i, kp)
        size = tok // len(pieces)
        return [
            pltpu.make_async_copy(piece, kv_s.at[ik, pl.ds(j * size, size)], sems.at[ik, j])
            for j, piece in enumerate(pieces)
        ]

    seg_q = [map_ref[place.query(own, j)] for j in range(parts)]
    counts = [jnp.int32(0)] * tiles
    landed = jnp.int32(0)
    for i in range(n_items):
        for kp in range(parts):
            ik = i * parts + kp
            seg_k = [map_ref[src] for src in place.sources(own, i, kp)]
            any_seen = jnp.int32(0)
            for qp in range(parts):
                seen = jnp.int32(0)
                for n in range(2):
                    seen_half = (mask_ref[seg_q[qp], seg_k[n]] > 0).astype(jnp.int32)
                    seen_s[qp, 2 * ik + n] = seen_half
                    seen = jnp.maximum(seen, seen_half)
                any_seen = jnp.maximum(any_seen, seen)
                if not mixed:
                    list_s[qp, counts[qp]] = ik
                    counts[qp] = counts[qp] + seen
            if mixed:
                list_s[0, counts[0]] = ik
                counts[0] = counts[0] + any_seen
            land_s[landed] = ik
            landed = landed + any_seen

            @pl.when(any_seen > 0)
            def _():
                if place.near:
                    pieces = place.refs(items, i, kp)
                    size = tok // len(pieces)
                    for j, piece in enumerate(pieces):
                        kv_s[ik, j * size : (j + 1) * size] = piece[...]
                else:
                    for one in copies(i, kp, ik):
                        one.start()

    ones = jnp.ones((ONES, tok), jnp.bfloat16)

    def land(t, carry):
        ik = land_s[t]
        if not place.near:
            for one in copies(0, 0, ik):
                one.wait()
        for kh in range(kv_heads):
            v = kv_s[ik, :, kvw + kh * HEAD_DIM : kvw + (kh + 1) * HEAD_DIM]
            vt_s[ik, kh, :HEAD_DIM] = v.T
            vt_s[ik, kh, HEAD_DIM:] = ones
        return carry

    lax.fori_loop(0, landed, land, 0)

    def blocks(qp, t):
        single = 2 * t + 1 >= full_s[qp]
        i0 = list_s[qp, 2 * t]
        i1 = list_s[qp, jnp.where(single, 2 * t, 2 * t + 1)]
        if mixed:
            left = lax.broadcasted_iota(jnp.int32, (STAT, rows), 1) < rows // 2
        bias = []
        for i in (i0, i1):
            for n in range(2):
                hidden = [
                    jnp.where(seen_s[part, 2 * i + n] > 0, jnp.float32(0.0), jnp.float32(NEG))
                    for part in ((0, 1) if mixed else (qp,))
                ]
                bias.append(jnp.where(left, hidden[0], hidden[1]) if mixed else hidden[0])
        again = jnp.where(single, jnp.float32(NEG), jnp.float32(0.0))
        bias[2:] = [one + again for one in bias[2:]]
        return i0, i1, bias

    def operands(kh, i0, i1):
        lanes = slice(kh * HEAD_DIM, (kh + 1) * HEAD_DIM)
        return (
            [jnp.concatenate([kv_s[i, :, lanes]] * 2, axis=1) for i in (i0, i1)],
            [vt_s[i, kh] for i in (i0, i1)],
        )

    def slow(units, qp, t):
        i0, i1, bias = blocks(qp, t)
        for h in range(heads):
            kh = h // GROUP
            unit = kh % UNITS
            s0_acc, s1_acc, pv_acc = units[unit]
            keys, values = operands(kh, i0, i1)
            pltpu.matmul_push_rhs(qt[qp, h], 0, unit)
            pltpu.matmul_acc_lhs(s0_acc, keys[0], 0)
            pltpu.matmul_acc_lhs(s1_acc, keys[1])
            s = [pltpu.matmul_pop(acc).reshape(-1, STAT, rows) for acc in (s0_acc, s1_acc)]
            before = st[qp, h, point]
            quarters = [x[n * (tok // 16) : (n + 1) * (tok // 16)] for x in s for n in range(2)]
            top = functools.reduce(jnp.maximum, [jnp.max(x, axis=0) + one for x, one in zip(quarters, bias)])
            now = jnp.maximum(before, jnp.max(top, axis=0, keepdims=True))
            for j, value in enumerate(values):
                p = [jnp.exp2(quarters[2 * j + n] - (now - bias[2 * j + n])[None]) for n in range(2)]
                p = jnp.concatenate(p, axis=0).reshape(tok, rows).astype(jnp.bfloat16)
                pltpu.matmul_push_rhs(p, 1, unit)
                pltpu.matmul_acc_lhs(pv_acc, value, 1)
            kept = st[qp, h, sums].reshape(-1, STAT, rows) * jnp.exp2(before - now)[None]
            st[qp, h, sums] = kept.reshape(-1, rows) + pltpu.matmul_pop(pv_acc)[sums]
            st[qp, h, point] = now

    def fast(units, qp, t):
        i0, i1, bias = blocks(qp, t)
        keys, values = zip(*[operands(kh, i0, i1) for kh in range(kv_heads)])

        def begin(kh, g):
            unit = units[kh % len(units)]
            pltpu.matmul_push_rhs(qt[qp, kh * GROUP + g], 0, kh % len(units))
            pltpu.matmul_acc_lhs(unit[0], keys[kh][0], 0)
            pltpu.matmul_acc_lhs(unit[1], keys[kh][1])

        def weights_of(kh, g, j):
            s = pltpu.matmul_pop(units[kh % len(units)][j]).reshape(-1, STAT, rows)
            ref = st[qp, kh * GROUP + g, point]
            p = [
                jnp.exp2(s[n * (tok // 16) : (n + 1) * (tok // 16)] - (ref - bias[2 * j + n])[None])
                for n in range(2)
            ]
            return jnp.concatenate(p, axis=0).reshape(tok, rows).astype(jnp.bfloat16)

        for first_kh in range(0, kv_heads, len(units)):
            together = range(first_kh, min(first_kh + len(units), kv_heads))
            for kh in together:
                begin(kh, 0)
            for g in range(GROUP):
                p = {(kh, j): weights_of(kh, g, j) for j in range(2) for kh in together}
                if g + 1 < GROUP:
                    for kh in together:
                        begin(kh, g + 1)
                for j in range(2):
                    for kh in together:
                        pltpu.matmul_push_rhs(p[kh, j], 1, kh % len(units))
                        pltpu.matmul_acc_lhs(units[kh % len(units)][2], values[kh][j], 1)
                for kh in together:
                    h = kh * GROUP + g
                    st[qp, h, sums] = st[qp, h, sums] + pltpu.matmul_pop(units[kh % len(units)][2])[sums]

    columns_of = slice(half * rows // 2, (half + 1) * rows // 2) if mixed else slice(0, rows)
    if mixed:
        for h in range(heads):
            qt_s[0, h] = jnp.concatenate([q_ref[part, h, :, columns_of] for part in range(2)], axis=1)
    for qp in range(tiles):
        full_s[qp] = counts[qp]
        count_s[qp] = (counts[qp] + 1) // 2

    def attempt(again, carry):
        @pl.when(jnp.logical_or(again == 0, top_s[0] > 0))
        def _():
            for qp in range(tiles):
                for h in range(heads):
                    if mixed:
                        st[0, h] = jnp.concatenate([state_in[part, h, :, columns_of] for part in range(2)], axis=1)
                    elif first:
                        st[qp, h, sums] = jnp.zeros((HEAD_DIM + STAT, rows), jnp.float32)
                        st[qp, h, point] = jnp.full((STAT, rows), NEG, jnp.float32)
                    else:
                        st[qp, h] = state_in[qp, h]

            def one_part(qp, carry):
                pairs = count_s[qp]
                switch = jnp.where(again > 0, pairs, 1 if first else 0)

                def both(*accs):
                    units = [accs[3 * unit : 3 * unit + 3] for unit in range(UNITS)]

                    def one_slow(t, carry):
                        slow(units, qp, t)
                        return carry

                    def one_fast(t, carry):
                        fast(units, qp, t)
                        return carry

                    lax.fori_loop(0, switch, one_slow, 0)
                    lax.fori_loop(switch, pairs, one_fast, 0)

                accumulators = []
                for unit in range(UNITS):
                    accumulators += [pltpu.ACC(unit)((tok, rows), jnp.float32)] * 2
                    accumulators.append(pltpu.ACC(unit)((HEAD_DIM + ONES, rows), jnp.float32))
                pl.run_scoped(both, *accumulators)
                return carry

            lax.fori_loop(0, tiles, one_part, 0)
            top = jnp.zeros((STAT, rows), jnp.float32)
            for qp in range(tiles):
                for h in range(heads):
                    top = jnp.maximum(top, jnp.where(st[qp, h, weights] < LARGE, 0.0, 1.0))
            top_s[0] = (jnp.max(top) > 0.0).astype(jnp.int32)

        return carry

    top_s[0] = 0
    lax.fori_loop(0, 2, attempt, 0)
    if last:
        for qp in range(tiles):
            for h in range(heads):
                lanes = slice(h * HEAD_DIM, (h + 1) * HEAD_DIM)
                inv = 1.0 / st[qp, h, weights]
                att = st[qp, h, :HEAD_DIM].reshape(-1, STAT, rows) * inv[None]
                att = att.reshape(HEAD_DIM, rows).T.astype(jnp.bfloat16)
                if mixed:
                    outs[0][:, lanes] = att[: rows // 2]
                    outs[1][:, lanes] = att[rows // 2 :]
                else:
                    outs[0][qp * rows : (qp + 1) * rows, lanes] = att


class GridPlace:
    near = True

    def __init__(self, metas, n_a, n_b, tok):
        self.metas, self.n_a, self.n_b, self.tok = metas, n_a, n_b, tok

    def query(self, own, part):
        return (own // CORES) * CORES + (own % CORES + part) % CORES

    def sources(self, own, i, part):
        a, b, c = own // (CORES * self.n_b), (own // CORES) % self.n_b, own % CORES
        return [
            ((a ^ flip) * self.n_b + (b + db) % self.n_b) * CORES + (c + part) % CORES
            for _, _, flip, db in self.metas[i]
        ]

    def refs(self, items, i, part):
        rows = self.tok // 2
        return [items[n].at[pl.ds(base + part * rows, rows)] for n, base, _, _ in self.metas[i]]


class FlatPlace:
    near = False

    def __init__(self, tok):
        self.tok = tok

    def query(self, own, part):
        return own

    def sources(self, own, i, part):
        return [i, i]

    def refs(self, items, i, part):
        return [items[0].at[pl.ds(i * self.tok, self.tok)]]


def other_columns(own, pieces):
    rows, width = pieces[0].shape
    half = width // CORES
    vmem = pl.BlockSpec(memory_space=pltpu.VMEM)

    def kernel(own_ref, *refs):
        lanes = pl.ds(pl.multiple_of((own_ref[0] + 1) % CORES * half, half), half)
        for i, ref in enumerate(refs[:-1]):
            refs[-1][i * rows : (i + 1) * rows] = ref[:, lanes]

    return pl.pallas_call(
        kernel,
        out_shape=jax.ShapeDtypeStruct((len(pieces) * rows, half), pieces[0].dtype),
        in_specs=[pl.BlockSpec(memory_space=pltpu.SMEM)] + [vmem] * len(pieces),
        out_specs=vmem,
        compiler_params=pltpu.CompilerParams(vmem_limit_bytes=VMEM_LIMIT),
        cost_estimate=LITTLE,
        name="other_columns",
    )(own, *pieces)


def moved(kernel, args, shapes, name):
    vmem = pl.BlockSpec(memory_space=pltpu.VMEM)
    return pl.pallas_call(
        kernel,
        out_shape=[jax.ShapeDtypeStruct(shape, jnp.bfloat16) for shape in shapes],
        in_specs=[pl.BlockSpec(memory_space=pltpu.SMEM)] + [vmem] * (len(args) - 1),
        out_specs=[vmem] * len(shapes),
        compiler_params=pltpu.CompilerParams(vmem_limit_bytes=VMEM_LIMIT),
        cost_estimate=SOME if name == "joined" else LITTLE,
        name=name,
    )(*args)


def joined(own, above, below):
    rows, width = above.shape

    def kernel(own_ref, above_ref, below_ref, out_ref):
        out_ref[:rows] = above_ref[...]
        out_ref[rows:] = below_ref[...]

    return moved(kernel, (own, above, below), [(2 * rows, width)], "joined")[0]


def lower_half(own, x):
    rows, width = x.shape

    def kernel(own_ref, x_ref, out_ref):
        out_ref[...] = x_ref[rows // 2 :]

    return moved(kernel, (own, x), [(rows // 2, width)], "lower_half")[0]


def picked(own, at_ends, at_middle, n_a, n_b):
    rows, width = at_ends.shape

    def kernel(own_ref, ends_ref, middle_ref, whole_ref, half_ref):
        a = own_ref[0] // (CORES * n_b)
        at_end = jnp.logical_or(a == 0, a == n_a - 1)

        def take(ref):
            whole_ref[...] = ref[...]
            half_ref[...] = ref[: rows // 2]

        pl.when(at_end)(lambda: take(ends_ref))
        pl.when(jnp.logical_not(at_end))(lambda: take(middle_ref))

    return moved(kernel, (own, at_ends, at_middle), [(rows, width), (rows // 2, width)], "picked")


def turn(own, parts):
    pieces = [x for part in parts for x in part]
    heads = min(x.shape[1] for x in pieces) // HEAD_DIM
    rows = sum(x.shape[0] for x in parts[0])
    vmem = pl.BlockSpec(memory_space=pltpu.VMEM)

    def kernel(own_ref, *refs):
        begin = own_ref[0] % CORES * heads * HEAD_DIM
        at = 0
        for qp, part in enumerate(parts):
            some = refs[at : at + len(part)]
            at += len(part)
            for h in range(heads):
                turned = []
                for ref in some:
                    first = h * HEAD_DIM
                    if ref.shape[1] > heads * HEAD_DIM:
                        first = pl.multiple_of(begin + first, HEAD_DIM)
                    turned.append(ref[:, pl.ds(first, HEAD_DIM)].astype(jnp.float32).T)
                scaled = jnp.concatenate(turned, axis=1) * SCALE
                high = scaled.astype(jnp.bfloat16)
                refs[-1][qp, h, :HEAD_DIM] = high
                refs[-1][qp, h, HEAD_DIM:] = (scaled - high.astype(jnp.float32)).astype(jnp.bfloat16)

    return pl.pallas_call(
        kernel,
        out_shape=pltpu.VMEM((len(parts), heads, 2 * HEAD_DIM, rows), jnp.bfloat16),
        in_specs=[pl.BlockSpec(memory_space=pltpu.SMEM)] + [vmem] * len(pieces),
        out_specs=vmem,
        compiler_params=pltpu.CompilerParams(vmem_limit_bytes=VMEM_LIMIT),
        cost_estimate=LITTLE,
        name="turn",
    )(own, *pieces)


def attend(scalars, q, state, arrays, place, n_items, parts, tok, last, half=None):
    first = state is None
    heads, rows = q.shape[1], q.shape[3]
    width = arrays[0].shape[1]
    smem = pl.BlockSpec(memory_space=pltpu.SMEM)
    vmem = pl.BlockSpec(memory_space=pltpu.VMEM)
    args = list(scalars) + [pinned(q)] + ([] if first else [pinned(state)])
    args += [pinned(x) if place.near else x for x in arrays]
    specs = [smem] * 3 + [vmem] + ([] if first else [vmem])
    specs += [vmem if place.near else pl.BlockSpec(memory_space=pl.ANY)] * len(arrays)
    shape = (parts, heads, HEAD_DIM + 2 * STAT, rows)
    tile_shape = shape if half is None else (1,) + shape[1:]
    blocks = n_items * parts
    scratch = [
        pltpu.VMEM(tile_shape if last else (STAT, HEAD_DIM), jnp.float32),
        pltpu.VMEM((1,) + q.shape[1:] if half is not None else (ONES, HEAD_DIM), jnp.bfloat16),
        pltpu.VMEM((blocks, tok, width), jnp.bfloat16),
        pltpu.VMEM((blocks, heads // GROUP, HEAD_DIM + ONES, tok), jnp.bfloat16),
        pltpu.SMEM((parts, blocks + 1), jnp.int32),
        pltpu.SMEM((blocks + 1,), jnp.int32),
        pltpu.SMEM((parts, 2 * blocks), jnp.int32),
        pltpu.SMEM((parts,), jnp.int32),
        pltpu.SMEM((parts,), jnp.int32),
        pltpu.SMEM((1,), jnp.int32),
        pltpu.SemaphoreType.DMA((blocks, 2)),
    ]
    if last:
        out_shape = [jax.ShapeDtypeStruct((parts * rows, heads * HEAD_DIM), jnp.bfloat16)]
        if half is not None:
            out_shape = [jax.ShapeDtypeStruct((rows // 2, heads * HEAD_DIM), jnp.bfloat16)] * 2
    else:
        out_shape = [pltpu.VMEM(shape, jnp.float32)]

    def kernel(*refs):
        attend_kernel(place, n_items, parts, half, rows, tok, first, last, refs)

    return pl.pallas_call(
        kernel,
        out_shape=out_shape,
        in_specs=specs,
        out_specs=[vmem] * len(out_shape),
        scratch_shapes=scratch,
        compiler_params=pltpu.CompilerParams(vmem_limit_bytes=VMEM_LIMIT),
        cost_estimate=LITTLE,
        name="attend",
    )(*args)


def pinned(x):
    return pltpu.with_memory_space_constraint(x, pltpu.VMEM)


def fetch(weight):
    chunks = 12
    rows = weight.shape[0] // chunks

    def kernel(weight_ref, out_ref, sems):
        copies = [
            pltpu.make_async_copy(
                weight_ref.at[pl.ds(i * rows, rows)], out_ref.at[pl.ds(i * rows, rows)], sems.at[i]
            )
            for i in range(chunks)
        ]
        for one in copies:
            one.start()
        for one in copies:
            one.wait()

    return pl.pallas_call(
        kernel,
        out_shape=pltpu.VMEM(weight.shape, weight.dtype),
        in_specs=[pl.BlockSpec(memory_space=pltpu.HBM)],
        out_specs=pl.BlockSpec(memory_space=pltpu.VMEM),
        scratch_shapes=[pltpu.SemaphoreType.DMA((chunks,))],
        compiler_params=pltpu.CompilerParams(vmem_limit_bytes=VMEM_LIMIT),
        cost_estimate=LITTLE,
        name="fetch",
    )(pltpu.with_memory_space_constraint(weight, pltpu.HBM))


def project(own, parts, weight, rows, partial=None, ending=None):
    width = weight.shape[1]
    depth = parts[0][0].shape[1]
    tile = math.gcd(width, 512)
    smem = pl.BlockSpec(memory_space=pltpu.SMEM)
    vmem = pl.BlockSpec(memory_space=pltpu.VMEM)
    n = len(parts)
    args = [own] + [x for x, _, _ in parts] + [pinned(weight)]
    specs = [smem] + [vmem] * (n + 1)
    scratch = []
    out_shape = [jax.ShapeDtypeStruct((rows, width), jnp.bfloat16)]
    if partial is not None:
        args.append(pinned(partial))
        specs.append(vmem)
    elif ending is not None:
        args += list(ending)
        args[-2] = pltpu.with_memory_space_constraint(args[-2], pltpu.HBM)
        specs += [smem] * 2 + [pl.BlockSpec(memory_space=pltpu.HBM), vmem]
        out_shape = [pltpu.VMEM((rows, width), jnp.float32), pltpu.VMEM((STAT, width), jnp.float32)]
        scratch = [pltpu.VMEM((STAT, width), jnp.float32), pltpu.SemaphoreType.DMA]
    else:
        out_shape = [pltpu.VMEM((rows, width), jnp.float32)]

    def kernel(*refs):
        own_ref, part_refs, weight_ref, refs = refs[0], refs[1 : n + 1], refs[n + 1], refs[n + 2 :]
        if ending is not None:
            steps_ref, map_ref, gate_ref, residual_ref, out_ref, row_ref, near, sem = refs
            step = steps_ref[map_ref[own_ref[0]]]
            copy = pltpu.make_async_copy(
                gate_ref.at[pl.ds(pl.multiple_of((step // STAT) * STAT, STAT), STAT)], near, sem
            )
            copy.start()
            copy.wait()
            chosen = lax.broadcasted_iota(jnp.int32, (STAT, width), 0) == step % STAT
            row = jnp.sum(jnp.where(chosen, near[...], 0.0), axis=0, keepdims=True)
            row_ref[...] = jnp.broadcast_to(row, (STAT, width))
        else:
            out_ref = refs[-1]

        def one(t, carry):
            lanes = pl.ds(pl.multiple_of(t * tile, tile), tile)
            total = None
            for j in range(n):
                first_row = parts[j][2]
                group = (own_ref[0] + parts[j][1]) % CORES
                weight_rows = pl.ds(pl.multiple_of(group * depth, depth), depth)
                term = jnp.dot(
                    part_refs[j][first_row : first_row + rows],
                    weight_ref[weight_rows, lanes],
                    preferred_element_type=jnp.float32,
                )
                total = term if total is None else total + term
            if partial is not None:
                total = total + refs[0][:, lanes]
            if ending is not None:
                gate = jnp.concatenate([row_ref[:, lanes]] * (rows // STAT), axis=0)
                total = residual_ref[:, lanes].astype(jnp.float32) + gate * total
            out_ref[:, lanes] = total.astype(out_ref.dtype)
            return carry

        lax.fori_loop(0, width // tile, one, 0)

    return pl.pallas_call(
        kernel,
        out_shape=out_shape,
        in_specs=specs,
        out_specs=[vmem] * len(out_shape),
        scratch_shapes=scratch,
        compiler_params=pltpu.CompilerParams(vmem_limit_bytes=VMEM_LIMIT),
        cost_estimate=pl.CostEstimate(
            flops=2 * rows * depth * n * width, bytes_accessed=2 * depth * n * width, transcendentals=0
        ),
        name="project",
    )(*args)


def columns(x, part, width):
    return lax.dynamic_slice_in_dim(x, part * width, width, 1)


def paired(query_rows, key_rows, value_rows, out_weight, scalars, ending, n_a, n_b):
    n_seq = n_a * n_b * CORES
    groups = 2 * CORES
    own = scalars[0]
    kvw = key_rows.shape[1] // groups
    rows = query_rows.shape[0]
    tok = 2 * rows
    x = lax.axis_index("head")
    c = lax.axis_index("seq") % CORES

    def index(a, b, k):
        return (a * n_b + b) * CORES + k

    def swapped(piece, dx, dc):
        pairs = [
            ((s ^ dc) * 2 + (h ^ dx), s * 2 + h) for s in range(n_seq) for h in range(2)
        ]
        return lax.ppermute(piece, ("seq", "head"), pairs)

    def along_a(piece, moves):
        pairs = [
            (index(a, b, k), index(to, b, k)) for a, to in moves for b in range(n_b) for k in range(CORES)
        ]
        return lax.ppermute(piece, "seq", pairs)

    def beside_of(piece, only):
        pairs = [
            (index(a, 1 - b, k), index(a, b, k)) for a in only for b in range(n_b) for k in range(CORES)
        ]
        return lax.ppermute(piece, "seq", pairs)

    def stage(state, q, arrays, metas, last=False, half=None):
        return attend(
            scalars, q, state, arrays, GridPlace(metas, n_a, n_b, tok), len(metas), CORES, tok, last, half
        )

    def halves_of(first, base, flip, db):
        if isinstance(first, int):
            return [(first, base, flip, db), (first, base + tok, flip, db)]
        return [(n, base, flip, db) for n in first]

    def kv_for(dx, dc):
        j = (x ^ dx) * CORES + (c ^ dc)
        return jnp.concatenate([columns(key_rows, j, kvw), columns(value_rows, j, kvw)], axis=1)

    chips = list(range(n_a))
    order = [(0, 0), (1, 0), (0, 1), (1, 1)]
    pieces = {d: kv_for(*d) if sum(d) == 0 else swapped(kv_for(*d), *d) for d in order}
    early = jnp.concatenate([pieces[0, 0], pieces[0, 1]], axis=0)
    later = jnp.concatenate([pieces[1, 0], pieces[1, 1]], axis=0)
    block = jnp.concatenate([early, later], axis=0)
    qw = query_rows.shape[1] // 2
    q_own, q_other = columns(query_rows, x, qw), columns(query_rows, 1 - x, qw)
    block, later, out_weight, q_own, q_other = lax.optimization_barrier(
        (block, later, out_weight, q_own, q_other)
    )
    by_one, by_two = [(a, a ^ 1) for a in chips], [(a, a ^ 2) for a in chips]
    beside = beside_of(block, chips)
    next_early, far_early = along_a(early, by_one), along_a(early, by_two)
    q_came = swapped(q_other, 1, 0)
    weight = fetch(out_weight)
    next_early, far_early, weight = lax.optimization_barrier((next_early, far_early, weight))
    both_early = joined(own, next_early, far_early)
    later, both_early = lax.optimization_barrier((later, both_early))
    beside, both_early, q_came = lax.optimization_barrier((beside, both_early, q_came))
    beside_early = beside_of(both_early, chips)
    next_later, far_later = along_a(later, by_one), along_a(later, by_two)
    q_core = swapped(other_columns(own, [q_own, q_came]), 0, 1)
    both_later, far = joined(own, next_later, far_later), joined(own, far_early, far_later)
    both_later, far, again, q_core = lax.optimization_barrier((both_later, far, block, q_core))
    to_ends = along_a(far, [(1, 0), (2, 3)])
    to_middle = along_a(again, [(1, 2), (2, 1)])
    both_later, beside_early = lax.optimization_barrier((both_later, beside_early))
    beside_later = beside_of(both_later, chips)
    q = turn(own, [[q_own, q_came], [q_core]])
    (state,) = stage(None, q, [block, beside], [halves_of(0, 0, 0, 0), halves_of(1, 0, 0, 1)])
    (state,) = stage(
        state, q, [next_early, next_later, far_early, far_later],
        [halves_of((0, 1), 0, 1, 0), halves_of((2, 3), 0, 2, 0)],
    )
    to_ends, to_middle, beside_later, state = lax.optimization_barrier((to_ends, to_middle, beside_later, state))
    last, last_upper = picked(own, to_ends, to_middle, n_a, n_b)
    beside_last = [beside_of(last_upper, chips), along_a(lower_half(own, beside_later), by_one)]
    (state,) = stage(
        state, q, [beside_early, beside_later, last],
        [[(0, 0, 1, 1), (0, tok, 2, 1)], [(1, 0, 1, 1), (1, tok, 2, 1)], halves_of(2, 0, 3, 0)],
    )
    last_block = [halves_of((0, 1), 0, 3, 1)]
    kept, sent = stage(state, q, beside_last, last_block, True, 1)
    came = swapped(sent, 0, 1)
    (begun,) = project(own, [(kept, 0, 0)], weight, rows)
    (theirs,) = project(own, [(came, 1, 0)], weight, rows, partial=begun)
    came_back = lax.ppermute(theirs, "head", [(0, 1), (1, 0)])
    state, theirs = lax.optimization_barrier((state, theirs))
    kept, sent = stage(state, q, beside_last, last_block, True, 0)
    came = swapped(sent, 0, 1)
    base, gate = project(own, [(kept, 0, 0), (came, 1, 0)], weight, rows, ending=ending)
    return (base + gate[:1] * came_back.astype(jnp.float32)).astype(jnp.bfloat16)


def gathered_attention(query_rows, key_rows, value_rows, scalars):
    spread = functools.partial(lax.all_to_all, axis_name="head", split_axis=1, concat_axis=0, tiled=True)
    local = jnp.concatenate([spread(key_rows), spread(value_rows)], axis=1)
    every = lax.all_gather(local, "seq", axis=0, tiled=True)
    tok = local.shape[0]
    return attend(
        scalars, turn(scalars[0], [[spread(query_rows)]]), None, [every], FlatPlace(tok), every.shape[0] // tok, 1, tok, True
    )[0]


def per_device(
    query_rows,
    key_rows,
    value_rows,
    residual,
    out_weight,
    gate_table,
    noise_steps,
    segment_mask,
    segment_map,
):
    n_seq = lax.axis_size("seq")
    n_head = lax.axis_size("head")
    own_seq = lax.axis_index("seq").astype(jnp.int32)
    own = own_seq.reshape(1)
    scalars = (own, segment_map, segment_mask)
    n_a, n_b = grid_of(n_seq)
    if n_head == 2 and n_a == 4 and n_b == 2:
        ending = (noise_steps, segment_map, gate_table, residual)
        return paired(query_rows, key_rows, value_rows, out_weight, scalars, ending, n_a, n_b)
    attended = gathered_attention(query_rows, key_rows, value_rows, scalars)
    projected = lax.psum_scatter(
        jnp.dot(attended, out_weight, preferred_element_type=jnp.float32).astype(jnp.bfloat16),
        "head",
        scatter_dimension=0,
        tiled=True,
    ).astype(jnp.float32)
    gate_row = lax.dynamic_slice_in_dim(gate_table, noise_steps[segment_map[own_seq]], 1, 0)
    return (residual.astype(jnp.float32) + gate_row * projected).astype(jnp.bfloat16)


def solution(mesh):
    placed = (
        P(("seq", "head"), None),
        P(("seq", "head"), None),
        P(("seq", "head"), None),
        P(("seq", "head"), None),
        P("head", None),
        P(),
        P(),
        P(),
        P(),
    )
    return jax.shard_map(
        per_device, mesh=mesh, in_specs=placed, out_specs=P(("seq", "head"), None), check_vma=False
    )
```

```python
import functools
import math

import jax
import jax.numpy as jnp
from jax import lax
from jax.experimental import pallas as pl
from jax.experimental.pallas import tpu as pltpu
from jax.sharding import PartitionSpec as P

Q_HEADS = 24
KV_HEADS = 8
HEAD_DIM = 128
GROUP = Q_HEADS // KV_HEADS
CORES = 2
UNITS = 2
NEG = -1e30
SCALE = 1.4426950408889634 * HEAD_DIM ** -0.5
STAT = 8
ONES = 16
LARGE = 1e27
VMEM_LIMIT = 24 * 1024 * 1024
SOME = pl.CostEstimate(flops=3000000000, bytes_accessed=1, transcendentals=0)
LITTLE = pl.CostEstimate(flops=1, bytes_accessed=1, transcendentals=0)


def grid_of(n_seq):
    chips = n_seq // CORES
    inner = 2 ** (int(math.log2(chips)) // 2)
    return chips // inner, inner


def attend_kernel(place, n_items, parts, half, rows, tok, first, last, refs):
    own_ref, map_ref, mask_ref, q_ref = refs[:4]
    mixed = half is not None
    tiles = 1 if mixed else parts
    state_in = None if first else refs[4]
    st_s, qt_s, kv_s, vt_s, list_s, land_s, seen_s, full_s, count_s, top_s, sems = refs[-11:]
    outs = 2 if mixed else 1
    items, outs = refs[4 if first else 5 : -11 - outs], refs[-11 - outs : -11]
    st, qt = st_s if last else outs[0], qt_s if mixed else q_ref
    heads = qt.shape[1]
    kv_heads = heads // GROUP
    kvw = kv_heads * HEAD_DIM
    own = own_ref[0]
    sums = slice(0, HEAD_DIM + STAT)
    weights = slice(HEAD_DIM, HEAD_DIM + STAT)
    point = slice(HEAD_DIM + STAT, HEAD_DIM + 2 * STAT)

    def copies(i, kp, ik):
        pieces = place.refs(items, i, kp)
        size = tok // len(pieces)
        return [
            pltpu.make_async_copy(piece, kv_s.at[ik, pl.ds(j * size, size)], sems.at[ik, j])
            for j, piece in enumerate(pieces)
        ]

    seg_q = [map_ref[place.query(own, j)] for j in range(parts)]
    counts = [jnp.int32(0)] * tiles
    landed = jnp.int32(0)
    for i in range(n_items):
        for kp in range(parts):
            ik = i * parts + kp
            seg_k = [map_ref[src] for src in place.sources(own, i, kp)]
            any_seen = jnp.int32(0)
            for qp in range(parts):
                seen = jnp.int32(0)
                for n in range(2):
                    seen_half = (mask_ref[seg_q[qp], seg_k[n]] > 0).astype(jnp.int32)
                    seen_s[qp, 2 * ik + n] = seen_half
                    seen = jnp.maximum(seen, seen_half)
                any_seen = jnp.maximum(any_seen, seen)
                if not mixed:
                    list_s[qp, counts[qp]] = ik
                    counts[qp] = counts[qp] + seen
            if mixed:
                list_s[0, counts[0]] = ik
                counts[0] = counts[0] + any_seen
            land_s[landed] = ik
            landed = landed + any_seen

            @pl.when(any_seen > 0)
            def _():
                if place.near:
                    pieces = place.refs(items, i, kp)
                    size = tok // len(pieces)
                    for j, piece in enumerate(pieces):
                        kv_s[ik, j * size : (j + 1) * size] = piece[...]
                else:
                    for one in copies(i, kp, ik):
                        one.start()

    ones = jnp.ones((ONES, tok), jnp.bfloat16)

    def land(t, carry):
        ik = land_s[t]
        if not place.near:
            for one in copies(0, 0, ik):
                one.wait()
        for kh in range(kv_heads):
            v = kv_s[ik, :, kvw + kh * HEAD_DIM : kvw + (kh + 1) * HEAD_DIM]
            vt_s[ik, kh, :HEAD_DIM] = v.T
            vt_s[ik, kh, HEAD_DIM:] = ones
        return carry

    lax.fori_loop(0, landed, land, 0)

    def blocks(qp, t):
        single = 2 * t + 1 >= full_s[qp]
        i0 = list_s[qp, 2 * t]
        i1 = list_s[qp, jnp.where(single, 2 * t, 2 * t + 1)]
        if mixed:
            left = lax.broadcasted_iota(jnp.int32, (STAT, rows), 1) < rows // 2
        bias = []
        for i in (i0, i1):
            for n in range(2):
                hidden = [
                    jnp.where(seen_s[part, 2 * i + n] > 0, jnp.float32(0.0), jnp.float32(NEG))
                    for part in ((0, 1) if mixed else (qp,))
                ]
                bias.append(jnp.where(left, hidden[0], hidden[1]) if mixed else hidden[0])
        again = jnp.where(single, jnp.float32(NEG), jnp.float32(0.0))
        bias[2:] = [one + again for one in bias[2:]]
        return i0, i1, bias

    def operands(kh, i0, i1):
        lanes = slice(kh * HEAD_DIM, (kh + 1) * HEAD_DIM)
        return (
            [jnp.concatenate([kv_s[i, :, lanes]] * 2, axis=1) for i in (i0, i1)],
            [vt_s[i, kh] for i in (i0, i1)],
        )

    def slow(units, qp, t):
        i0, i1, bias = blocks(qp, t)
        for h in range(heads):
            kh = h // GROUP
            unit = kh % UNITS
            s0_acc, s1_acc, pv_acc = units[unit]
            keys, values = operands(kh, i0, i1)
            pltpu.matmul_push_rhs(qt[qp, h], 0, unit)
            pltpu.matmul_acc_lhs(s0_acc, keys[0], 0)
            pltpu.matmul_acc_lhs(s1_acc, keys[1])
            s = [pltpu.matmul_pop(acc).reshape(-1, STAT, rows) for acc in (s0_acc, s1_acc)]
            before = st[qp, h, point]
            quarters = [x[n * (tok // 16) : (n + 1) * (tok // 16)] for x in s for n in range(2)]
            top = functools.reduce(jnp.maximum, [jnp.max(x, axis=0) + one for x, one in zip(quarters, bias)])
            now = jnp.maximum(before, jnp.max(top, axis=0, keepdims=True))
            for j, value in enumerate(values):
                p = [jnp.exp2(quarters[2 * j + n] - (now - bias[2 * j + n])[None]) for n in range(2)]
                p = jnp.concatenate(p, axis=0).reshape(tok, rows).astype(jnp.bfloat16)
                pltpu.matmul_push_rhs(p, 1, unit)
                pltpu.matmul_acc_lhs(pv_acc, value, 1)
            kept = st[qp, h, sums].reshape(-1, STAT, rows) * jnp.exp2(before - now)[None]
            st[qp, h, sums] = kept.reshape(-1, rows) + pltpu.matmul_pop(pv_acc)[sums]
            st[qp, h, point] = now

    def fast(units, qp, t):
        i0, i1, bias = blocks(qp, t)
        keys, values = zip(*[operands(kh, i0, i1) for kh in range(kv_heads)])

        def begin(kh, g):
            unit = units[kh % len(units)]
            pltpu.matmul_push_rhs(qt[qp, kh * GROUP + g], 0, kh % len(units))
            pltpu.matmul_acc_lhs(unit[0], keys[kh][0], 0)
            pltpu.matmul_acc_lhs(unit[1], keys[kh][1])

        def weights_of(kh, g, j):
            s = pltpu.matmul_pop(units[kh % len(units)][j]).reshape(-1, STAT, rows)
            ref = st[qp, kh * GROUP + g, point]
            p = [
                jnp.exp2(s[n * (tok // 16) : (n + 1) * (tok // 16)] - (ref - bias[2 * j + n])[None])
                for n in range(2)
            ]
            return jnp.concatenate(p, axis=0).reshape(tok, rows).astype(jnp.bfloat16)

        for first_kh in range(0, kv_heads, len(units)):
            together = range(first_kh, min(first_kh + len(units), kv_heads))
            for kh in together:
                begin(kh, 0)
            for g in range(GROUP):
                p = {(kh, j): weights_of(kh, g, j) for j in range(2) for kh in together}
                if g + 1 < GROUP:
                    for kh in together:
                        begin(kh, g + 1)
                for j in range(2):
                    for kh in together:
                        pltpu.matmul_push_rhs(p[kh, j], 1, kh % len(units))
                        pltpu.matmul_acc_lhs(units[kh % len(units)][2], values[kh][j], 1)
                for kh in together:
                    h = kh * GROUP + g
                    st[qp, h, sums] = st[qp, h, sums] + pltpu.matmul_pop(units[kh % len(units)][2])[sums]

    columns_of = slice(half * rows // 2, (half + 1) * rows // 2) if mixed else slice(0, rows)
    if mixed:
        for h in range(heads):
            qt_s[0, h] = jnp.concatenate([q_ref[part, h, :, columns_of] for part in range(2)], axis=1)
    for qp in range(tiles):
        full_s[qp] = counts[qp]
        count_s[qp] = (counts[qp] + 1) // 2

    def attempt(again, carry):
        @pl.when(jnp.logical_or(again == 0, top_s[0] > 0))
        def _():
            for qp in range(tiles):
                for h in range(heads):
                    if mixed:
                        st[0, h] = jnp.concatenate([state_in[part, h, :, columns_of] for part in range(2)], axis=1)
                    elif first:
                        st[qp, h, sums] = jnp.zeros((HEAD_DIM + STAT, rows), jnp.float32)
                        st[qp, h, point] = jnp.full((STAT, rows), NEG, jnp.float32)
                    else:
                        st[qp, h] = state_in[qp, h]

            def one_part(qp, carry):
                pairs = count_s[qp]
                switch = jnp.where(again > 0, pairs, 1 if first else 0)

                def both(*accs):
                    units = [accs[3 * unit : 3 * unit + 3] for unit in range(UNITS)]

                    def one_slow(t, carry):
                        slow(units, qp, t)
                        return carry

                    def one_fast(t, carry):
                        fast(units, qp, t)
                        return carry

                    lax.fori_loop(0, switch, one_slow, 0)
                    lax.fori_loop(switch, pairs, one_fast, 0)

                accumulators = []
                for unit in range(UNITS):
                    accumulators += [pltpu.ACC(unit)((tok, rows), jnp.float32)] * 2
                    accumulators.append(pltpu.ACC(unit)((HEAD_DIM + ONES, rows), jnp.float32))
                pl.run_scoped(both, *accumulators)
                return carry

            lax.fori_loop(0, tiles, one_part, 0)
            top = jnp.zeros((STAT, rows), jnp.float32)
            for qp in range(tiles):
                for h in range(heads):
                    top = jnp.maximum(top, jnp.where(st[qp, h, weights] < LARGE, 0.0, 1.0))
            top_s[0] = (jnp.max(top) > 0.0).astype(jnp.int32)

        return carry

    top_s[0] = 0
    lax.fori_loop(0, 2, attempt, 0)
    if last:
        for qp in range(tiles):
            for h in range(heads):
                lanes = slice(h * HEAD_DIM, (h + 1) * HEAD_DIM)
                inv = 1.0 / st[qp, h, weights]
                att = st[qp, h, :HEAD_DIM].reshape(-1, STAT, rows) * inv[None]
                att = att.reshape(HEAD_DIM, rows).T.astype(jnp.bfloat16)
                if mixed:
                    outs[0][:, lanes] = att[: rows // 2]
                    outs[1][:, lanes] = att[rows // 2 :]
                else:
                    outs[0][qp * rows : (qp + 1) * rows, lanes] = att


class GridPlace:
    near = True

    def __init__(self, metas, n_a, n_b, tok):
        self.metas, self.n_a, self.n_b, self.tok = metas, n_a, n_b, tok

    def query(self, own, part):
        return (own // CORES) * CORES + (own % CORES + part) % CORES

    def sources(self, own, i, part):
        a, b, c = own // (CORES * self.n_b), (own // CORES) % self.n_b, own % CORES
        return [
            ((a ^ flip) * self.n_b + (b + db) % self.n_b) * CORES + (c + part) % CORES
            for _, _, flip, db in self.metas[i]
        ]

    def refs(self, items, i, part):
        rows = self.tok // 2
        return [items[n].at[pl.ds(base + part * rows, rows)] for n, base, _, _ in self.metas[i]]


class FlatPlace:
    near = False

    def __init__(self, tok):
        self.tok = tok

    def query(self, own, part):
        return own

    def sources(self, own, i, part):
        return [i, i]

    def refs(self, items, i, part):
        return [items[0].at[pl.ds(i * self.tok, self.tok)]]


def other_columns(own, pieces):
    rows, width = pieces[0].shape
    half = width // CORES
    vmem = pl.BlockSpec(memory_space=pltpu.VMEM)

    def kernel(own_ref, *refs):
        lanes = pl.ds(pl.multiple_of((own_ref[0] + 1) % CORES * half, half), half)
        for i, ref in enumerate(refs[:-1]):
            refs[-1][i * rows : (i + 1) * rows] = ref[:, lanes]

    return pl.pallas_call(
        kernel,
        out_shape=jax.ShapeDtypeStruct((len(pieces) * rows, half), pieces[0].dtype),
        in_specs=[pl.BlockSpec(memory_space=pltpu.SMEM)] + [vmem] * len(pieces),
        out_specs=vmem,
        compiler_params=pltpu.CompilerParams(vmem_limit_bytes=VMEM_LIMIT),
        cost_estimate=LITTLE,
        name="other_columns",
    )(own, *pieces)


def moved(kernel, args, shapes, name):
    vmem = pl.BlockSpec(memory_space=pltpu.VMEM)
    return pl.pallas_call(
        kernel,
        out_shape=[jax.ShapeDtypeStruct(shape, jnp.bfloat16) for shape in shapes],
        in_specs=[pl.BlockSpec(memory_space=pltpu.SMEM)] + [vmem] * (len(args) - 1),
        out_specs=[vmem] * len(shapes),
        compiler_params=pltpu.CompilerParams(vmem_limit_bytes=VMEM_LIMIT),
        cost_estimate=SOME if name in ("joined", "picked") else LITTLE,
        name=name,
    )(*args)


def joined(own, above, below):
    rows, width = above.shape

    def kernel(own_ref, above_ref, below_ref, out_ref):
        out_ref[:rows] = above_ref[...]
        out_ref[rows:] = below_ref[...]

    return moved(kernel, (own, above, below), [(2 * rows, width)], "joined")[0]


def lower_half(own, x):
    rows, width = x.shape

    def kernel(own_ref, x_ref, out_ref):
        out_ref[...] = x_ref[rows // 2 :]

    return moved(kernel, (own, x), [(rows // 2, width)], "lower_half")[0]


def picked(own, at_ends, at_middle, n_a, n_b):
    rows, width = at_ends.shape

    def kernel(own_ref, ends_ref, middle_ref, whole_ref, half_ref):
        a = own_ref[0] // (CORES * n_b)
        at_end = jnp.logical_or(a == 0, a == n_a - 1)

        def take(ref):
            whole_ref[...] = ref[...]
            half_ref[...] = ref[: rows // 2]

        pl.when(at_end)(lambda: take(ends_ref))
        pl.when(jnp.logical_not(at_end))(lambda: take(middle_ref))

    return moved(kernel, (own, at_ends, at_middle), [(rows, width), (rows // 2, width)], "picked")


def turn(own, parts):
    pieces = [x for part in parts for x in part]
    heads = min(x.shape[1] for x in pieces) // HEAD_DIM
    rows = sum(x.shape[0] for x in parts[0])
    vmem = pl.BlockSpec(memory_space=pltpu.VMEM)

    def kernel(own_ref, *refs):
        begin = own_ref[0] % CORES * heads * HEAD_DIM
        at = 0
        for qp, part in enumerate(parts):
            some = refs[at : at + len(part)]
            at += len(part)
            for h in range(heads):
                turned = []
                for ref in some:
                    first = h * HEAD_DIM
                    if ref.shape[1] > heads * HEAD_DIM:
                        first = pl.multiple_of(begin + first, HEAD_DIM)
                    turned.append(ref[:, pl.ds(first, HEAD_DIM)].astype(jnp.float32).T)
                scaled = jnp.concatenate(turned, axis=1) * SCALE
                high = scaled.astype(jnp.bfloat16)
                refs[-1][qp, h, :HEAD_DIM] = high
                refs[-1][qp, h, HEAD_DIM:] = (scaled - high.astype(jnp.float32)).astype(jnp.bfloat16)

    return pl.pallas_call(
        kernel,
        out_shape=pltpu.VMEM((len(parts), heads, 2 * HEAD_DIM, rows), jnp.bfloat16),
        in_specs=[pl.BlockSpec(memory_space=pltpu.SMEM)] + [vmem] * len(pieces),
        out_specs=vmem,
        compiler_params=pltpu.CompilerParams(vmem_limit_bytes=VMEM_LIMIT),
        cost_estimate=LITTLE,
        name="turn",
    )(own, *pieces)


def attend(scalars, q, state, arrays, place, n_items, parts, tok, last, half=None):
    first = state is None
    heads, rows = q.shape[1], q.shape[3]
    width = arrays[0].shape[1]
    smem = pl.BlockSpec(memory_space=pltpu.SMEM)
    vmem = pl.BlockSpec(memory_space=pltpu.VMEM)
    args = list(scalars) + [pinned(q)] + ([] if first else [pinned(state)])
    args += [pinned(x) if place.near else x for x in arrays]
    specs = [smem] * 3 + [vmem] + ([] if first else [vmem])
    specs += [vmem if place.near else pl.BlockSpec(memory_space=pl.ANY)] * len(arrays)
    shape = (parts, heads, HEAD_DIM + 2 * STAT, rows)
    tile_shape = shape if half is None else (1,) + shape[1:]
    blocks = n_items * parts
    scratch = [
        pltpu.VMEM(tile_shape if last else (STAT, HEAD_DIM), jnp.float32),
        pltpu.VMEM((1,) + q.shape[1:] if half is not None else (ONES, HEAD_DIM), jnp.bfloat16),
        pltpu.VMEM((blocks, tok, width), jnp.bfloat16),
        pltpu.VMEM((blocks, heads // GROUP, HEAD_DIM + ONES, tok), jnp.bfloat16),
        pltpu.SMEM((parts, blocks + 1), jnp.int32),
        pltpu.SMEM((blocks + 1,), jnp.int32),
        pltpu.SMEM((parts, 2 * blocks), jnp.int32),
        pltpu.SMEM((parts,), jnp.int32),
        pltpu.SMEM((parts,), jnp.int32),
        pltpu.SMEM((1,), jnp.int32),
        pltpu.SemaphoreType.DMA((blocks, 2)),
    ]
    if last:
        out_shape = [jax.ShapeDtypeStruct((parts * rows, heads * HEAD_DIM), jnp.bfloat16)]
        if half is not None:
            out_shape = [jax.ShapeDtypeStruct((rows // 2, heads * HEAD_DIM), jnp.bfloat16)] * 2
    else:
        out_shape = [pltpu.VMEM(shape, jnp.float32)]

    def kernel(*refs):
        attend_kernel(place, n_items, parts, half, rows, tok, first, last, refs)

    return pl.pallas_call(
        kernel,
        out_shape=out_shape,
        in_specs=specs,
        out_specs=[vmem] * len(out_shape),
        scratch_shapes=scratch,
        compiler_params=pltpu.CompilerParams(vmem_limit_bytes=VMEM_LIMIT),
        cost_estimate=LITTLE,
        name="attend",
    )(*args)


def pinned(x):
    return pltpu.with_memory_space_constraint(x, pltpu.VMEM)


def fetch(weight):
    chunks = 12
    rows = weight.shape[0] // chunks

    def kernel(weight_ref, out_ref, sems):
        copies = [
            pltpu.make_async_copy(
                weight_ref.at[pl.ds(i * rows, rows)], out_ref.at[pl.ds(i * rows, rows)], sems.at[i]
            )
            for i in range(chunks)
        ]
        for one in copies:
            one.start()
        for one in copies:
            one.wait()

    return pl.pallas_call(
        kernel,
        out_shape=pltpu.VMEM(weight.shape, weight.dtype),
        in_specs=[pl.BlockSpec(memory_space=pltpu.HBM)],
        out_specs=pl.BlockSpec(memory_space=pltpu.VMEM),
        scratch_shapes=[pltpu.SemaphoreType.DMA((chunks,))],
        compiler_params=pltpu.CompilerParams(vmem_limit_bytes=VMEM_LIMIT),
        cost_estimate=LITTLE,
        name="fetch",
    )(pltpu.with_memory_space_constraint(weight, pltpu.HBM))


def project(own, parts, weight, rows, partial=None, ending=None):
    width = weight.shape[1]
    depth = parts[0][0].shape[1]
    tile = math.gcd(width, 512)
    smem = pl.BlockSpec(memory_space=pltpu.SMEM)
    vmem = pl.BlockSpec(memory_space=pltpu.VMEM)
    n = len(parts)
    args = [own] + [x for x, _, _ in parts] + [pinned(weight)]
    specs = [smem] + [vmem] * (n + 1)
    scratch = []
    out_shape = [jax.ShapeDtypeStruct((rows, width), jnp.bfloat16)]
    if partial is not None:
        args.append(pinned(partial))
        specs.append(vmem)
    elif ending is not None:
        args += list(ending)
        args[-2] = pltpu.with_memory_space_constraint(args[-2], pltpu.HBM)
        specs += [smem] * 2 + [pl.BlockSpec(memory_space=pltpu.HBM), vmem]
        out_shape = [pltpu.VMEM((rows, width), jnp.float32), pltpu.VMEM((STAT, width), jnp.float32)]
        scratch = [pltpu.VMEM((STAT, width), jnp.float32), pltpu.SemaphoreType.DMA]
    else:
        out_shape = [pltpu.VMEM((rows, width), jnp.float32)]

    def kernel(*refs):
        own_ref, part_refs, weight_ref, refs = refs[0], refs[1 : n + 1], refs[n + 1], refs[n + 2 :]
        if ending is not None:
            steps_ref, map_ref, gate_ref, residual_ref, out_ref, row_ref, near, sem = refs
            step = steps_ref[map_ref[own_ref[0]]]
            copy = pltpu.make_async_copy(
                gate_ref.at[pl.ds(pl.multiple_of((step // STAT) * STAT, STAT), STAT)], near, sem
            )
            copy.start()
            copy.wait()
            chosen = lax.broadcasted_iota(jnp.int32, (STAT, width), 0) == step % STAT
            row = jnp.sum(jnp.where(chosen, near[...], 0.0), axis=0, keepdims=True)
            row_ref[...] = jnp.broadcast_to(row, (STAT, width))
        else:
            out_ref = refs[-1]

        def one(t, carry):
            lanes = pl.ds(pl.multiple_of(t * tile, tile), tile)
            total = None
            for j in range(n):
                first_row = parts[j][2]
                group = (own_ref[0] + parts[j][1]) % CORES
                weight_rows = pl.ds(pl.multiple_of(group * depth, depth), depth)
                term = jnp.dot(
                    part_refs[j][first_row : first_row + rows],
                    weight_ref[weight_rows, lanes],
                    preferred_element_type=jnp.float32,
                )
                total = term if total is None else total + term
            if partial is not None:
                total = total + refs[0][:, lanes]
            if ending is not None:
                gate = jnp.concatenate([row_ref[:, lanes]] * (rows // STAT), axis=0)
                total = residual_ref[:, lanes].astype(jnp.float32) + gate * total
            out_ref[:, lanes] = total.astype(out_ref.dtype)
            return carry

        lax.fori_loop(0, width // tile, one, 0)

    return pl.pallas_call(
        kernel,
        out_shape=out_shape,
        in_specs=specs,
        out_specs=[vmem] * len(out_shape),
        scratch_shapes=scratch,
        compiler_params=pltpu.CompilerParams(vmem_limit_bytes=VMEM_LIMIT),
        cost_estimate=pl.CostEstimate(
            flops=2 * rows * depth * n * width, bytes_accessed=2 * depth * n * width, transcendentals=0
        ),
        name="project",
    )(*args)


def columns(x, part, width):
    return lax.dynamic_slice_in_dim(x, part * width, width, 1)


def paired(query_rows, key_rows, value_rows, out_weight, scalars, ending, n_a, n_b):
    n_seq = n_a * n_b * CORES
    groups = 2 * CORES
    own = scalars[0]
    kvw = key_rows.shape[1] // groups
    rows = query_rows.shape[0]
    tok = 2 * rows
    x = lax.axis_index("head")
    c = lax.axis_index("seq") % CORES

    def index(a, b, k):
        return (a * n_b + b) * CORES + k

    def swapped(piece, dx, dc):
        pairs = [
            ((s ^ dc) * 2 + (h ^ dx), s * 2 + h) for s in range(n_seq) for h in range(2)
        ]
        return lax.ppermute(piece, ("seq", "head"), pairs)

    def along_a(piece, moves):
        pairs = [
            (index(a, b, k), index(to, b, k)) for a, to in moves for b in range(n_b) for k in range(CORES)
        ]
        return lax.ppermute(piece, "seq", pairs)

    def beside_of(piece, only):
        pairs = [
            (index(a, 1 - b, k), index(a, b, k)) for a in only for b in range(n_b) for k in range(CORES)
        ]
        return lax.ppermute(piece, "seq", pairs)

    def stage(state, q, arrays, metas, last=False, half=None):
        return attend(
            scalars, q, state, arrays, GridPlace(metas, n_a, n_b, tok), len(metas), CORES, tok, last, half
        )

    def halves_of(first, base, flip, db):
        if isinstance(first, int):
            return [(first, base, flip, db), (first, base + tok, flip, db)]
        return [(n, base, flip, db) for n in first]

    def kv_for(dx, dc):
        j = (x ^ dx) * CORES + (c ^ dc)
        return jnp.concatenate([columns(key_rows, j, kvw), columns(value_rows, j, kvw)], axis=1)

    chips = list(range(n_a))
    order = [(0, 0), (1, 0), (0, 1), (1, 1)]
    pieces = {d: kv_for(*d) if sum(d) == 0 else swapped(kv_for(*d), *d) for d in order}
    early = jnp.concatenate([pieces[0, 0], pieces[0, 1]], axis=0)
    later = jnp.concatenate([pieces[1, 0], pieces[1, 1]], axis=0)
    block = jnp.concatenate([early, later], axis=0)
    qw = query_rows.shape[1] // 2
    q_own, q_other = columns(query_rows, x, qw), columns(query_rows, 1 - x, qw)
    block, later, out_weight, q_own, q_other = lax.optimization_barrier(
        (block, later, out_weight, q_own, q_other)
    )
    by_one, by_two = [(a, a ^ 1) for a in chips], [(a, a ^ 2) for a in chips]
    beside = beside_of(block, chips)
    next_early, far_early = along_a(early, by_one), along_a(early, by_two)
    q_came = swapped(q_other, 1, 0)
    weight = fetch(out_weight)
    next_early, far_early, weight = lax.optimization_barrier((next_early, far_early, weight))
    both_early = joined(own, next_early, far_early)
    later, both_early = lax.optimization_barrier((later, both_early))
    beside, both_early, q_came = lax.optimization_barrier((beside, both_early, q_came))
    beside_early = beside_of(both_early, chips)
    next_later, far_later = along_a(later, by_one), along_a(later, by_two)
    q_core = swapped(other_columns(own, [q_own, q_came]), 0, 1)
    both_later, far = joined(own, next_later, far_later), joined(own, far_early, far_later)
    both_later, far, again, q_core = lax.optimization_barrier((both_later, far, block, q_core))
    to_ends = along_a(far, [(1, 0), (2, 3)])
    to_middle = along_a(again, [(1, 2), (2, 1)])
    q = turn(own, [[q_own, q_came], [q_core]])
    (state,) = stage(None, q, [block], [halves_of(0, 0, 0, 0)])
    both_later, beside_early, state = lax.optimization_barrier((both_later, beside_early, state))
    beside_later = beside_of(both_later, chips)
    (state,) = stage(
        state, q, [next_early, next_later, far_early, far_later, beside],
        [halves_of((0, 1), 0, 1, 0), halves_of((2, 3), 0, 2, 0), halves_of(4, 0, 0, 1)],
    )
    to_ends, to_middle, state = lax.optimization_barrier((to_ends, to_middle, state))
    last, last_upper = picked(own, to_ends, to_middle, n_a, n_b)
    last, last_upper, beside_later = lax.optimization_barrier((last, last_upper, beside_later))
    beside_last = [beside_of(last_upper, chips), along_a(lower_half(own, beside_later), by_one)]
    (state,) = stage(
        state, q, [beside_early, beside_later, last],
        [[(0, 0, 1, 1), (0, tok, 2, 1)], [(1, 0, 1, 1), (1, tok, 2, 1)], halves_of(2, 0, 3, 0)],
    )
    last_block = [halves_of((0, 1), 0, 3, 1)]
    kept, sent = stage(state, q, beside_last, last_block, True, 1)
    came = swapped(sent, 0, 1)
    (begun,) = project(own, [(kept, 0, 0)], weight, rows)
    (theirs,) = project(own, [(came, 1, 0)], weight, rows, partial=begun)
    came_back = lax.ppermute(theirs, "head", [(0, 1), (1, 0)])
    state, theirs = lax.optimization_barrier((state, theirs))
    kept, sent = stage(state, q, beside_last, last_block, True, 0)
    came = swapped(sent, 0, 1)
    base, gate = project(own, [(kept, 0, 0), (came, 1, 0)], weight, rows, ending=ending)
    return (base + gate[:1] * came_back.astype(jnp.float32)).astype(jnp.bfloat16)


def gathered_attention(query_rows, key_rows, value_rows, scalars):
    spread = functools.partial(lax.all_to_all, axis_name="head", split_axis=1, concat_axis=0, tiled=True)
    local = jnp.concatenate([spread(key_rows), spread(value_rows)], axis=1)
    every = lax.all_gather(local, "seq", axis=0, tiled=True)
    tok = local.shape[0]
    return attend(
        scalars, turn(scalars[0], [[spread(query_rows)]]), None, [every], FlatPlace(tok), every.shape[0] // tok, 1, tok, True
    )[0]


def per_device(
    query_rows,
    key_rows,
    value_rows,
    residual,
    out_weight,
    gate_table,
    noise_steps,
    segment_mask,
    segment_map,
):
    n_seq = lax.axis_size("seq")
    n_head = lax.axis_size("head")
    own_seq = lax.axis_index("seq").astype(jnp.int32)
    own = own_seq.reshape(1)
    scalars = (own, segment_map, segment_mask)
    n_a, n_b = grid_of(n_seq)
    if n_head == 2 and n_a == 4 and n_b == 2:
        ending = (noise_steps, segment_map, gate_table, residual)
        return paired(query_rows, key_rows, value_rows, out_weight, scalars, ending, n_a, n_b)
    attended = gathered_attention(query_rows, key_rows, value_rows, scalars)
    projected = lax.psum_scatter(
        jnp.dot(attended, out_weight, preferred_element_type=jnp.float32).astype(jnp.bfloat16),
        "head",
        scatter_dimension=0,
        tiled=True,
    ).astype(jnp.float32)
    gate_row = lax.dynamic_slice_in_dim(gate_table, noise_steps[segment_map[own_seq]], 1, 0)
    return (residual.astype(jnp.float32) + gate_row * projected).astype(jnp.bfloat16)


def solution(mesh):
    placed = (
        P(("seq", "head"), None),
        P(("seq", "head"), None),
        P(("seq", "head"), None),
        P(("seq", "head"), None),
        P("head", None),
        P(),
        P(),
        P(),
        P(),
    )
    return jax.shard_map(
        per_device, mesh=mesh, in_specs=placed, out_specs=P(("seq", "head"), None), check_vma=False
    )
```
